256 devices in a mesh: scan: 32 (over z, y), head: 8 (over x, core).
Axes of the slice: x: 4, y: 4, z: 8, core: 2. Of those that a mesh axis runs over, the one named last changes fastest.
Arguments:
- owner_ids: int32 [32768, 1], P('scan'), may hold values from 0 to 31; in each aligned block of 1024 rows (0 to 1023, 1024 to 2047, ...) at most 128 rows name the same one
- owned_points: bfloat16 [512, 135168], P('head', 'scan'), may hold values from -32 to 32
- norm_gain: float32 [512], replicated, may hold values from 0.25 to 1.75
- qkv_weight: bfloat16 [3, 512, 512], P(None, 'head'), may hold values from -5 to 5
- out_weight: bfloat16 [512, 512], P('head'), may hold values from -0.25 to 0.25
- cotangent: bfloat16 [512, 32768], P('head', 'scan'), may hold values from -15 to 15
Outputs:
- mixed_rows: bfloat16 [512, 32768], P('head', 'scan')
- grad_owned: bfloat16 [512, 135168], P('head', 'scan')
- qkv_grad: float32 [3, 512, 512], P(None, 'head', 'scan')
- out_grad: float32 [512, 512], P('head', 'scan')
- gain_grad: float32 [512], P('head')
The draws below stay inside these ranges and needn't reach their ends.
Inputs may be any that keep to these rules, and one draw needn't show every extreme that they name: `owner_ids`: in each aligned block of 1024 rows (the rows of one index of scan) no owner is named more than 128 times, a bound that some block reaches; every owner is named somewhere.
All inputs are finite; a program needn't handle non-finite values.
Results may differ from the reference program's by a relative error of at most 0.014.
The reference program's roundings to bfloat16 on the way (of `points`, `scaled`, `context_b`, `grads_b` and `grad_points`) count: a program that leaves them out, or rounds other values in their place, can miss the bound.
Values may be sent and summed in bfloat16 or wider, within the bound.
A program may use at most 64 MiB of HBM per device.

```python
import math
import jax
import jax.numpy as jnp
import numpy as np
from jax import lax

HEADS = 32
HD = 16
C = 512
P_SIZE = 1024
ROWS_DEV = 1024
BUCKET = 128
CAP = 4224
TOTAL = 32768
N_SCAN = 32
N_HEAD = 8


def draw_owned_points(key, part):
    key = jax.random.fold_in(key, 11)
    row_count = N_SCAN * CAP
    channels = HEADS * HD
    key_list = jax.random.split(key, 3)
    noise = jnp.clip(jax.random.normal(key_list[0], (row_count, channels), jnp.float32), -5.0, 5.0)
    position = jnp.arange(channels, dtype=jnp.float32) / channels
    row_scale = 0.25 * jnp.exp(jax.random.uniform(key_list[1], (row_count, 1), jnp.float32, 0.0, math.log(10.0)))
    spread = jnp.exp(jax.random.uniform(key_list[2], (1, channels), jnp.float32, 0.0, math.log(1.5)))
    column_scale = 0.35 * spread * (3.0 ** position)[None, :]
    return (noise * row_scale * column_scale).T.astype(jnp.bfloat16)


def draw_qkv_weight(key, part):
    key = jax.random.fold_in(key, 12)
    channels = HEADS * HD
    base = jnp.clip(jax.random.normal(key, (3, channels, channels), jnp.float32), -4.0, 4.0) * channels ** (-0.5)
    return base.transpose(0, 2, 1).astype(jnp.bfloat16)


def draw_cotangent(key, part):
    key = jax.random.fold_in(key, 13)
    row_count = N_SCAN * ROWS_DEV
    channels = HEADS * HD
    key_list = jax.random.split(key, 1)
    noise = jnp.clip(jax.random.normal(key_list[0], (row_count, channels), jnp.float32), -5.0, 5.0)
    position = (jnp.arange(row_count, dtype=jnp.float32) / row_count)[:, None]
    return (noise * 0.5 * 3.0 ** position).T.astype(jnp.bfloat16)


def level_of(stream_key, extent, cuts, low, largest):
    gain, own = 1.0, jax.random.fold_in(stream_key, 6)
    for dim, shards_of in cuts:
        draws = jnp.exp(jax.random.uniform(jax.random.fold_in(own, dim), (shards_of,), jnp.float32, low / len(cuts), largest / len(cuts)))
        gain = gain * jnp.repeat(draws, extent[dim] // shards_of).reshape([-1 if axis == dim else 1 for axis in range(len(extent))])
    return gain


def routed_block(stream_key, own, number, rows, amount, top, limit, slope):
    ranking = jax.random.permutation(stream_key, amount)
    heavy_load, usual = load_shares(amount, rows * top, limit, slope, True), load_shares(amount, rows * top, limit, slope, False)
    places = jnp.arange(amount)

    def named(sizes, rotation):
        used = int((sizes > 0).sum())
        fixed = max(1, used // 4)
        shifted = fixed + (places - fixed + rotation * (used - fixed)) % max(1, amount - fixed)
        return jnp.zeros((amount,), jnp.int32).at[ranking[jnp.where(places < fixed, places, shifted)]].set(jnp.asarray(sizes, jnp.int32))

    sizes = jnp.where(number % 4 == 0, named(heavy_load, number // 4), named(usual, number - number // 4 - 1))
    mixed = jax.random.permutation(jax.random.fold_in(own, 3), amount)
    source_of, sink = mixed[0:amount // 2 * 2:2], mixed[1:amount // 2 * 2:2]
    room = jnp.minimum(sizes[source_of] - 1, limit - sizes[sink]) // 2
    room = jnp.where((source_of == ranking[0]) | (sink == ranking[0]) | (sizes[sink] == 0), 0, jnp.maximum(room, 0))
    shifted = jax.random.randint(jax.random.fold_in(own, 4), (amount // 2,), 0, 1 << 20) % (room + 1)
    sizes = sizes.at[source_of].add(-shifted).at[sink].add(shifted)
    members = jnp.searchsorted(jnp.cumsum(sizes), jnp.arange(rows * top), side="right").astype(jnp.int32)
    listing = members.reshape(top, rows).T
    listing = listing[jax.random.permutation(jax.random.fold_in(own, 1), rows)]
    rotation = jax.random.randint(jax.random.fold_in(own, 2), (rows, 1), 0, top)
    return jnp.take_along_axis(listing, (jnp.arange(top)[None, :] + rotation) % top, axis=1)


def load_shares(count, total, most, skew, full):
    weights = [(1 << 20) // math.isqrt(grade ** skew) + 1 for grade in range(1, count + 1)]
    largest = most if full else min(most, max(-(-total // count), total * weights[0] // sum(weights)))
    least = 1 if total - largest >= count - 1 else 0
    counts, spare = [largest] + [least] * (count - 1), total - largest - least * (count - 1)
    while spare > 0:
        candidates = [i for i in range(1, count) if counts[i] < largest] or [i for i in range(1, count) if counts[i] < most]
        whole, budget = sum([weights[i] for i in candidates]), spare
        for i in candidates:
            more = min(most - counts[i], max(1, budget * weights[i] // whole), spare)
            counts[i] = counts[i] + more
            spare = spare - more
    return np.array(counts)


def normal_values(key, shape, width, bound, cuts=(), held_as=jnp.bfloat16):
    drawn = jax.random.normal(key, shape, jnp.float32) * width
    if len(cuts) > 0:
        drawn = level_of(key, shape, cuts, -0.22, 0.18) * drawn
    return jnp.clip(drawn, min=-bound, max=bound).astype(held_as)


def setup_inputs(seed: int = 0) -> dict:
    streams_of = jax.random.split(jax.random.key(seed), 7)
    owner_ids_keys = jax.random.split(jax.random.fold_in(streams_of[0], 1), TOTAL // ROWS_DEV)
    owner_ids_turns = jax.random.permutation(jax.random.fold_in(streams_of[0], 3), TOTAL // ROWS_DEV)
    owner_ids = jax.vmap(lambda own, number: routed_block(jax.random.fold_in(streams_of[0], 2), own, number, ROWS_DEV, N_SCAN, 1, BUCKET, 2))(owner_ids_keys, owner_ids_turns).reshape((TOTAL, 1))
    owned_points = draw_owned_points(jax.random.fold_in(streams_of[6], 71), 0)
    norm_gain = jnp.clip(1.0 + 0.15 * jax.random.normal(streams_of[2], (C,), jnp.float32), 0.25, 1.75)
    qkv_weight = draw_qkv_weight(jax.random.fold_in(streams_of[6], 71), 0)
    out_weight = normal_values(streams_of[4], (C, C), C ** -0.5, 0.25, ((0, 8),))
    cotangent = draw_cotangent(jax.random.fold_in(streams_of[6], 71), 0)
    return {"owner_ids": owner_ids, "owned_points": owned_points, "norm_gain": norm_gain, "qkv_weight": qkv_weight, "out_weight": out_weight, "cotangent": cotangent}


EPS = 1e-05
PRECISE = lax.Precision.HIGHEST

def head_split(matrix):
    return matrix.reshape(P_SIZE, HEADS, HD).transpose(1, 2, 0)

def head_join(tensor):
    return tensor.transpose(2, 0, 1).reshape(P_SIZE, HEADS * HD)

def softmax_rows(scores):
    row_peak = lax.optimization_barrier(jnp.max(scores, axis=-1, keepdims=True))
    weights = jnp.exp(scores - row_peak)
    return weights / lax.optimization_barrier(jnp.sum(weights, axis=-1, keepdims=True))

def round_trip(values):
    lowered = values.astype(jnp.bfloat16)
    return lax.optimization_barrier(lowered).astype(jnp.float32)

def reference(owner_ids, owned_points, norm_gain, qkv_weight, out_weight, cotangent):
    channels = HEADS * HD
    group_width = channels // N_HEAD
    score_scale = HD ** (-0.5)
    owners = owner_ids[:, 0]
    onehot = (owners[:, None] == jnp.arange(N_SCAN, dtype=jnp.int32)[None, :]).astype(jnp.int32)
    rank_global = lax.optimization_barrier(jnp.sum((jnp.cumsum(onehot, axis=0) - onehot) * onehot, axis=1))
    slots = (owners * CAP + rank_global).astype(jnp.int32)
    patch_slots = slots.reshape(-1, P_SIZE)
    patch_grads = cotangent.T.reshape(-1, P_SIZE, channels)
    qkv_wide = qkv_weight.astype(jnp.float32).transpose(0, 2, 1)
    qkv_groups = qkv_wide.reshape(3, channels, N_HEAD, group_width)
    out_groups = out_weight.astype(jnp.float32).reshape(N_HEAD, group_width, channels)

    def per_patch(running_sums, inputs):
        qkv_acc, out_acc, gain_acc = running_sums
        chosen_slots, upstream = inputs
        points = owned_points[:, chosen_slots].T
        floats = points.astype(jnp.float32)
        row_mean = lax.optimization_barrier(jnp.mean(floats, axis=1, keepdims=True))
        centered = floats - row_mean
        inv_scale = lax.rsqrt(lax.optimization_barrier(jnp.mean(centered * centered, axis=1, keepdims=True)) + EPS)
        normed = centered * inv_scale
        scaled = (normed * norm_gain[None, :]).astype(jnp.bfloat16)
        scaled_wide = scaled.astype(jnp.float32)
        triple = jnp.einsum('rc,icw->irw', scaled_wide, qkv_wide)
        queries = head_split(triple[0])
        key_rows = head_split(triple[1])
        values = head_split(triple[2])
        scores = jnp.einsum('hdq,hdk->hqk', queries, key_rows, precision=PRECISE) * score_scale
        weights = softmax_rows(scores)
        context = jnp.einsum('hqk,hdk->hdq', weights, values, precision=PRECISE)
        context_b = head_join(context).astype(jnp.bfloat16)
        grouped = jnp.einsum('rgw,gwc->grc', context_b.astype(jnp.float32).reshape(P_SIZE, N_HEAD, group_width), out_groups)
        branch = lax.optimization_barrier(jnp.sum(round_trip(grouped), axis=0))
        mixed_rows = (floats + branch).astype(jnp.bfloat16)
        grad_context = jnp.dot(upstream, out_weight.T, preferred_element_type=jnp.float32)
        out_acc = out_acc + jnp.dot(context_b.T, upstream, preferred_element_type=jnp.float32)
        grad_heads = head_split(grad_context)
        value_grad = jnp.einsum('hqk,hdq->hdk', weights, grad_heads, precision=PRECISE)
        weight_grad = jnp.einsum('hdq,hdk->hqk', grad_heads, values, precision=PRECISE)
        center = lax.optimization_barrier(jnp.sum(weights * weight_grad, axis=-1, keepdims=True))
        score_grad = weights * (weight_grad - center) * score_scale
        query_grad = jnp.einsum('hqk,hdk->hdq', score_grad, key_rows, precision=PRECISE)
        key_grad = jnp.einsum('hqk,hdq->hdk', score_grad, queries, precision=PRECISE)
        grads_b = jnp.stack([head_join(query_grad), head_join(key_grad), head_join(value_grad)]).astype(jnp.bfloat16)
        grads_wide = grads_b.astype(jnp.float32)
        qkv_acc = qkv_acc + jnp.einsum('rc,irw->icw', scaled_wide, grads_wide)
        partial_sums = jnp.einsum('irgw,icgw->grc', grads_wide.reshape(3, P_SIZE, N_HEAD, group_width), qkv_groups)
        normed_grad = lax.optimization_barrier(jnp.sum(round_trip(partial_sums), axis=0))
        weighted = normed_grad * norm_gain[None, :]
        mean_first = lax.optimization_barrier(jnp.mean(weighted, axis=1, keepdims=True))
        mean_second = lax.optimization_barrier(jnp.mean(weighted * normed, axis=1, keepdims=True))
        grad_points = (upstream.astype(jnp.float32) + inv_scale * (weighted - mean_first - normed * mean_second)).astype(jnp.bfloat16)
        gain_acc = gain_acc + lax.optimization_barrier(jnp.sum(normed_grad * normed, axis=0))
        return ((qkv_acc, out_acc, gain_acc), (mixed_rows, grad_points))
    initial = (jnp.zeros((3, channels, channels), jnp.float32), jnp.zeros((channels, channels), jnp.float32), jnp.zeros((channels,), jnp.float32))
    sums_out, rows_out = lax.scan(per_patch, initial, (patch_slots, patch_grads))
    qkv_grad, out_grad, gain_grad = sums_out
    mixed_rows, grad_points = rows_out
    grad_owned = jnp.zeros_like(owned_points).at[:, slots].set(grad_points.reshape(-1, channels).T)
    return (mixed_rows.reshape(-1, channels).T, grad_owned, qkv_grad.transpose(0, 2, 1), out_grad, gain_grad)
```

```python
import functools

import jax
import jax.numpy as jnp
from jax import lax
from jax.experimental import pallas as pl
from jax.experimental.pallas import tpu as pltpu
from jax.sharding import PartitionSpec as P

HD = 16
BUCKET = 128
EPS = 1e-05
SPAN = 256
LOG2E = 1.4426950408889634
MESH = pl.DeviceIdType.MESH
F32 = jnp.float32
BF16 = jnp.bfloat16
VMEM = pl.BlockSpec(memory_space=pltpu.VMEM)
SMEM = pl.BlockSpec(memory_space=pltpu.SMEM)
LIMIT = 56 * 1024 * 1024


def dot_nn(a, b):
    return lax.dot_general(a, b, (((1,), (0,)), ((), ())), preferred_element_type=F32)


def dot_nt(a, b):
    return lax.dot_general(a, b, (((1,), (1,)), ((), ())), preferred_element_type=F32)


def dot_tn(a, b):
    return lax.dot_general(a, b, (((0,), (0,)), ((), ())), preferred_element_type=F32)


def split2(x):
    high = x.astype(BF16)
    return high, (x - high.astype(F32)).astype(BF16)


def split3(x):
    high = x.astype(BF16)
    rest = x - high.astype(F32)
    middle = rest.astype(BF16)
    return high, middle, (rest - middle.astype(F32)).astype(BF16)


def left_stack(x):
    a, b, c = split3(x)
    return [a, b, a, b, c, a]


def right_stack(x):
    a, b, c = split3(x)
    return [a, a, b, b, a, c]


def greet(ns, nh, scan, head):
    s, h = lax.axis_index("scan"), lax.axis_index("head")
    barrier = pltpu.get_barrier_semaphore()
    count = 0
    if scan:
        count += ns - 1

        def along_scan(j, carry):
            pl.semaphore_signal(
                barrier, inc=1, device_id=(lax.rem(s + j, ns), h), device_id_type=MESH
            )
            return carry

        lax.fori_loop(1, ns, along_scan, 0)
    if head:
        count += nh - 1

        def along_head(j, carry):
            pl.semaphore_signal(
                barrier, inc=1, device_id=(s, lax.rem(h + j, nh)), device_id_type=MESH
            )
            return carry

        lax.fori_loop(1, nh, along_head, 0)
    return barrier, count


def tally_kernel(ns, owner_ref, code_ref, sizes_ref, tall, send_sem, recv_sem):
    s, h = lax.axis_index("scan"), lax.axis_index("head")
    barrier, count = greet(ns, 1, True, False)
    owners = owner_ref[...]
    rows = owners.shape[1]
    hot = lax.broadcasted_iota(jnp.int32, (ns, rows), 0) == owners
    ones = jnp.where(hot, 1.0, 0.0)
    total = jnp.sum(ones, axis=1, keepdims=True).astype(jnp.int32)
    tall[...] = jnp.broadcast_to(total, (ns, 128))
    pl.semaphore_wait(barrier, count)

    def copy(j):
        peer = lax.rem(s + j, ns)
        return pltpu.make_async_remote_copy(
            src_ref=tall.at[pl.ds(peer, 1), :],
            dst_ref=sizes_ref.at[pl.ds(s, 1), :],
            send_sem=send_sem.at[j],
            recv_sem=recv_sem.at[j],
            device_id=(peer, h),
            device_id_type=MESH,
        )

    def start(j, carry):
        copy(j).start()
        return carry

    lax.fori_loop(1, ns, start, 0)
    sizes_ref[pl.ds(s, 1), :] = tall[pl.ds(s, 1), :]
    before = jnp.where(
        lax.broadcasted_iota(jnp.int32, (128, 128), 0)
        < lax.broadcasted_iota(jnp.int32, (128, 128), 1),
        1.0,
        0.0,
    ).astype(BF16)
    carried = jnp.zeros((ns, 1), F32)
    for b in range(0, rows, 128):
        part = ones[:, b : b + 128]
        running = dot_nn(part.astype(BF16), before) + carried
        rank = jnp.sum(running * part, axis=0, keepdims=True)
        code_ref[:, b : b + 128] = owners[:, b : b + 128] * BUCKET + rank.astype(jnp.int32)
        carried = carried + jnp.sum(part, axis=1, keepdims=True)

    def finish(j, carry):
        copy(j).wait()
        return carry

    lax.fori_loop(1, ns, finish, 0)


def window_kernel(ns, sizes_ref, points_ref, out_ref):
    def one(d, begin):
        tile = begin // 128
        off = begin - tile * 128
        window = points_ref[:, pl.ds(pl.multiple_of(tile * 128, 128), 256)].astype(F32)
        rolled = pltpu.roll(window, lax.rem(256 - off, 256), 1)
        out_ref[d] = rolled[:, :128].astype(BF16)
        return begin + sizes_ref[d, 0]

    lax.fori_loop(0, ns, one, jnp.int32(0))


def hot_block(code, first, height):
    ids = lax.broadcasted_iota(jnp.int32, (height, code.shape[1]), 0) + first
    return jnp.where(ids == code, 1.0, 0.0).astype(BF16)


def gather_kernel(
    ns, nh, send_ref, code_ref, cot_ref, full_ref, cotfull_ref,
    arrived, hots, far_send, far_recv, near_send, near_recv,
):
    s, h = lax.axis_index("scan"), lax.axis_index("head")
    width = send_ref.shape[1]
    nx = nh // 2
    x, core = h // 2, lax.rem(h, 2)
    twin = x * 2 + 1 - core
    barrier, count = greet(ns, nh, True, True)
    pl.semaphore_wait(barrier, count)

    def far(j):
        peer = lax.rem(s + j, ns)
        return pltpu.make_async_remote_copy(
            src_ref=send_ref.at[peer],
            dst_ref=arrived.at[s],
            send_sem=far_send.at[j],
            recv_sem=far_recv.at[j],
            device_id=(peer, h),
            device_id_type=MESH,
        )

    def far_start(j, carry):
        far(j).start()
        return carry

    def push(which, ref, piece, slot, to):
        block = ref.at[pl.ds(pl.multiple_of(piece * width, width), width), :]
        return pltpu.make_async_remote_copy(
            src_ref=block,
            dst_ref=block,
            send_sem=near_send.at[which, slot],
            recv_sem=near_recv.at[which, piece],
            device_id=(s, to),
            device_id_type=MESH,
        )

    def spread(which, ref):
        for j in range(1, nx):
            push(which, ref, h, j, lax.rem(x + j, nx) * 2 + core).start()
        push(which, ref, h, 0, twin).start()

    def relay(which, ref):
        for j in range(1, nx):
            piece = lax.rem(x + nx - j, nx) * 2 + core
            push(which, ref, piece, nx + j, twin).wait_recv()
            push(which, ref, piece, nx + j, twin).start()

    def settle(which, ref):
        for j in range(1, nx):
            push(which, ref, h, j, twin).wait_send()
            push(which, ref, h, nx + j, twin).wait_send()
        push(which, ref, h, 0, twin).wait_send()
        for j in range(nx):
            piece = lax.rem(x + nx - j, nx) * 2 + 1 - core
            push(which, ref, piece, 0, twin).wait_recv()

    mine = pl.ds(pl.multiple_of(h * width, width), width)
    lax.fori_loop(1, ns, far_start, 0)
    cotfull_ref[mine, :] = cot_ref[...]
    spread(0, cotfull_ref)
    arrived[pl.ds(s, 1)] = send_ref[pl.ds(s, 1)]
    code = code_ref[...]

    def build(i, carry):
        first = pl.multiple_of(i * 256, 256)
        hots[pl.ds(first, 256), :] = hot_block(code, first, 256)
        return carry

    lax.fori_loop(0, ns // 2, build, 0)
    relay(0, cotfull_ref)

    def far_finish(j, carry):
        far(j).wait()
        return carry

    lax.fori_loop(1, ns, far_finish, 0)
    total = jnp.zeros((width, code.shape[1]), F32)
    for i in range(ns // 4):
        pieces = jnp.concatenate([arrived[4 * i + t] for t in range(4)], axis=1)
        total = total + dot_nn(pieces, hots[512 * i : 512 * (i + 1), :])
    full_ref[mine, :] = total.astype(BF16)
    spread(1, full_ref)
    relay(1, full_ref)
    settle(0, cotfull_ref)
    settle(1, full_ref)


def block_kernel(
    full_ref, cot_ref, gain_ref, weight_ref, outw_ref, head_ref,
    branch_ref, part_ref, stats_ref, wgrad_ref, own_ref, normown_ref, gainown_ref,
    normed, scaled, query, keys, value, gradc, context, grads, key_t, value_t,
):
    channels, rows = full_ref.shape
    width = outw_ref.shape[0]
    gain = jnp.transpose(jnp.broadcast_to(gain_ref[...], (8, channels)))[:, :1]
    floats = full_ref[...].astype(F32)
    mean = jnp.sum(floats, axis=0, keepdims=True) * (1.0 / channels)
    centered = floats - mean
    inv = lax.rsqrt(jnp.sum(centered * centered, axis=0, keepdims=True) * (1.0 / channels) + EPS)
    normed[...] = centered * inv
    scaled[...] = (normed[...] * gain).astype(BF16)
    for i, ref in enumerate((query, keys, value)):
        ref[...] = dot_nn(weight_ref[i], scaled[...])
    gradc[...] = dot_nn(outw_ref[...], cot_ref[...])

    def one_head(head, carry):
        at = pl.ds(pl.multiple_of(head * HD, HD), HD)
        q, k, v, g = query[at, :], keys[at, :], value[at, :], gradc[at, :]
        key_t[...] = jnp.transpose(jnp.concatenate(left_stack(k), axis=0))
        ones = jnp.ones((HD, rows), BF16)
        value_t[...] = jnp.transpose(jnp.concatenate(left_stack(v) + [ones], axis=0))
        v_rows = jnp.concatenate(list(split2(v)) + [ones], axis=0)
        k_rows = jnp.concatenate(list(split2(k)), axis=0)
        key_grad = jnp.zeros((HD * 2, rows), F32)
        value_grad = jnp.zeros((HD * 2, rows), F32)
        for b in range(0, rows, SPAN):
            qb, gb = q[:, b : b + SPAN], g[:, b : b + SPAN]
            q_stack = jnp.concatenate(right_stack(qb * (HD**-0.5 * LOG2E)), axis=0)
            scores = dot_nn(key_t[...], q_stack)
            peak = jnp.max(scores, axis=0, keepdims=True)
            weights = jnp.exp2(scores - peak).astype(BF16)
            sums = dot_nn(v_rows, weights)
            share = 1.0 / sums[2 * HD : 2 * HD + 1]
            ctx = (sums[:HD] + sums[HD : 2 * HD]) * share
            context[at, b : b + SPAN] = ctx.astype(BF16)
            gs = gb * share
            center = jnp.sum(gs * ctx, axis=0, keepdims=True) * (-(HD**-0.5))
            parts = [jnp.broadcast_to(t, (HD, SPAN)).astype(F32) for t in split3(center)]
            row = lax.broadcasted_iota(jnp.int32, (HD, SPAN), 0)
            tail = jnp.where(
                row == 0, parts[0], jnp.where(row == 1, parts[1], jnp.where(row == 2, parts[2], 0.0))
            ).astype(BF16)
            g_stack = jnp.concatenate(right_stack(gs * HD**-0.5) + [tail], axis=0)
            delta = dot_nn(value_t[...], g_stack)
            score_grad = (weights.astype(F32) * delta).astype(BF16)
            value_grad = value_grad + dot_nt(jnp.concatenate(list(split2(gs)), axis=0), weights)
            dq = dot_nn(k_rows, score_grad)
            grads[at, b : b + SPAN] = (dq[:HD] + dq[HD:]).astype(BF16)
            key_grad = key_grad + dot_nt(jnp.concatenate(list(split2(qb)), axis=0), score_grad)
        k_at = pl.ds(pl.multiple_of(width + head * HD, HD), HD)
        v_at = pl.ds(pl.multiple_of(2 * width + head * HD, HD), HD)
        grads[k_at, :] = (key_grad[:HD] + key_grad[HD:]).astype(BF16)
        grads[v_at, :] = (value_grad[:HD] + value_grad[HD:]).astype(BF16)
        return carry

    lax.fori_loop(0, width // HD, one_head, 0)
    branch_ref[...] = dot_tn(outw_ref[...], context[...]).astype(BF16)
    wgrad_ref[:, : 3 * width] = dot_nt(scaled[...], grads[...])
    wgrad_ref[:, 3 * width :] = dot_nt(cot_ref[...], context[...])
    whole = jnp.concatenate([weight_ref[i] for i in range(3)], axis=0)
    part = dot_tn(whole, grads[...]).astype(BF16)
    part_ref[...] = part
    weighted = part.astype(F32) * gain
    stats_ref[0:1, :] = jnp.sum(weighted, axis=0, keepdims=True)
    stats_ref[1:2, :] = jnp.sum(weighted * normed[...], axis=0, keepdims=True)
    stats_ref[2:3, :] = inv
    stats_ref[3:8, :] = jnp.zeros((5, rows), F32)
    own = pl.ds(pl.multiple_of(head_ref[0] * width, width), width)
    own_ref[...] = full_ref[own, :]
    normown_ref[...] = normed[own, :]
    gainown_ref[...] = jnp.broadcast_to(gain, (channels, 128))


def return_kernel(
    ns, nh, branch_ref, part_ref, stats_ref, wgrad_ref, own_ref, normown_ref, gain_ref, cot_ref, code_ref,
    mixed_ref, back_ref, wsum_ref, gsum_ref,
    branch_in, part_in, stats_in, wgrad_in, gain_out, gain_in, buckets,
    head_send, head_recv, scan_send, scan_recv,
):
    s, h = lax.axis_index("scan"), lax.axis_index("head")
    width, rows = own_ref.shape
    channels = width * nh
    strip = channels // ns
    barrier, count = greet(ns, nh, True, True)
    pl.semaphore_wait(barrier, count)

    def remote(src, dst, send, recv, to):
        return pltpu.make_async_remote_copy(
            src_ref=src, dst_ref=dst, send_sem=send, recv_sem=recv, device_id=to, device_id_type=MESH
        )

    def head_copy(which, j):
        peer = lax.rem(h + j, nh)
        piece = pl.ds(pl.multiple_of(peer * width, width), width)
        src = (part_ref.at[piece, :], branch_ref.at[piece, :], stats_ref)[which]
        dst = (part_in, branch_in, stats_in)[which].at[h]
        return remote(src, dst, head_send.at[which, j], head_recv.at[which, j], (s, peer))

    def scan_copy(which, j):
        peer = lax.rem(s + j, ns)
        if which == 0:
            src = wgrad_ref.at[pl.ds(pl.multiple_of(peer * strip, strip), strip), :]
            dst = wgrad_in.at[s]
        elif which == 1:
            src, dst = buckets.at[peer], back_ref.at[s]
        else:
            src, dst = gain_out, gain_in.at[s]
        return remote(src, dst, scan_send.at[which, j], scan_recv.at[which, j], (peer, h))

    def each(count, act):
        def body(j, carry):
            act(j)
            return carry

        lax.fori_loop(1, count, body, 0)

    each(nh, lambda j: head_copy(2, j).start())
    each(nh, lambda j: head_copy(0, j).start())
    each(nh, lambda j: head_copy(1, j).start())
    each(ns, lambda j: scan_copy(0, j).start())
    mine = pl.ds(pl.multiple_of(h * width, width), width)
    part_in[pl.ds(h, 1)] = part_ref[mine, :][None]
    branch_in[pl.ds(h, 1)] = branch_ref[mine, :][None]
    stats_in[pl.ds(h, 1)] = stats_ref[...][None]
    wgrad_in[pl.ds(s, 1)] = wgrad_ref[pl.ds(pl.multiple_of(s * strip, strip), strip), :][None]
    each(nh, lambda j: head_copy(2, j).wait())
    each(nh, lambda j: head_copy(0, j).wait())
    normed_grad = part_in[0].astype(F32)
    stats = stats_in[0]
    for i in range(1, nh):
        normed_grad = normed_grad + part_in[i].astype(F32)
        stats = stats + stats_in[i]
    gain = gain_ref[mine, :][:, :1]
    normed = normown_ref[...]
    inv = stats_ref[2:3, :]
    first, second = stats[0:1] * (1.0 / channels), stats[1:2] * (1.0 / channels)
    grad = inv * (normed_grad * gain - first - normed * second)
    points_grad = (cot_ref[...].astype(F32) + grad).astype(BF16)
    code = code_ref[...]
    for i in range(ns // 4):
        block = dot_nt(points_grad, hot_block(code, 512 * i, 512)).astype(BF16)
        for t in range(4):
            buckets[4 * i + t] = block[:, 128 * t : 128 * (t + 1)]
    each(ns, lambda j: scan_copy(1, j).start())
    back_ref[pl.ds(s, 1)] = buckets[pl.ds(s, 1)]
    product = normed_grad * normed
    folded = product[:, :128]
    for b in range(128, rows, 128):
        folded = folded + product[:, b : b + 128]
    gain_row = jnp.sum(jnp.transpose(folded), axis=0, keepdims=True)
    gain_out[...] = jnp.zeros_like(gain_out)
    gain_out[0:1, :width] = gain_row
    each(ns, lambda j: scan_copy(2, j).start())
    gain_in[pl.ds(s, 1)] = gain_out[...][None]
    each(nh, lambda j: head_copy(1, j).wait())
    branch = branch_in[0].astype(F32)
    for i in range(1, nh):
        branch = branch + branch_in[i].astype(F32)
    mixed_ref[...] = (own_ref[...].astype(F32) + branch).astype(BF16)
    each(ns, lambda j: scan_copy(0, j).wait())
    wsum_ref[...] = jnp.sum(wgrad_in[...], axis=0)
    each(ns, lambda j: scan_copy(2, j).wait())
    gsum_ref[...] = jnp.sum(gain_in[...], axis=0)
    each(ns, lambda j: scan_copy(1, j).wait())


def slots_kernel(
    ns, sizes_ref, back_ref, mixed_in, wsum_ref, gsum_ref,
    mixed_ref, owned_ref, qkv_ref, out_ref, gain_ref, slots,
):
    width = back_ref.shape[1]
    slots[...] = jnp.zeros_like(slots)
    lane = lax.broadcasted_iota(jnp.int32, (width, 128), 1)

    def one(d, begin):
        size = sizes_ref[d, 0]
        tile = begin // 128
        off = begin - tile * 128
        block = jnp.where(lane < size, back_ref[d].astype(F32), 0.0)
        wide = jnp.concatenate([block, jnp.zeros_like(block)], axis=1)
        at = pl.ds(pl.multiple_of(tile * 128, 128), 256)
        slots[:, at] = slots[:, at] + pltpu.roll(wide, off, 1)
        return begin + size

    lax.fori_loop(0, ns, one, jnp.int32(0))
    owned_ref[...] = slots[...].astype(BF16)
    mixed_ref[...] = mixed_in[...]
    turned = jnp.transpose(wsum_ref[...])
    for i in range(3):
        qkv_ref[i] = turned[i * width : (i + 1) * width]
    out_ref[...] = turned[3 * width :]
    gain_ref[...] = gsum_ref[0:1, :width]


def per_device(owner_ids, owned_points, norm_gain, qkv_weight, out_weight, cotangent):
    ns, nh = lax.axis_size("scan"), lax.axis_size("head")
    rows = owner_ids.shape[0]
    width, slot_count = owned_points.shape
    channels = width * nh
    strip = channels // ns
    shape = jax.ShapeDtypeStruct
    dma = pltpu.SemaphoreType.DMA

    def remote_params(number):
        return pltpu.CompilerParams(
            collective_id=number, has_side_effects=True, vmem_limit_bytes=LIMIT
        )

    local_params = pltpu.CompilerParams(vmem_limit_bytes=LIMIT)
    code, sizes = pl.pallas_call(
        functools.partial(tally_kernel, ns),
        out_shape=(shape((1, rows), jnp.int32), shape((ns, 128), jnp.int32)),
        in_specs=[VMEM],
        out_specs=(VMEM, VMEM),
        scratch_shapes=[pltpu.VMEM((ns, 128), jnp.int32), dma((ns,)), dma((ns,))],
        compiler_params=remote_params(1),
        name="tally",
    )(owner_ids.reshape(1, rows))
    send_rows = pl.pallas_call(
        functools.partial(window_kernel, ns),
        out_shape=shape((ns, width, BUCKET), BF16),
        in_specs=[SMEM, VMEM],
        out_specs=VMEM,
        compiler_params=local_params,
        name="windows",
    )(sizes, owned_points)
    full, cot_full = pl.pallas_call(
        functools.partial(gather_kernel, ns, nh),
        out_shape=(shape((channels, rows), BF16), shape((channels, rows), BF16)),
        in_specs=[VMEM] * 3,
        out_specs=(VMEM, VMEM),
        scratch_shapes=[
            pltpu.VMEM((ns, width, BUCKET), BF16),
            pltpu.VMEM((ns * BUCKET, rows), BF16),
            dma((ns,)),
            dma((ns,)),
            dma((2, nh)),
            dma((2, nh)),
        ],
        compiler_params=remote_params(2),
        name="gather_points",
    )(send_rows, code, cotangent)
    branch, part, stats, wgrad, own, normown, gain_wide = pl.pallas_call(
        block_kernel,
        out_shape=(
            shape((channels, rows), BF16),
            shape((channels, rows), BF16),
            shape((8, rows), F32),
            shape((channels, 4 * width), F32),
            shape((width, rows), BF16),
            shape((width, rows), F32),
            shape((channels, 128), F32),
        ),
        in_specs=[VMEM] * 5 + [SMEM],
        out_specs=(VMEM,) * 7,
        scratch_shapes=[
            pltpu.VMEM((channels, rows), F32),
            pltpu.VMEM((channels, rows), BF16),
            pltpu.VMEM((width, rows), F32),
            pltpu.VMEM((width, rows), F32),
            pltpu.VMEM((width, rows), F32),
            pltpu.VMEM((width, rows), F32),
            pltpu.VMEM((width, rows), BF16),
            pltpu.VMEM((3 * width, rows), BF16),
            pltpu.VMEM((rows, 6 * HD), BF16),
            pltpu.VMEM((rows, 7 * HD), BF16),
        ],
        compiler_params=local_params,
        name="attention_block",
    )(
        full, cot_full, norm_gain.reshape(1, channels), qkv_weight, out_weight,
        lax.axis_index("head").astype(jnp.int32).reshape(1),
    )
    mixed, back, wsum, gsum = pl.pallas_call(
        functools.partial(return_kernel, ns, nh),
        out_shape=(
            shape((width, rows), BF16),
            shape((ns, width, BUCKET), BF16),
            shape((strip, 4 * width), F32),
            shape((8, 128), F32),
        ),
        in_specs=[VMEM] * 9,
        out_specs=(VMEM,) * 4,
        scratch_shapes=[
            pltpu.VMEM((nh, width, rows), BF16),
            pltpu.VMEM((nh, width, rows), BF16),
            pltpu.VMEM((nh, 8, rows), F32),
            pltpu.VMEM((ns, strip, 4 * width), F32),
            pltpu.VMEM((8, 128), F32),
            pltpu.VMEM((ns, 8, 128), F32),
            pltpu.VMEM((ns, width, BUCKET), BF16),
            dma((3, nh)),
            dma((3, nh)),
            dma((3, ns)),
            dma((3, ns)),
        ],
        compiler_params=remote_params(3),
        name="return_points",
    )(branch, part, stats, wgrad, own, normown, gain_wide, cotangent, code)
    mixed_rows, grad_owned, qkv_grad, out_grad, gain_grad = pl.pallas_call(
        functools.partial(slots_kernel, ns),
        out_shape=(
            shape((width, rows), BF16),
            shape((width, slot_count), BF16),
            shape((3, width, strip), F32),
            shape((width, strip), F32),
            shape((1, width), F32),
        ),
        in_specs=[SMEM] + [VMEM] * 4,
        out_specs=(VMEM,) * 5,
        scratch_shapes=[pltpu.VMEM((width, slot_count), F32)],
        compiler_params=local_params,
        name="slots",
    )(sizes, back, mixed, wsum, gsum)
    return mixed_rows, grad_owned, qkv_grad, out_grad, gain_grad.reshape(width)


def solution(mesh):
    in_specs = (
        P("scan", None),
        P("head", "scan"),
        P(),
        P(None, "head", None),
        P("head", None),
        P("head", "scan"),
    )
    out_specs = (
        P("head", "scan"),
        P("head", "scan"),
        P(None, "head", "scan"),
        P("head", "scan"),
        P("head"),
    )
    return jax.shard_map(
        per_device, mesh=mesh, in_specs=in_specs, out_specs=out_specs, check_vma=False
    )
```

```python
import functools

import jax
import jax.numpy as jnp
from jax import lax
from jax.experimental import pallas as pl
from jax.experimental.pallas import tpu as pltpu
from jax.sharding import PartitionSpec as P

HD = 16
BUCKET = 128
EPS = 1e-05
SPAN = 256
LOG2E = 1.4426950408889634
MESH = pl.DeviceIdType.MESH
F32 = jnp.float32
BF16 = jnp.bfloat16
VMEM = pl.BlockSpec(memory_space=pltpu.VMEM)
SMEM = pl.BlockSpec(memory_space=pltpu.SMEM)
LIMIT = 56 * 1024 * 1024


def dot_nn(a, b):
    return lax.dot_general(a, b, (((1,), (0,)), ((), ())), preferred_element_type=F32)


def dot_nt(a, b):
    return lax.dot_general(a, b, (((1,), (1,)), ((), ())), preferred_element_type=F32)


def dot_tn(a, b):
    return lax.dot_general(a, b, (((0,), (0,)), ((), ())), preferred_element_type=F32)


def split2(x):
    high = x.astype(BF16)
    return high, (x - high.astype(F32)).astype(BF16)


def split3(x):
    high = x.astype(BF16)
    rest = x - high.astype(F32)
    middle = rest.astype(BF16)
    return high, middle, (rest - middle.astype(F32)).astype(BF16)


def left_stack(x):
    a, b, c = split3(x)
    return [a, b, a, b, c, a]


def right_stack(x):
    a, b, c = split3(x)
    return [a, a, b, b, a, c]


def hot_block(code, first, height):
    ids = lax.broadcasted_iota(jnp.int32, (height, code.shape[1]), 0) + first
    return jnp.where(ids == code, 1.0, 0.0).astype(BF16)


def aligned(first, size):
    return pl.ds(pl.multiple_of(first, size), size)


def each(first, last, act):
    def body(j, carry):
        act(j)
        return carry

    lax.fori_loop(first, last, body, 0)


TALLY, POINTS, WGRAD, BACK, GAIN = range(5)
COT, FULL, BRANCH, STATS, TWIN, PAIR = range(6)


def main_kernel(
    ns, nh, owner_ref, points_ref, cot_ref, gain_ref, weight_ref, outw_ref,
    sizes_ref, mixed_ref, back_ref, wsum_ref, gsum_ref,
    tall, tiles, offsets, windows, arrived, hots, full, cot, code_ref, gain_wide,
    normed, scaled, query, keys, value, gradc, context, grads, weights_all, shares,
    key_t, value_t, branch_out, branch_in, part_out, twin_in, pair_out, pair_in, stats_out, stats_in,
    wgrad_out, wgrad_in, gain_out, gain_in, buckets,
    scan_send, scan_recv, head_send, head_recv,
):
    s, h = lax.axis_index("scan"), lax.axis_index("head")
    nx = nh // 2
    x, core = h // 2, lax.rem(h, 2)
    twin = x * 2 + 1 - core
    width, rows = cot_ref.shape
    channels = width * nh
    strip = channels // ns
    mine = aligned(h * width, width)

    def remote(src, dst, send, recv, to):
        return pltpu.make_async_remote_copy(
            src_ref=src, dst_ref=dst, send_sem=send, recv_sem=recv, device_id=to, device_id_type=MESH
        )

    def scan_copy(which, j):
        peer = lax.rem(s + j, ns)
        if which == TALLY:
            src, dst = tall.at[pl.ds(peer, 1), :], sizes_ref.at[pl.ds(s, 1), :]
        elif which == POINTS:
            src, dst = windows.at[peer], arrived.at[s]
        elif which == WGRAD:
            src, dst = wgrad_out.at[aligned(peer * strip, strip), :], wgrad_in.at[s]
        elif which == BACK:
            src, dst = buckets.at[peer], back_ref.at[s]
        else:
            src, dst = gain_out, gain_in.at[s]
        return remote(src, dst, scan_send.at[which, j], scan_recv.at[which, j], (peer, h))

    def head_copy(which, j):
        peer = lax.rem(h + j, nh)
        if which == BRANCH:
            src, dst = branch_out.at[aligned(peer * width, width), :], branch_in.at[h]
        else:
            src, dst = stats_out, stats_in.at[h]
        return remote(src, dst, head_send.at[which, j], head_recv.at[which, j], (s, peer))

    def push(which, ref, piece, slot, to):
        block = ref.at[aligned(piece * width, width), :]
        return remote(block, block, head_send.at[which, slot], head_recv.at[which, piece], (s, to))

    def spread(which, ref):
        for j in (nx // 2, *[j for j in range(1, nx) if j != nx // 2]):
            push(which, ref, h, j, lax.rem(x + j, nx) * 2 + core).start()
        push(which, ref, h, 0, twin).start()

    def relay(which, ref):
        for j in range(1, nx):
            piece = lax.rem(x + nx - j, nx) * 2 + core
            push(which, ref, piece, nx + j, twin).wait_recv()
            push(which, ref, piece, nx + j, twin).start()

    def arrive(which, ref):
        for j in range(nx):
            piece = lax.rem(x + nx - j, nx) * 2 + 1 - core
            push(which, ref, piece, 0, twin).wait_recv()

    def sent(which, ref):
        for j in range(1, nx):
            push(which, ref, h, j, twin).wait_send()
            push(which, ref, h, nx + j, twin).wait_send()
        push(which, ref, h, 0, twin).wait_send()

    barrier = pltpu.get_barrier_semaphore()

    def greet_scan(j):
        pl.semaphore_signal(
            barrier, inc=1, device_id=(lax.rem(s + j, ns), h), device_id_type=MESH
        )

    def greet_head(j):
        pl.semaphore_signal(
            barrier, inc=1, device_id=(s, lax.rem(h + j, nh)), device_id_type=MESH
        )

    each(1, ns, greet_scan)
    each(1, nh, greet_head)
    owners = owner_ref[...]
    hot = lax.broadcasted_iota(jnp.int32, (ns, rows), 0) == owners
    ones = jnp.where(hot, 1.0, 0.0)
    total = jnp.sum(jnp.where(hot, 1, 0), axis=1, keepdims=True)
    tall[...] = jnp.broadcast_to(total, (ns, 128))
    cot[mine, :] = cot_ref[...]
    pl.semaphore_wait(barrier, ns + nh - 2)

    each(1, ns, lambda j: scan_copy(TALLY, j).start())
    spread(COT, cot)
    sizes_ref[pl.ds(s, 1), :] = tall[pl.ds(s, 1), :]
    before = jnp.where(
        lax.broadcasted_iota(jnp.int32, (128, 128), 0)
        < lax.broadcasted_iota(jnp.int32, (128, 128), 1),
        1.0,
        0.0,
    ).astype(BF16)
    carried = jnp.zeros((ns, 1), F32)
    for b in range(0, rows, 128):
        part = ones[:, b : b + 128]
        running = dot_nn(part.astype(BF16), before) + carried
        rank = jnp.sum(running * part, axis=0, keepdims=True)
        code_ref[:, b : b + 128] = owners[:, b : b + 128] * BUCKET + rank.astype(jnp.int32)
        carried = carried + jnp.sum(part, axis=1, keepdims=True)
    each(1, ns, lambda j: scan_copy(TALLY, j).wait())

    earlier = jnp.where(
        lax.broadcasted_iota(jnp.int32, (ns, ns), 1) < lax.broadcasted_iota(jnp.int32, (ns, ns), 0),
        1.0,
        0.0,
    ).astype(BF16)
    begins = dot_nn(earlier, sizes_ref[...].astype(F32).astype(BF16)).astype(jnp.int32)
    tiles[...] = begins // 128
    offsets[...] = begins - begins // 128 * 128
    span = lax.broadcasted_iota(jnp.int32, (256, 128), 0) - lax.broadcasted_iota(
        jnp.int32, (256, 128), 1
    )
    groups = ns // 4

    def nth_group(i):
        half = (i + 1) // 2
        shift = groups // 2 + jnp.where(lax.rem(i, 2) == 1, half, -half)
        return lax.rem(s // 4 + shift + groups, groups)

    def cut_and_send(i):
        group = nth_group(i)
        places = [jnp.broadcast_to(tiles[pl.ds(group * 4 + t, 1), :], (16, 128)) for t in range(4)]
        low = [jnp.zeros((width // 16, 16, 128), BF16) for t in range(4)]
        high = [jnp.zeros((width // 16, 16, 128), BF16) for t in range(4)]
        previous = [jnp.zeros((1, 16, 128), BF16) for t in range(4)]
        for n in range(ns + 1):
            tile = points_ref[:, 128 * n : 128 * (n + 1)].reshape(width // 16, 16, 128)
            for t in range(4):
                here = jnp.where(places[t] == n, 1.0, 0.0).astype(BF16)[None]
                high[t] = high[t] + tile * previous[t]
                if n < ns:
                    low[t] = low[t] + tile * here
                previous[t] = here
        for t in range(4):
            peer = group * 4 + t
            window = jnp.concatenate(
                [low[t].reshape(width, 128), high[t].reshape(width, 128)], axis=1
            )
            pick = jnp.where(span == offsets[pl.ds(peer, 1), :], 1.0, 0.0).astype(BF16)
            windows[peer] = dot_nn(window, pick).astype(BF16)

            @pl.when(peer != s)
            def _():
                scan_copy(POINTS, lax.rem(peer - s + ns, ns)).start()

    each(0, groups, cut_and_send)
    arrived[pl.ds(s, 1)] = windows[pl.ds(s, 1)]
    code = code_ref[...]

    def build(i):
        first = pl.multiple_of(i * 256, 256)
        hots[pl.ds(first, 256), :] = hot_block(code, first, 256)

    each(0, ns // 2, build)
    relay(COT, cot)
    gain = jnp.transpose(jnp.broadcast_to(gain_ref[...], (8, channels)))[:, :1]
    gain_wide[...] = jnp.broadcast_to(gain, gain_wide.shape)
    arrive(COT, cot)
    gradc[...] = dot_nn(outw_ref[...], cot[...])

    gathered = jnp.zeros((width, rows), F32)
    for i in range(groups):
        group = nth_group(i)
        for t in range(4):
            source = group * 4 + t

            @pl.when(source != s)
            def _():
                scan_copy(POINTS, lax.rem(s - source + ns, ns)).wait_recv()

        pieces = jnp.concatenate([arrived[group * 4 + t] for t in range(4)], axis=1)
        gathered = gathered + dot_nn(pieces, hots[aligned(group * 512, 512), :])
    full[mine, :] = gathered.astype(BF16)
    spread(FULL, full)
    relay(FULL, full)
    arrive(FULL, full)

    floats = full[...].astype(F32)
    mean = jnp.sum(floats, axis=0, keepdims=True) * (1.0 / channels)
    centered = floats - mean
    inv = lax.rsqrt(jnp.sum(centered * centered, axis=0, keepdims=True) * (1.0 / channels) + EPS)
    normed[...] = centered * inv
    scaled[...] = (normed[...] * gain_wide[:, :1]).astype(BF16)
    for i, ref in enumerate((query, keys, value)):
        ref[...] = dot_nn(weight_ref[i], scaled[...])

    def forward(head):
        at = aligned(head * HD, HD)
        q, k, v = query[at, :], keys[at, :], value[at, :]
        key_t[...] = jnp.transpose(jnp.concatenate(left_stack(k), axis=0))
        v_rows = jnp.concatenate(list(split2(v)) + [jnp.ones((HD, rows), BF16)], axis=0)
        for b in range(0, rows, SPAN):
            q_stack = jnp.concatenate(
                right_stack(q[:, b : b + SPAN] * (HD**-0.5 * LOG2E)), axis=0
            )
            scores = dot_nn(key_t[...], q_stack)
            peak = jnp.max(scores, axis=0, keepdims=True)
            weights = jnp.exp2(scores - peak).astype(BF16)
            weights_all[head, :, b : b + SPAN] = weights
            sums = dot_nn(v_rows, weights)
            share = 1.0 / sums[2 * HD : 2 * HD + 1]
            shares[head, :, b : b + SPAN] = share
            ctx = (sums[:HD] + sums[HD : 2 * HD]) * share
            context[at, b : b + SPAN] = ctx

    each(0, width // HD, forward)
    context_b = context[...].astype(BF16)
    branch_out[...] = dot_tn(outw_ref[...], context_b).astype(BF16)
    each(1, nh, lambda j: head_copy(BRANCH, j).start())

    def backward(head):
        at = aligned(head * HD, HD)
        q, k, v = query[at, :], keys[at, :], value[at, :]
        row = lax.broadcasted_iota(jnp.int32, (HD, rows), 0)
        ones = jnp.ones((HD, rows), BF16)
        value_t[...] = jnp.transpose(jnp.concatenate(left_stack(v) + [ones], axis=0))
        k_rows = jnp.concatenate(list(split2(k)), axis=0)
        gs = gradc[at, :] * shares[head]
        center = jnp.sum(gs * context[at, :], axis=0, keepdims=True) * (-(HD**-0.5))
        parts = [t.astype(F32) for t in split3(center)]
        tail = jnp.where(
            row == 0, parts[0], jnp.where(row == 1, parts[1], jnp.where(row == 2, parts[2], 0.0))
        ).astype(BF16)
        g_stack = jnp.concatenate(right_stack(gs * HD**-0.5) + [tail], axis=0)
        g_rows = jnp.concatenate(list(split2(gs)), axis=0)
        q_rows = jnp.concatenate(list(split2(q)), axis=0)
        key_grad = jnp.zeros((HD * 2, rows), F32)
        value_grad = jnp.zeros((HD * 2, rows), F32)
        for b in range(0, rows, SPAN):
            weights = weights_all[head, :, b : b + SPAN]
            delta = dot_nn(value_t[...], g_stack[:, b : b + SPAN])
            score_grad = (weights.astype(F32) * delta).astype(BF16)
            value_grad = value_grad + dot_nt(g_rows[:, b : b + SPAN], weights)
            dq = dot_nn(k_rows, score_grad)
            grads[at, b : b + SPAN] = (dq[:HD] + dq[HD:]).astype(BF16)
            key_grad = key_grad + dot_nt(q_rows[:, b : b + SPAN], score_grad)
        k_at = aligned(width + head * HD, HD)
        v_at = aligned(2 * width + head * HD, HD)
        grads[k_at, :] = (key_grad[:HD] + key_grad[HD:]).astype(BF16)
        grads[v_at, :] = (value_grad[:HD] + value_grad[HD:]).astype(BF16)

    each(0, width // HD, backward)

    whole = jnp.concatenate([weight_ref[i] for i in range(3)], axis=0)
    part_out[...] = dot_tn(whole, grads[...]).astype(BF16)

    def twin_copy(j):
        to = lax.rem(x + j, nx)
        src = part_out.at[aligned((to * 2 + 1 - core) * width, width), :]
        return remote(src, twin_in.at[j], head_send.at[TWIN, j], head_recv.at[TWIN, j], (s, twin))

    def pair_copy(j):
        to = lax.rem(x + j, nx) * 2 + core
        return remote(
            pair_out.at[j], pair_in.at[j], head_send.at[PAIR, j], head_recv.at[PAIR, j], (s, to)
        )

    order = (*([nx // 2] if nx > 1 else []), *[j for j in range(1, nx) if j != nx // 2])
    for j in (*order, 0):
        twin_copy(j).start()
    weighted = part_out[...].astype(F32) * gain_wide[:, :1]
    stats_out[0:1, :] = jnp.sum(weighted, axis=0, keepdims=True)
    stats_out[1:2, :] = jnp.sum(weighted * normed[...], axis=0, keepdims=True)
    each(1, nh, lambda j: head_copy(STATS, j).start())

    def pair_sum(j):
        twin_copy(j).wait_recv()
        own = part_out[aligned((lax.rem(x + j, nx) * 2 + core) * width, width), :]
        return own.astype(F32) + twin_in[j].astype(F32)

    for j in order:
        pair_out[j] = pair_sum(j).astype(BF16)
        pair_copy(j).start()
    normed_grad = pair_sum(0)
    wgrad_out[:, : 3 * width] = dot_nt(scaled[...], grads[...]).astype(BF16)
    wgrad_out[:, 3 * width :] = dot_nt(cot[...], context_b).astype(BF16)
    each(1, ns, lambda j: scan_copy(WGRAD, j).start())
    wgrad_in[pl.ds(s, 1)] = wgrad_out[aligned(s * strip, strip), :][None]
    each(1, nh, lambda j: head_copy(BRANCH, j).wait())
    branch = branch_out[mine, :].astype(F32)
    for i in range(1, nh):
        branch = branch + branch_in[lax.rem(h + i, nh)].astype(F32)
    mixed_ref[...] = (full[mine, :].astype(F32) + branch).astype(BF16)
    each(1, nh, lambda j: head_copy(STATS, j).wait())
    stats = stats_out[...]
    for i in range(1, nh):
        stats = stats + stats_in[lax.rem(h + i, nh)]
    for j in order:
        pair_copy(j).wait_recv()
        normed_grad = normed_grad + pair_in[j].astype(F32)
    normed_own = normed[mine, :]
    first, second = stats[0:1] * (1.0 / channels), stats[1:2] * (1.0 / channels)
    grad = inv * (normed_grad * gain_wide[mine, :1] - first - normed_own * second)
    points_grad = (cot_ref[...].astype(F32) + grad).astype(BF16)

    for i in range(groups):
        group = nth_group(i)
        block = dot_nt(points_grad, hots[aligned(group * 512, 512), :]).astype(BF16)
        for t in range(4):
            peer = group * 4 + t
            buckets[peer] = block[:, 128 * t : 128 * (t + 1)]

            @pl.when(peer != s)
            def _():
                scan_copy(BACK, lax.rem(peer - s + ns, ns)).start()

    back_ref[pl.ds(s, 1)] = buckets[pl.ds(s, 1)]
    product = normed_grad * normed_own
    folded = product[:, :128]
    for b in range(128, rows, 128):
        folded = folded + product[:, b : b + 128]
    gain_out[...] = jnp.zeros_like(gain_out)
    gain_out[:, :width] = jnp.sum(jnp.transpose(folded), axis=0, keepdims=True)
    each(1, ns, lambda j: scan_copy(GAIN, j).start())
    gain_in[pl.ds(s, 1)] = gain_out[...][None]
    each(1, ns, lambda j: scan_copy(WGRAD, j).wait())
    wsum_ref[...] = jnp.sum(wgrad_in[...].astype(F32), axis=0)
    each(1, ns, lambda j: scan_copy(GAIN, j).wait())
    gsum_ref[...] = jnp.sum(gain_in[...], axis=0)
    sent(COT, cot)
    sent(FULL, full)
    for j in (*order, 0):
        twin_copy(j).wait_send()
    for j in order:
        pair_copy(j).wait_send()
    each(1, ns, lambda j: scan_copy(POINTS, j).wait_send())
    each(1, ns, lambda j: scan_copy(BACK, j).wait())


def slots_kernel(
    ns, sizes_ref, back_ref, mixed_in, wsum_ref, gsum_ref,
    mixed_ref, owned_ref, qkv_ref, out_ref, gain_ref, slots,
):
    width = back_ref.shape[1]
    slots[...] = jnp.zeros_like(slots)
    lane = lax.broadcasted_iota(jnp.int32, (width, 128), 1)

    def one(d, begin):
        size = sizes_ref[d, 0]
        tile = begin // 128
        off = begin - tile * 128
        block = jnp.where(lane < size, back_ref[d].astype(F32), 0.0)
        wide = jnp.concatenate([block, jnp.zeros_like(block)], axis=1)
        at = pl.ds(pl.multiple_of(tile * 128, 128), 256)
        slots[:, at] = slots[:, at] + pltpu.roll(wide, off, 1)
        return begin + size

    lax.fori_loop(0, ns, one, jnp.int32(0))
    owned_ref[...] = slots[...].astype(BF16)
    mixed_ref[...] = mixed_in[...]
    for i in range(3):
        qkv_ref[i] = wsum_ref[:, i * width : (i + 1) * width]
    out_ref[...] = wsum_ref[:, 3 * width :]
    gain_ref[...] = gsum_ref[:, :width]


def per_device(owner_ids, owned_points, norm_gain, qkv_weight, out_weight, cotangent):
    ns, nh = lax.axis_size("scan"), lax.axis_size("head")
    nx = nh // 2
    rows = owner_ids.shape[0]
    width, slot_count = owned_points.shape
    channels = width * nh
    strip = channels // ns
    shape = jax.ShapeDtypeStruct
    dma = pltpu.SemaphoreType.DMA
    vmem = pltpu.VMEM
    sizes, mixed, back, wsum, gsum = pl.pallas_call(
        functools.partial(main_kernel, ns, nh),
        out_shape=(
            shape((ns, 128), jnp.int32),
            shape((width, rows), BF16),
            shape((ns, width, BUCKET), BF16),
            shape((strip, 4 * width), F32),
            shape((1, 128), F32),
        ),
        in_specs=[VMEM] * 6,
        out_specs=(VMEM,) * 5,
        scratch_shapes=[
            vmem((ns, 128), jnp.int32),
            vmem((ns, 128), jnp.int32),
            vmem((ns, 128), jnp.int32),
            vmem((ns, width, BUCKET), BF16),
            vmem((ns, width, BUCKET), BF16),
            vmem((ns * BUCKET, rows), BF16),
            vmem((channels, rows), BF16),
            vmem((channels, rows), BF16),
            vmem((1, rows), jnp.int32),
            vmem((channels, 128), F32),
            vmem((channels, rows), F32),
            vmem((channels, rows), BF16),
            vmem((width, rows), F32),
            vmem((width, rows), F32),
            vmem((width, rows), F32),
            vmem((width, rows), F32),
            vmem((width, rows), F32),
            vmem((3 * width, rows), BF16),
            vmem((width // HD, rows, rows), BF16),
            vmem((width // HD, 1, rows), F32),
            vmem((rows, 6 * HD), BF16),
            vmem((rows, 7 * HD), BF16),
            vmem((channels, rows), BF16),
            vmem((nh, width, rows), BF16),
            vmem((channels, rows), BF16),
            vmem((nx, width, rows), BF16),
            vmem((nx, width, rows), BF16),
            vmem((nx, width, rows), BF16),
            vmem((2, rows), F32),
            vmem((nh, 2, rows), F32),
            vmem((channels, 4 * width), BF16),
            vmem((ns, strip, 4 * width), BF16),
            vmem((1, 128), F32),
            vmem((ns, 1, 128), F32),
            vmem((ns, width, BUCKET), BF16),
            dma((5, ns)),
            dma((5, ns)),
            dma((6, nh)),
            dma((6, nh)),
        ],
        compiler_params=pltpu.CompilerParams(
            collective_id=1, has_side_effects=True, vmem_limit_bytes=LIMIT
        ),
        name="patch_block",
    )(owner_ids.reshape(1, rows), owned_points, cotangent, norm_gain.reshape(1, channels), qkv_weight, out_weight)
    mixed_rows, grad_owned, qkv_grad, out_grad, gain_grad = pl.pallas_call(
        functools.partial(slots_kernel, ns),
        out_shape=(
            shape((width, rows), BF16),
            shape((width, slot_count), BF16),
            shape((3, strip, width), F32),
            shape((strip, width), F32),
            shape((1, width), F32),
        ),
        in_specs=[SMEM] + [VMEM] * 4,
        out_specs=(VMEM,) * 5,
        scratch_shapes=[vmem((width, slot_count), F32)],
        compiler_params=pltpu.CompilerParams(vmem_limit_bytes=LIMIT),
        name="slots",
    )(sizes, back, mixed, wsum, gsum)
    return (
        mixed_rows,
        grad_owned,
        qkv_grad.transpose(0, 2, 1),
        out_grad.T,
        gain_grad.reshape(width),
    )


def solution(mesh):
    in_specs = (
        P("scan", None),
        P("head", "scan"),
        P(),
        P(None, "head", None),
        P("head", None),
        P("head", "scan"),
    )
    out_specs = (
        P("head", "scan"),
        P("head", "scan"),
        P(None, "head", "scan"),
        P("head", "scan"),
        P("head"),
    )
    return jax.shard_map(
        per_device, mesh=mesh, in_specs=in_specs, out_specs=out_specs, check_vma=False
    )
```

```python
import functools

import jax
import jax.numpy as jnp
from jax import lax
from jax.experimental import pallas as pl
from jax.experimental.pallas import tpu as pltpu
from jax.sharding import PartitionSpec as P

HD = 16
BUCKET = 128
EPS = 1e-05
SPAN = 1024
LOG2E = 1.4426950408889634
MESH = pl.DeviceIdType.MESH
F32 = jnp.float32
BF16 = jnp.bfloat16
VMEM = pl.BlockSpec(memory_space=pltpu.VMEM)
ANY = pl.BlockSpec(memory_space=pl.ANY)
SMEM = pl.BlockSpec(memory_space=pltpu.SMEM)
LIMIT = 56 * 1024 * 1024


def dot_nn(a, b):
    return lax.dot_general(a, b, (((1,), (0,)), ((), ())), preferred_element_type=F32)


def dot_nt(a, b):
    return lax.dot_general(a, b, (((1,), (1,)), ((), ())), preferred_element_type=F32)


def dot_tn(a, b):
    return lax.dot_general(a, b, (((0,), (0,)), ((), ())), preferred_element_type=F32)


def split2(x):
    high = x.astype(BF16)
    return high, (x - high.astype(F32)).astype(BF16)


def split3(x):
    high = x.astype(BF16)
    rest = x - high.astype(F32)
    middle = rest.astype(BF16)
    return high, middle, (rest - middle.astype(F32)).astype(BF16)


def left_stack(x):
    a, b, c = split3(x)
    return [a, b, a, b, c, a]


def right_stack(x):
    a, b, c = split3(x)
    return [a, a, b, b, a, c]


def hot_block(code, first, height):
    ids = lax.broadcasted_iota(jnp.int32, (height, code.shape[1]), 0) + first
    return jnp.where(ids == code, 1.0, 0.0).astype(BF16)


def aligned(first, size):
    return pl.ds(pl.multiple_of(first, size), size)


def each(first, last, act):
    def body(j, carry):
        act(j)
        return carry

    lax.fori_loop(first, last, body, 0)


TALLY, POINTS, WGRAD, BACK, GAIN = range(5)
COT, FULL, BRANCH, STATS, TWIN, HALF, SUM = range(7)


def main_kernel(
    ns, nh, owner_ref, points_hbm, cot_hbm, gain_ref, weight_hbm, outw_hbm,
    sizes_ref, mixed_ref, back_ref, wsum_ref, gsum_ref,
    tall, tiles, offsets, windows, arrived, hots, full, cot, code_ref, gain_wide,
    normed, scaled, query, keys, value, gradc, context, grads, weights_all, shares,
    key_t, value_t, branch_out, branch_in, part_out, twin_in, half_out, half_in, pair_out, pair_in, stats_out, stats_in,
    wgrad_out, wgrad_in, gain_out, gain_in, buckets, points_ref, weight_ref, outw_ref,
    local_sem, scan_send, scan_recv, head_send, head_recv,
):
    s, h = lax.axis_index("scan"), lax.axis_index("head")
    nx = nh // 2
    x, core = h // 2, lax.rem(h, 2)
    twin = x * 2 + 1 - core
    width, rows = cot_hbm.shape
    channels = width * nh
    strip = channels // ns
    mine = aligned(h * width, width)

    def remote(src, dst, send, recv, to):
        return pltpu.make_async_remote_copy(
            src_ref=src, dst_ref=dst, send_sem=send, recv_sem=recv, device_id=to, device_id_type=MESH
        )

    def scan_copy(which, j):
        peer = lax.rem(s + j, ns)
        if which == TALLY:
            src, dst = tall.at[pl.ds(peer, 1), :], sizes_ref.at[pl.ds(s, 1), :]
        elif which == POINTS:
            src, dst = windows.at[peer], arrived.at[s]
        elif which == WGRAD:
            src, dst = wgrad_out.at[aligned(peer * strip, strip), :], wgrad_in.at[s]
        elif which == BACK:
            src, dst = buckets.at[peer], back_ref.at[s]
        else:
            src, dst = gain_out, gain_in.at[s]
        return remote(src, dst, scan_send.at[which, j], scan_recv.at[which, j], (peer, h))

    def head_copy(which, j):
        peer = lax.rem(h + j, nh)
        if which == BRANCH:
            src, dst = branch_out.at[aligned(peer * width, width), :], branch_in.at[h]
        else:
            src, dst = stats_out, stats_in.at[h]
        return remote(src, dst, head_send.at[which, j], head_recv.at[which, j], (s, peer))

    def push(which, ref, piece, slot, to):
        block = ref.at[aligned(piece * width, width), :]
        return remote(block, block, head_send.at[which, slot], head_recv.at[which, piece], (s, to))

    left, right, across = lax.rem(x + nx - 1, nx), lax.rem(x + 1, nx), lax.rem(x + 2, nx)
    mid = width // 2

    def half_piece(piece, half, slot, to):
        block = full.at[aligned(piece * width + half * mid, mid), :]
        return remote(block, block, head_send.at[HALF, slot], head_recv.at[HALF, slot], (s, to))

    def spread(which, ref):
        for j in (nx // 2, *[j for j in range(1, nx) if j != nx // 2]):
            push(which, ref, h, j, lax.rem(x + j, nx) * 2 + core).start()
        push(which, ref, h, 0, twin).start()

    def relay(which, ref):
        for j in range(1, nx):
            piece = lax.rem(x + nx - j, nx) * 2 + core
            push(which, ref, piece, nx + j, twin).wait_recv()
            push(which, ref, piece, nx + j, twin).start()

    def arrive(which, ref):
        for j in range(nx):
            piece = lax.rem(x + nx - j, nx) * 2 + 1 - core
            push(which, ref, piece, 0, twin).wait_recv()

    def sent(which, ref):
        for j in range(1, nx):
            push(which, ref, h, j, twin).wait_send()
            push(which, ref, h, nx + j, twin).wait_send()
        push(which, ref, h, 0, twin).wait_send()

    barrier = pltpu.get_barrier_semaphore()

    def greet_scan(j):
        pl.semaphore_signal(
            barrier, inc=1, device_id=(lax.rem(s + j, ns), h), device_id_type=MESH
        )

    def greet_head(j):
        pl.semaphore_signal(
            barrier, inc=1, device_id=(s, lax.rem(h + j, nh)), device_id_type=MESH
        )

    each(1, ns, greet_scan)
    each(1, nh, greet_head)
    fetches = [
        pltpu.make_async_copy(src, dst, local_sem.at[i])
        for i, (src, dst) in enumerate(
            [
                (cot_hbm, cot.at[mine, :]),
                (points_hbm, points_ref),
                (outw_hbm, outw_ref),
                (weight_hbm, weight_ref),
            ]
        )
    ]
    for fetch in fetches:
        fetch.start()
    owners = owner_ref[...]
    hot = lax.broadcasted_iota(jnp.int32, (ns, rows), 0) == owners
    ones = jnp.where(hot, 1.0, 0.0)
    total = jnp.sum(jnp.where(hot, 1, 0), axis=1, keepdims=True)
    tall[...] = jnp.broadcast_to(total, (ns, 128))
    pl.semaphore_wait(barrier, ns + nh - 2)

    each(1, ns, lambda j: scan_copy(TALLY, j).start())
    fetches[0].wait()
    spread(COT, cot)
    sizes_ref[pl.ds(s, 1), :] = tall[pl.ds(s, 1), :]
    before = jnp.where(
        lax.broadcasted_iota(jnp.int32, (128, 128), 0)
        < lax.broadcasted_iota(jnp.int32, (128, 128), 1),
        1.0,
        0.0,
    ).astype(BF16)
    carried = jnp.zeros((ns, 1), F32)
    for b in range(0, rows, 128):
        part = ones[:, b : b + 128]
        running = dot_nn(part.astype(BF16), before) + carried
        rank = jnp.sum(running * part, axis=0, keepdims=True)
        code_ref[:, b : b + 128] = owners[:, b : b + 128] * BUCKET + rank.astype(jnp.int32)
        carried = carried + jnp.sum(part, axis=1, keepdims=True)
    each(1, ns, lambda j: scan_copy(TALLY, j).wait())

    earlier = jnp.where(
        lax.broadcasted_iota(jnp.int32, (ns, ns), 1) < lax.broadcasted_iota(jnp.int32, (ns, ns), 0),
        1.0,
        0.0,
    ).astype(BF16)
    begins = dot_nn(earlier, sizes_ref[...].astype(F32).astype(BF16)).astype(jnp.int32)
    tiles[...] = begins // 128
    offsets[...] = begins - begins // 128 * 128
    span = lax.broadcasted_iota(jnp.int32, (256, 128), 0) - lax.broadcasted_iota(
        jnp.int32, (256, 128), 1
    )
    groups = ns // 4

    def nth_group(i):
        half = (i + 1) // 2
        shift = groups // 2 + half * (lax.rem(i, 2) * 2 - 1)
        return lax.rem(s // 4 + shift + groups, groups)

    def send_group(which, group, last):
        for t in range(4):
            peer = group * 4 + t
            if last:

                @pl.when(peer != s)
                def _():
                    scan_copy(which, lax.rem(peer - s + ns, ns)).start()

            else:
                scan_copy(which, lax.rem(peer - s + ns, ns)).start()

    def cut_and_send(i, last):
        group = nth_group(i)
        places = [
            jnp.broadcast_to(tiles[pl.ds(group * 4 + t, 1), :], (16, 128)).astype(F32).astype(BF16)
            for t in range(4)
        ]
        zero = jnp.zeros((width // 16, 16, 128), BF16)

        held = [zero] * 8
        for n in range(ns + 1):
            tile = points_ref[:, 128 * n : 128 * (n + 1)].reshape(zero.shape)
            for t in range(4):
                if n < ns:
                    held[t] = jnp.where((places[t] == n)[None], tile, held[t])
                if n > 0:
                    held[4 + t] = jnp.where((places[t] == n - 1)[None], tile, held[4 + t])
        low, high = held[:4], held[4:]
        for t in range(4):
            peer = group * 4 + t
            window = jnp.concatenate(
                [low[t].reshape(width, 128), high[t].reshape(width, 128)], axis=1
            )
            pick = jnp.where(span == offsets[pl.ds(peer, 1), :], 1.0, 0.0).astype(BF16)
            windows[peer] = dot_nn(window, pick).astype(BF16)
        send_group(POINTS, group, last)

    for fetch in fetches[1:]:
        fetch.wait()
    each(0, groups - 1, lambda i: cut_and_send(i, False))
    cut_and_send(groups - 1, True)
    arrived[pl.ds(s, 1)] = windows[pl.ds(s, 1)]
    code = code_ref[...]

    def build(i):
        first = pl.multiple_of(i * 256, 256)
        hots[pl.ds(first, 256), :] = hot_block(code, first, 256)

    each(0, ns // 2, build)
    relay(COT, cot)
    gain = jnp.transpose(jnp.broadcast_to(gain_ref[...], (8, channels)))[:, :1]
    gain_wide[...] = jnp.broadcast_to(gain, gain_wide.shape)
    arrive(COT, cot)
    gradc[...] = dot_nn(outw_ref[...], cot[...])

    gathered = jnp.zeros((width, rows), F32)
    for i in range(groups):
        group = nth_group(i)
        for t in range(4):
            source = group * 4 + t

            def landed(source=source):
                scan_copy(POINTS, lax.rem(s - source + ns, ns)).wait_recv()

            if i < groups - 1:
                landed()
            else:
                pl.when(source != s)(landed)
        pieces = jnp.concatenate([arrived[group * 4 + t] for t in range(4)], axis=1)
        gathered = gathered + dot_nn(pieces, hots[aligned(group * 512, 512), :])
    full[mine, :] = gathered.astype(BF16)
    push(FULL, full, h, 1, right * 2 + core).start()
    push(FULL, full, h, 3, left * 2 + core).start()
    push(FULL, full, h, 0, twin).start()
    for at, side, half, to in ((left, 1, 0, right), (right, 3, 1, left)):
        piece = at * 2 + core
        push(FULL, full, piece, nx + side, twin).wait_recv()
        half_piece(piece, half, half, to * 2 + core).start()
        push(FULL, full, piece, nx + side, twin).start()
    for half in range(2):
        half_piece(across * 2 + core, half, half, twin).wait_recv()
        half_piece(across * 2 + core, half, 2 + half, twin).start()
    for at in (x, left, right):
        push(FULL, full, at * 2 + 1 - core, 0, twin).wait_recv()
    for half in range(2):
        half_piece(across * 2 + 1 - core, half, 2 + half, twin).wait_recv()

    floats = full[...].astype(F32)
    mean = jnp.sum(floats, axis=0, keepdims=True) * (1.0 / channels)
    centered = floats - mean
    inv = lax.rsqrt(jnp.sum(centered * centered, axis=0, keepdims=True) * (1.0 / channels) + EPS)
    normed[...] = centered * inv
    scaled[...] = (normed[...] * gain_wide[:, :1]).astype(BF16)
    for i, ref in enumerate((query, keys, value)):
        ref[...] = dot_nn(weight_ref[i], scaled[...])

    def forward(head):
        at = aligned(head * HD, HD)
        q, k, v = query[at, :], keys[at, :], value[at, :]
        key_t[...] = jnp.transpose(jnp.concatenate(left_stack(k), axis=0))
        v_rows = jnp.concatenate(list(split2(v)) + [jnp.ones((HD, rows), BF16)], axis=0)
        for b in range(0, rows, SPAN):
            q_stack = jnp.concatenate(
                right_stack(q[:, b : b + SPAN] * (HD**-0.5 * LOG2E)), axis=0
            )
            scores = dot_nn(key_t[...], q_stack)
            peak = jnp.max(scores, axis=0, keepdims=True)
            weights = jnp.exp2(scores - peak).astype(BF16)
            weights_all[head, :, b : b + SPAN] = weights
            sums = dot_nn(v_rows, weights)
            share = 1.0 / sums[2 * HD : 2 * HD + 1]
            shares[head, :, b : b + SPAN] = share
            ctx = (sums[:HD] + sums[HD : 2 * HD]) * share
            context[at, b : b + SPAN] = ctx

    for head in range(width // HD):
        forward(head)
    context_b = context[...].astype(BF16)
    branch_out[...] = dot_tn(outw_ref[...], context_b).astype(BF16)
    each(1, nh, lambda j: head_copy(BRANCH, j).start())

    def backward(head):
        at = aligned(head * HD, HD)
        q, k, v = query[at, :], keys[at, :], value[at, :]
        row = lax.broadcasted_iota(jnp.int32, (HD, rows), 0)
        ones = jnp.ones((HD, rows), BF16)
        value_t[...] = jnp.transpose(jnp.concatenate(left_stack(v) + [ones], axis=0))
        k_rows = jnp.concatenate(list(split2(k)), axis=0)
        gs = gradc[at, :] * shares[head]
        center = jnp.sum(gs * context[at, :], axis=0, keepdims=True) * (-(HD**-0.5))
        parts = [t.astype(F32) for t in split3(center)]
        tail = jnp.where(
            row == 0, parts[0], jnp.where(row == 1, parts[1], jnp.where(row == 2, parts[2], 0.0))
        ).astype(BF16)
        g_stack = jnp.concatenate(right_stack(gs * HD**-0.5) + [tail], axis=0)
        g_rows = jnp.concatenate(list(split2(gs)), axis=0)
        q_rows = jnp.concatenate(list(split2(q)), axis=0)
        key_grad = jnp.zeros((HD * 2, rows), F32)
        value_grad = jnp.zeros((HD * 2, rows), F32)
        for b in range(0, rows, SPAN):
            weights = weights_all[head, :, b : b + SPAN]
            delta = dot_nn(value_t[...], g_stack[:, b : b + SPAN])
            score_grad = (weights.astype(F32) * delta).astype(BF16)
            value_grad = value_grad + dot_nt(g_rows[:, b : b + SPAN], weights)
            dq = dot_nn(k_rows, score_grad)
            grads[at, b : b + SPAN] = (dq[:HD] + dq[HD:]).astype(BF16)
            key_grad = key_grad + dot_nt(q_rows[:, b : b + SPAN], score_grad)
        k_at = aligned(width + head * HD, HD)
        v_at = aligned(2 * width + head * HD, HD)
        grads[k_at, :] = (key_grad[:HD] + key_grad[HD:]).astype(BF16)
        grads[v_at, :] = (value_grad[:HD] + value_grad[HD:]).astype(BF16)

    for head in range(width // HD):
        backward(head)

    whole = jnp.concatenate([weight_ref[i] for i in range(3)], axis=0)
    part_out[...] = dot_tn(whole, grads[...]).astype(BF16)

    def twin_copy(j):
        to = lax.rem(x + j, nx)
        src = part_out.at[aligned((to * 2 + 1 - core) * width, width), :]
        return remote(src, twin_in.at[j], head_send.at[TWIN, j], head_recv.at[TWIN, j], (s, twin))

    def sum_copy(slot):
        side, half = ((0, 0), (1, 1), (0, 1), (1, 0), (0, 0), (1, 1))[slot]
        if slot < 2:
            src, dst = half_out.at[side], half_in.at[side]
        else:
            rows_of = pl.ds(half * mid, mid)
            src, dst = pair_out.at[side, rows_of, :], pair_in.at[side, rows_of, :]
        to = (right, left)[side] * 2 + core
        return remote(src, dst, head_send.at[SUM, slot], head_recv.at[SUM, slot], (s, to))

    for j in (2, 1, 3, 0):
        twin_copy(j).start()
    weighted = part_out[...].astype(F32) * gain_wide[:, :1]
    stats_out[0:1, :] = jnp.sum(weighted, axis=0, keepdims=True)
    stats_out[1:2, :] = jnp.sum(weighted * normed[...], axis=0, keepdims=True)
    each(1, nh, lambda j: head_copy(STATS, j).start())

    def pair_sum(j):
        twin_copy(j).wait_recv()
        own = part_out[aligned((lax.rem(x + j, nx) * 2 + core) * width, width), :]
        return own.astype(F32) + twin_in[j].astype(F32)

    far_sum = pair_sum(2).astype(BF16)
    half_out[0] = far_sum[:mid]
    half_out[1] = far_sum[mid:]
    sum_copy(0).start()
    sum_copy(1).start()
    to_right, to_left = pair_sum(1), pair_sum(3)
    pair_out[0, mid:, :] = to_right[mid:].astype(BF16)
    sum_copy(2).start()
    pair_out[1, :mid, :] = to_left[:mid].astype(BF16)
    sum_copy(3).start()
    sum_copy(0).wait_recv()
    pair_out[0, :mid, :] = (to_right[:mid] + half_in[0].astype(F32)).astype(BF16)
    sum_copy(4).start()
    sum_copy(1).wait_recv()
    pair_out[1, mid:, :] = (to_left[mid:] + half_in[1].astype(F32)).astype(BF16)
    sum_copy(5).start()
    normed_grad = pair_sum(0)
    wgrad_out[:, : 3 * width] = dot_nt(scaled[...], grads[...]).astype(BF16)
    wgrad_out[:, 3 * width :] = dot_nt(cot[...], context_b).astype(BF16)
    each(1, ns, lambda j: scan_copy(WGRAD, j).start())
    wgrad_in[pl.ds(s, 1)] = wgrad_out[aligned(s * strip, strip), :][None]
    each(1, nh, lambda j: head_copy(BRANCH, j).wait())
    branch = branch_out[mine, :].astype(F32)
    for i in range(1, nh):
        branch = branch + branch_in[lax.rem(h + i, nh)].astype(F32)
    mixed_ref[...] = (full[mine, :].astype(F32) + branch).astype(BF16)
    each(1, nh, lambda j: head_copy(STATS, j).wait())
    stats = stats_out[...]
    for i in range(1, nh):
        stats = stats + stats_in[lax.rem(h + i, nh)]
    for slot in range(2, 6):
        sum_copy(slot).wait_recv()
    normed_grad = normed_grad + pair_in[0].astype(F32) + pair_in[1].astype(F32)
    normed_own = normed[mine, :]
    first, second = stats[0:1] * (1.0 / channels), stats[1:2] * (1.0 / channels)
    grad = inv * (normed_grad * gain_wide[mine, :1] - first - normed_own * second)
    points_grad = (cot[mine, :].astype(F32) + grad).astype(BF16)

    for i in range(groups):
        group = nth_group(i)
        block = dot_nt(points_grad, hots[aligned(group * 512, 512), :]).astype(BF16)
        for t in range(4):
            buckets[group * 4 + t] = block[:, 128 * t : 128 * (t + 1)]
        send_group(BACK, group, i == groups - 1)

    back_ref[pl.ds(s, 1)] = buckets[pl.ds(s, 1)]
    product = normed_grad * normed_own
    folded = product[:, :128]
    for b in range(128, rows, 128):
        folded = folded + product[:, b : b + 128]
    gain_out[...] = jnp.zeros_like(gain_out)
    gain_out[:, :width] = jnp.sum(jnp.transpose(folded), axis=0, keepdims=True)
    each(1, ns, lambda j: scan_copy(GAIN, j).start())
    gain_in[pl.ds(s, 1)] = gain_out[...][None]
    each(1, ns, lambda j: scan_copy(WGRAD, j).wait())
    wsum_ref[...] = jnp.sum(wgrad_in[...].astype(F32), axis=0)
    each(1, ns, lambda j: scan_copy(GAIN, j).wait())
    gsum_ref[...] = jnp.sum(gain_in[...], axis=0)
    sent(COT, cot)
    for slot in (0, 1, 3, nx + 1, nx + 3):
        push(FULL, full, h, slot, twin).wait_send()
    for slot in range(4):
        half_piece(h, 0, slot, twin).wait_send()
    for j in range(nx):
        twin_copy(j).wait_send()
    for slot in range(6):
        sum_copy(slot).wait_send()
    each(1, ns, lambda j: scan_copy(POINTS, j).wait_send())
    each(1, ns, lambda j: scan_copy(BACK, j).wait())


def slots_kernel(
    ns, sizes_ref, back_ref, mixed_in, wsum_ref, gsum_ref,
    mixed_ref, owned_ref, qkv_ref, out_ref, gain_ref, slots,
):
    width = back_ref.shape[1]
    slots[...] = jnp.zeros_like(slots)
    lane = lax.broadcasted_iota(jnp.int32, (width, 128), 1)

    def one(d, begin):
        size = sizes_ref[d, 0]
        tile = begin // 128
        off = begin - tile * 128
        block = jnp.where(lane < size, back_ref[d].astype(F32), 0.0)
        wide = jnp.concatenate([block, jnp.zeros_like(block)], axis=1)
        at = pl.ds(pl.multiple_of(tile * 128, 128), 256)
        slots[:, at] = slots[:, at] + pltpu.roll(wide, off, 1)
        return begin + size

    lax.fori_loop(0, ns, one, jnp.int32(0))
    owned_ref[...] = slots[...].astype(BF16)
    mixed_ref[...] = mixed_in[...]
    for i in range(3):
        qkv_ref[i] = wsum_ref[:, i * width : (i + 1) * width]
    out_ref[...] = wsum_ref[:, 3 * width :]
    gain_ref[...] = gsum_ref[:, :width]


def per_device(owner_ids, owned_points, norm_gain, qkv_weight, out_weight, cotangent):
    ns, nh = lax.axis_size("scan"), lax.axis_size("head")
    nx = nh // 2
    rows = owner_ids.shape[0]
    width, slot_count = owned_points.shape
    channels = width * nh
    strip = channels // ns
    shape = jax.ShapeDtypeStruct
    dma = pltpu.SemaphoreType.DMA
    vmem = pltpu.VMEM
    sizes, mixed, back, wsum, gsum = pl.pallas_call(
        functools.partial(main_kernel, ns, nh),
        out_shape=(
            shape((ns, 128), jnp.int32),
            shape((width, rows), BF16),
            shape((ns, width, BUCKET), BF16),
            shape((strip, 4 * width), F32),
            shape((1, 128), F32),
        ),
        in_specs=[VMEM, ANY, ANY, VMEM, ANY, ANY],
        out_specs=(VMEM,) * 5,
        scratch_shapes=[
            vmem((ns, 128), jnp.int32),
            vmem((ns, 128), jnp.int32),
            vmem((ns, 128), jnp.int32),
            vmem((ns, width, BUCKET), BF16),
            vmem((ns, width, BUCKET), BF16),
            vmem((ns * BUCKET, rows), BF16),
            vmem((channels, rows), BF16),
            vmem((channels, rows), BF16),
            vmem((1, rows), jnp.int32),
            vmem((channels, 128), F32),
            vmem((channels, rows), F32),
            vmem((channels, rows), BF16),
            vmem((width, rows), F32),
            vmem((width, rows), F32),
            vmem((width, rows), F32),
            vmem((width, rows), F32),
            vmem((width, rows), F32),
            vmem((3 * width, rows), BF16),
            vmem((width // HD, rows, rows), BF16),
            vmem((width // HD, 1, rows), F32),
            vmem((rows, 6 * HD), BF16),
            vmem((rows, 7 * HD), BF16),
            vmem((channels, rows), BF16),
            vmem((nh, width, rows), BF16),
            vmem((channels, rows), BF16),
            vmem((nx, width, rows), BF16),
            vmem((2, width // 2, rows), BF16),
            vmem((2, width // 2, rows), BF16),
            vmem((2, width, rows), BF16),
            vmem((2, width, rows), BF16),
            vmem((2, rows), F32),
            vmem((nh, 2, rows), F32),
            vmem((channels, 4 * width), BF16),
            vmem((ns, strip, 4 * width), BF16),
            vmem((1, 128), F32),
            vmem((ns, 1, 128), F32),
            vmem((ns, width, BUCKET), BF16),
            vmem((width, slot_count), BF16),
            vmem((3, width, channels), BF16),
            vmem((width, channels), BF16),
            dma((4,)),
            dma((5, ns)),
            dma((5, ns)),
            dma((7, nh)),
            dma((7, nh)),
        ],
        compiler_params=pltpu.CompilerParams(
            collective_id=1, has_side_effects=True, vmem_limit_bytes=LIMIT
        ),
        name="patch_block",
    )(owner_ids.reshape(1, rows), owned_points, cotangent, norm_gain.reshape(1, channels), qkv_weight, out_weight)
    mixed_rows, grad_owned, qkv_grad, out_grad, gain_grad = pl.pallas_call(
        functools.partial(slots_kernel, ns),
        out_shape=(
            shape((width, rows), BF16),
            shape((width, slot_count), BF16),
            shape((3, strip, width), F32),
            shape((strip, width), F32),
            shape((1, width), F32),
        ),
        in_specs=[SMEM] + [VMEM] * 4,
        out_specs=(VMEM,) * 5,
        scratch_shapes=[vmem((width, slot_count), F32)],
        compiler_params=pltpu.CompilerParams(vmem_limit_bytes=LIMIT),
        name="slots",
    )(sizes, back, mixed, wsum, gsum)
    return (
        mixed_rows,
        grad_owned,
        qkv_grad.transpose(0, 2, 1),
        out_grad.T,
        gain_grad.reshape(width),
    )


def solution(mesh):
    in_specs = (
        P("scan", None),
        P("head", "scan"),
        P(),
        P(None, "head", None),
        P("head", None),
        P("head", "scan"),
    )
    out_specs = (
        P("head", "scan"),
        P("head", "scan"),
        P(None, "head", "scan"),
        P("head", "scan"),
        P("head"),
    )
    return jax.shard_map(
        per_device, mesh=mesh, in_specs=in_specs, out_specs=out_specs, check_vma=False
    )
```

```python
import functools

import jax
import jax.numpy as jnp
from jax import lax
from jax.experimental import pallas as pl
from jax.experimental.pallas import tpu as pltpu
from jax.sharding import PartitionSpec as P

HD = 16
BUCKET = 128
EPS = 1e-05
SPAN = 1024
LOG2E = 1.4426950408889634
MESH = pl.DeviceIdType.MESH
F32 = jnp.float32
BF16 = jnp.bfloat16
VMEM = pl.BlockSpec(memory_space=pltpu.VMEM)
ANY = pl.BlockSpec(memory_space=pl.ANY)
SMEM = pl.BlockSpec(memory_space=pltpu.SMEM)
LIMIT = 56 * 1024 * 1024


def dot_nn(a, b):
    return lax.dot_general(a, b, (((1,), (0,)), ((), ())), preferred_element_type=F32)


def dot_nt(a, b):
    return lax.dot_general(a, b, (((1,), (1,)), ((), ())), preferred_element_type=F32)


def dot_tn(a, b):
    return lax.dot_general(a, b, (((0,), (0,)), ((), ())), preferred_element_type=F32)


def split2(x):
    high = x.astype(BF16)
    return high, (x - high.astype(F32)).astype(BF16)


def split3(x):
    high = x.astype(BF16)
    rest = x - high.astype(F32)
    middle = rest.astype(BF16)
    return high, middle, (rest - middle.astype(F32)).astype(BF16)


def left_stack(x):
    a, b, c = split3(x)
    return [a, b, a, b, c, a]


def right_stack(x):
    a, b, c = split3(x)
    return [a, a, b, b, a, c]


def hot_block(code, first, height):
    ids = lax.broadcasted_iota(jnp.int32, (height, code.shape[1]), 0) + first
    return jnp.where(ids == code, 1.0, 0.0).astype(BF16)


def aligned(first, size):
    return pl.ds(pl.multiple_of(first, size), size)


def each(first, last, act, unroll=True):
    def body(j, carry):
        act(j)
        return carry

    lax.fori_loop(first, last, body, 0, unroll=unroll)


TALLY, POINTS, WGRAD, BACK, GAIN = range(5)
COT, FULL, STATS, HALF, TWIN, _, SUM, _ = range(8)


def main_kernel(
    ns, nh, owner_ref, points_hbm, cot_hbm, gain_ref, weight_hbm, outw_hbm,
    sizes_ref, mixed_ref, back_ref, wsum_ref, gsum_ref,
    tall, tiles, offsets, windows, arrived, hots, full, cot, code_ref, gain_wide,
    normed, scaled, query, keys, value, gradc, context, grads, weights_all, shares,
    key_t, value_t, branch_out, near, part_out, twin_in, half_out, half_in, pair_out, pair_in, stats_out, stats_in,
    wgrad_out, wgrad_in, gain_out, gain_in, buckets, points_ref, weight_ref, outw_ref,
    local_sem, scan_send, scan_recv, head_send, head_recv,
):
    s, h = lax.axis_index("scan"), lax.axis_index("head")
    nx = nh // 2
    x, core = h // 2, lax.rem(h, 2)
    twin = x * 2 + 1 - core
    width, rows = cot_hbm.shape
    channels = width * nh
    strip = channels // ns
    mine = aligned(h * width, width)

    def remote(src, dst, send, recv, to):
        return pltpu.make_async_remote_copy(
            src_ref=src, dst_ref=dst, send_sem=send, recv_sem=recv, device_id=to, device_id_type=MESH
        )

    def scan_copy(which, j):
        peer = lax.rem(s + j, ns)
        if which == TALLY:
            src, dst = tall.at[pl.ds(peer, 1), :], sizes_ref.at[pl.ds(s, 1), :]
        elif which == POINTS:
            src, dst = windows.at[peer], arrived.at[s]
        elif which == WGRAD:
            src, dst = wgrad_out.at[aligned(peer * strip, strip), :], wgrad_in.at[s]
        elif which == BACK:
            src, dst = buckets.at[peer], back_ref.at[s]
        else:
            src, dst = gain_out, gain_in.at[s]
        return remote(src, dst, scan_send.at[which, j], scan_recv.at[which, j], (peer, h))

    def stats_copy(j):
        peer = lax.rem(h + j, nh)
        return remote(
            stats_out, stats_in.at[h], head_send.at[STATS, j], head_recv.at[STATS, j], (s, peer)
        )

    def push(which, ref, piece, slot, to):
        block = ref.at[aligned(piece * width, width), :]
        return remote(block, block, head_send.at[which, slot], head_recv.at[which, piece], (s, to))

    left, right, across = lax.rem(x + nx - 1, nx), lax.rem(x + 1, nx), lax.rem(x + 2, nx)
    mid = width // 2

    def half_piece(piece, half, slot, to):
        block = full.at[aligned(piece * width + half * mid, mid), :]
        return remote(block, block, head_send.at[HALF, slot], head_recv.at[HALF, slot], (s, to))

    def spread(which, ref):
        for j in (nx // 2, *[j for j in range(1, nx) if j != nx // 2]):
            push(which, ref, h, j, lax.rem(x + j, nx) * 2 + core).start()
        push(which, ref, h, 0, twin).start()

    def relay(which, ref):
        for j in range(1, nx):
            piece = lax.rem(x + nx - j, nx) * 2 + core
            push(which, ref, piece, nx + j, twin).wait_recv()
            push(which, ref, piece, nx + j, twin).start()

    def arrive(which, ref):
        for j in range(nx):
            piece = lax.rem(x + nx - j, nx) * 2 + 1 - core
            push(which, ref, piece, 0, twin).wait_recv()

    def sent(which, ref):
        for j in range(1, nx):
            push(which, ref, h, j, twin).wait_send()
            push(which, ref, h, nx + j, twin).wait_send()
        push(which, ref, h, 0, twin).wait_send()

    def twin_copy(k, j):
        to = lax.rem(x + j, nx)
        src = (part_out, branch_out)[k].at[aligned((to * 2 + 1 - core) * width, width), :]
        dst = twin_in.at[k, j]
        return remote(src, dst, head_send.at[TWIN + k, j], head_recv.at[TWIN + k, j], (s, twin))

    def sum_copy(k, slot):
        side, half = ((0, 0), (1, 1), (0, 1), (1, 0), (0, 0), (1, 1))[slot]
        if slot < 2:
            src, dst = half_out.at[k, side], half_in.at[k, side]
        else:
            rows_of = pl.ds(half * mid, mid)
            src, dst = pair_out.at[k, side, rows_of, :], pair_in.at[k, side, rows_of, :]
        to = (right, left)[side] * 2 + core
        return remote(src, dst, head_send.at[SUM + k, slot], head_recv.at[SUM + k, slot], (s, to))

    def pair_sum(k, j):
        twin_copy(k, j).wait_recv()
        ref = (part_out, branch_out)[k]
        own = ref[aligned((lax.rem(x + j, nx) * 2 + core) * width, width), :]
        return own.astype(F32) + twin_in[k, j].astype(F32)

    def sum_begin(k):
        for j in (2, 1, 3, 0):
            twin_copy(k, j).start()

    def sum_far(k):
        far_sum = pair_sum(k, 2).astype(BF16)
        half_out[k, 0] = far_sum[:mid]
        half_out[k, 1] = far_sum[mid:]
        sum_copy(k, 0).start()
        sum_copy(k, 1).start()
        to_right, to_left = pair_sum(k, 1), pair_sum(k, 3)
        pair_out[k, 0, mid:, :] = to_right[mid:].astype(BF16)
        sum_copy(k, 2).start()
        pair_out[k, 1, :mid, :] = to_left[:mid].astype(BF16)
        sum_copy(k, 3).start()
        near[k, 0] = to_right[:mid]
        near[k, 1] = to_left[mid:]

    def sum_near(k):
        sum_copy(k, 0).wait_recv()
        pair_out[k, 0, :mid, :] = (near[k, 0] + half_in[k, 0].astype(F32)).astype(BF16)
        sum_copy(k, 4).start()
        sum_copy(k, 1).wait_recv()
        pair_out[k, 1, mid:, :] = (near[k, 1] + half_in[k, 1].astype(F32)).astype(BF16)
        sum_copy(k, 5).start()

    def sum_end(k):
        own = pair_sum(k, 0)
        for slot in range(2, 6):
            sum_copy(k, slot).wait_recv()
        return own + pair_in[k, 0].astype(F32) + pair_in[k, 1].astype(F32)

    def sum_sent(k):
        for j in range(nx):
            twin_copy(k, j).wait_send()
        for slot in range(6):
            sum_copy(k, slot).wait_send()

    barrier = pltpu.get_barrier_semaphore()

    def greet_scan(j):
        pl.semaphore_signal(
            barrier, inc=1, device_id=(lax.rem(s + j, ns), h), device_id_type=MESH
        )

    def greet_head(j):
        pl.semaphore_signal(
            barrier, inc=1, device_id=(s, lax.rem(h + j, nh)), device_id_type=MESH
        )

    each(1, ns, greet_scan)
    each(1, nh, greet_head)
    fetches = [
        pltpu.make_async_copy(src, dst, local_sem.at[i])
        for i, (src, dst) in enumerate(
            [
                (cot_hbm, cot.at[mine, :]),
                (points_hbm, points_ref),
                (outw_hbm, outw_ref),
                (weight_hbm, weight_ref),
            ]
        )
    ]
    for fetch in fetches:
        fetch.start()
    owners = owner_ref[...]
    hot = lax.broadcasted_iota(jnp.int32, (ns, rows), 0) == owners
    ones = jnp.where(hot, 1.0, 0.0)
    total = jnp.sum(jnp.where(hot, 1, 0), axis=1, keepdims=True)
    tall[...] = jnp.broadcast_to(total, (ns, 128))
    pl.semaphore_wait(barrier, ns + nh - 2)

    each(1, ns, lambda j: scan_copy(TALLY, j).start())
    fetches[0].wait()
    spread(COT, cot)
    sizes_ref[pl.ds(s, 1), :] = tall[pl.ds(s, 1), :]
    before = jnp.where(
        lax.broadcasted_iota(jnp.int32, (128, 128), 0)
        < lax.broadcasted_iota(jnp.int32, (128, 128), 1),
        1.0,
        0.0,
    ).astype(BF16)
    carried = jnp.zeros((ns, 1), F32)
    for b in range(0, rows, 128):
        part = ones[:, b : b + 128]
        running = dot_nn(part.astype(BF16), before) + carried
        rank = jnp.sum(running * part, axis=0, keepdims=True)
        code_ref[:, b : b + 128] = owners[:, b : b + 128] * BUCKET + rank.astype(jnp.int32)
        carried = carried + jnp.sum(part, axis=1, keepdims=True)
    each(1, ns, lambda j: scan_copy(TALLY, j).wait())

    earlier = jnp.where(
        lax.broadcasted_iota(jnp.int32, (ns, ns), 1) < lax.broadcasted_iota(jnp.int32, (ns, ns), 0),
        1.0,
        0.0,
    ).astype(BF16)
    begins = dot_nn(earlier, sizes_ref[...].astype(F32).astype(BF16)).astype(jnp.int32)
    tiles[...] = begins // 128
    offsets[...] = begins - begins // 128 * 128
    span = lax.broadcasted_iota(jnp.int32, (256, 128), 0) - lax.broadcasted_iota(
        jnp.int32, (256, 128), 1
    )
    groups = ns // 4

    def nth_group(i):
        half = (i + 1) // 2
        shift = groups // 2 + half * (lax.rem(i, 2) * 2 - 1)
        return lax.rem(s // 4 + shift + groups, groups)

    def send_group(which, group, last):
        for t in range(4):
            peer = group * 4 + t
            if last:

                @pl.when(peer != s)
                def _():
                    scan_copy(which, lax.rem(peer - s + ns, ns)).start()

            else:
                scan_copy(which, lax.rem(peer - s + ns, ns)).start()

    def cut_and_send(i, last):
        group = nth_group(i)
        places = [
            jnp.broadcast_to(tiles[pl.ds(group * 4 + t, 1), :], (16, 128)).astype(F32).astype(BF16)
            for t in range(4)
        ]
        zero = jnp.zeros((width // 16, 16, 128), BF16)

        held = [zero] * 8
        for n in range(ns + 1):
            tile = points_ref[:, 128 * n : 128 * (n + 1)].reshape(zero.shape)
            for t in range(4):
                if n < ns:
                    held[t] = jnp.where((places[t] == n)[None], tile, held[t])
                if n > 0:
                    held[4 + t] = jnp.where((places[t] == n - 1)[None], tile, held[4 + t])
        low, high = held[:4], held[4:]
        for t in range(4):
            peer = group * 4 + t
            window = jnp.concatenate(
                [low[t].reshape(width, 128), high[t].reshape(width, 128)], axis=1
            )
            pick = jnp.where(span == offsets[pl.ds(peer, 1), :], 1.0, 0.0).astype(BF16)
            windows[peer] = dot_nn(window, pick).astype(BF16)
        send_group(POINTS, group, last)

    for fetch in fetches[1:]:
        fetch.wait()
    each(0, groups - 1, lambda i: cut_and_send(i, False), False)
    cut_and_send(groups - 1, True)
    arrived[pl.ds(s, 1)] = windows[pl.ds(s, 1)]
    code = code_ref[...]

    def build(i):
        first = pl.multiple_of(i * 256, 256)
        hots[pl.ds(first, 256), :] = hot_block(code, first, 256)

    each(0, ns // 2, build)
    relay(COT, cot)
    gain = jnp.transpose(jnp.broadcast_to(gain_ref[...], (8, channels)))[:, :1]
    gain_wide[...] = jnp.broadcast_to(gain, gain_wide.shape)
    arrive(COT, cot)
    gradc[...] = dot_nn(outw_ref[...], cot[...])

    gathered = jnp.zeros((width, rows), F32)
    for i in range(groups):
        group = nth_group(i)
        for t in range(4):
            source = group * 4 + t

            def landed(source=source):
                scan_copy(POINTS, lax.rem(s - source + ns, ns)).wait_recv()

            if i < groups - 1:
                landed()
            else:
                pl.when(source != s)(landed)
        pieces = jnp.concatenate([arrived[group * 4 + t] for t in range(4)], axis=1)
        gathered = gathered + dot_nn(pieces, hots[aligned(group * 512, 512), :])
    full[mine, :] = gathered.astype(BF16)
    push(FULL, full, h, 1, right * 2 + core).start()
    push(FULL, full, h, 3, left * 2 + core).start()
    push(FULL, full, h, 0, twin).start()
    for at, side, half, to in ((left, 1, 0, right), (right, 3, 1, left)):
        piece = at * 2 + core
        push(FULL, full, piece, nx + side, twin).wait_recv()
        half_piece(piece, half, half, to * 2 + core).start()
        push(FULL, full, piece, nx + side, twin).start()
    for half in range(2):
        half_piece(across * 2 + core, half, half, twin).wait_recv()
        half_piece(across * 2 + core, half, 2 + half, twin).start()
    for at in (x, left, right):
        push(FULL, full, at * 2 + 1 - core, 0, twin).wait_recv()
    for half in range(2):
        half_piece(across * 2 + 1 - core, half, 2 + half, twin).wait_recv()

    floats = full[...].astype(F32)
    mean = jnp.sum(floats, axis=0, keepdims=True) * (1.0 / channels)
    centered = floats - mean
    inv = lax.rsqrt(jnp.sum(centered * centered, axis=0, keepdims=True) * (1.0 / channels) + EPS)
    normed[...] = centered * inv
    scaled[...] = (normed[...] * gain_wide[:, :1]).astype(BF16)
    for i, ref in enumerate((query, keys, value)):
        ref[...] = dot_nn(weight_ref[i], scaled[...])

    def forward(head):
        at = aligned(head * HD, HD)
        q, k, v = query[at, :], keys[at, :], value[at, :]
        key_t[...] = jnp.transpose(jnp.concatenate(left_stack(k), axis=0))
        v_rows = jnp.concatenate(list(split2(v)) + [jnp.ones((HD, rows), BF16)], axis=0)
        for b in range(0, rows, SPAN):
            q_stack = jnp.concatenate(
                right_stack(q[:, b : b + SPAN] * (HD**-0.5 * LOG2E)), axis=0
            )
            scores = dot_nn(key_t[...], q_stack)
            peak = jnp.max(scores, axis=0, keepdims=True)
            weights = jnp.exp2(scores - peak).astype(BF16)
            weights_all[head, :, b : b + SPAN] = weights
            sums = dot_nn(v_rows, weights)
            share = 1.0 / sums[2 * HD : 2 * HD + 1]
            shares[head, :, b : b + SPAN] = share
            ctx = (sums[:HD] + sums[HD : 2 * HD]) * share
            context[at, b : b + SPAN] = ctx

    for head in range(width // HD):
        forward(head)
    context_b = context[...].astype(BF16)
    branch_out[...] = dot_tn(outw_ref[...], context_b).astype(BF16)
    sum_begin(1)

    def backward(head):
        at = aligned(head * HD, HD)
        q, k, v = query[at, :], keys[at, :], value[at, :]
        row = lax.broadcasted_iota(jnp.int32, (HD, rows), 0)
        ones = jnp.ones((HD, rows), BF16)
        value_t[...] = jnp.transpose(jnp.concatenate(left_stack(v) + [ones], axis=0))
        k_rows = jnp.concatenate(list(split2(k)), axis=0)
        gs = gradc[at, :] * shares[head]
        center = jnp.sum(gs * context[at, :], axis=0, keepdims=True) * (-(HD**-0.5))
        parts = [t.astype(F32) for t in split3(center)]
        tail = jnp.where(
            row == 0, parts[0], jnp.where(row == 1, parts[1], jnp.where(row == 2, parts[2], 0.0))
        ).astype(BF16)
        g_stack = jnp.concatenate(right_stack(gs * HD**-0.5) + [tail], axis=0)
        g_rows = jnp.concatenate(list(split2(gs)), axis=0)
        q_rows = jnp.concatenate(list(split2(q)), axis=0)
        key_grad = jnp.zeros((HD * 2, rows), F32)
        value_grad = jnp.zeros((HD * 2, rows), F32)
        for b in range(0, rows, SPAN):
            weights = weights_all[head, :, b : b + SPAN]
            delta = dot_nn(value_t[...], g_stack[:, b : b + SPAN])
            score_grad = (weights.astype(F32) * delta).astype(BF16)
            value_grad = value_grad + dot_nt(g_rows[:, b : b + SPAN], weights)
            dq = dot_nn(k_rows, score_grad)
            grads[at, b : b + SPAN] = (dq[:HD] + dq[HD:]).astype(BF16)
            key_grad = key_grad + dot_nt(q_rows[:, b : b + SPAN], score_grad)
        k_at = aligned(width + head * HD, HD)
        v_at = aligned(2 * width + head * HD, HD)
        grads[k_at, :] = (key_grad[:HD] + key_grad[HD:]).astype(BF16)
        grads[v_at, :] = (value_grad[:HD] + value_grad[HD:]).astype(BF16)

    for head in range(width // HD):
        backward(head)
        if head == 0:
            sum_far(1)
        elif head == 1:
            sum_near(1)

    whole = jnp.concatenate([weight_ref[i] for i in range(3)], axis=0)
    part_out[...] = dot_tn(whole, grads[...]).astype(BF16)

    sum_begin(0)
    weighted = part_out[...].astype(F32) * gain_wide[:, :1]
    stats_out[0:1, :] = jnp.sum(weighted, axis=0, keepdims=True)
    stats_out[1:2, :] = jnp.sum(weighted * normed[...], axis=0, keepdims=True)
    each(1, nh, lambda j: stats_copy(j).start())

    sum_far(0)
    sum_near(0)
    wgrad_out[:, : 3 * width] = dot_nt(scaled[...], grads[...]).astype(BF16)
    wgrad_out[:, 3 * width :] = dot_nt(cot[...], context_b).astype(BF16)
    each(1, ns, lambda j: scan_copy(WGRAD, j).start())
    wgrad_in[pl.ds(s, 1)] = wgrad_out[aligned(s * strip, strip), :][None]
    branch = sum_end(1)
    mixed_ref[...] = (full[mine, :].astype(F32) + branch).astype(BF16)
    each(1, nh, lambda j: stats_copy(j).wait())
    stats = stats_out[...]
    for i in range(1, nh):
        stats = stats + stats_in[lax.rem(h + i, nh)]
    normed_grad = sum_end(0)
    normed_own = normed[mine, :]
    first, second = stats[0:1] * (1.0 / channels), stats[1:2] * (1.0 / channels)
    grad = inv * (normed_grad * gain_wide[mine, :1] - first - normed_own * second)
    points_grad = (cot[mine, :].astype(F32) + grad).astype(BF16)

    for i in range(groups):
        group = nth_group(i)
        block = dot_nt(points_grad, hots[aligned(group * 512, 512), :]).astype(BF16)
        for t in range(4):
            buckets[group * 4 + t] = block[:, 128 * t : 128 * (t + 1)]
        send_group(BACK, group, i == groups - 1)

    back_ref[pl.ds(s, 1)] = buckets[pl.ds(s, 1)]
    product = normed_grad * normed_own
    folded = product[:, :128]
    for b in range(128, rows, 128):
        folded = folded + product[:, b : b + 128]
    gain_out[...] = jnp.zeros_like(gain_out)
    gain_out[:, :width] = jnp.sum(jnp.transpose(folded), axis=0, keepdims=True)
    each(1, ns, lambda j: scan_copy(GAIN, j).start())
    gain_in[pl.ds(s, 1)] = gain_out[...][None]
    each(1, ns, lambda j: scan_copy(WGRAD, j).wait())
    wsum_ref[...] = jnp.sum(wgrad_in[...].astype(F32), axis=0)
    each(1, ns, lambda j: scan_copy(GAIN, j).wait())
    gsum_ref[...] = jnp.sum(gain_in[...], axis=0)
    sent(COT, cot)
    for slot in (0, 1, 3, nx + 1, nx + 3):
        push(FULL, full, h, slot, twin).wait_send()
    for slot in range(4):
        half_piece(h, 0, slot, twin).wait_send()
    sum_sent(0)
    sum_sent(1)
    each(1, ns, lambda j: scan_copy(POINTS, j).wait_send())
    each(1, ns, lambda j: scan_copy(BACK, j).wait())


def slots_kernel(
    ns, sizes_ref, back_ref, mixed_in, wsum_ref, gsum_ref,
    mixed_ref, owned_ref, qkv_ref, out_ref, gain_ref, slots,
):
    width = back_ref.shape[1]
    slots[...] = jnp.zeros_like(slots)
    lane = lax.broadcasted_iota(jnp.int32, (width, 128), 1)

    def one(d, begin):
        size = sizes_ref[d, 0]
        tile = begin // 128
        off = begin - tile * 128
        block = jnp.where(lane < size, back_ref[d].astype(F32), 0.0)
        wide = jnp.concatenate([block, jnp.zeros_like(block)], axis=1)
        at = pl.ds(pl.multiple_of(tile * 128, 128), 256)
        slots[:, at] = slots[:, at] + pltpu.roll(wide, off, 1)
        return begin + size

    lax.fori_loop(0, ns, one, jnp.int32(0))
    owned_ref[...] = slots[...].astype(BF16)
    mixed_ref[...] = mixed_in[...]
    for i in range(3):
        qkv_ref[i] = wsum_ref[:, i * width : (i + 1) * width]
    out_ref[...] = wsum_ref[:, 3 * width :]
    gain_ref[...] = gsum_ref[:, :width]


def per_device(owner_ids, owned_points, norm_gain, qkv_weight, out_weight, cotangent):
    ns, nh = lax.axis_size("scan"), lax.axis_size("head")
    nx = nh // 2
    rows = owner_ids.shape[0]
    width, slot_count = owned_points.shape
    channels = width * nh
    strip = channels // ns
    shape = jax.ShapeDtypeStruct
    dma = pltpu.SemaphoreType.DMA
    vmem = pltpu.VMEM
    sizes, mixed, back, wsum, gsum = pl.pallas_call(
        functools.partial(main_kernel, ns, nh),
        out_shape=(
            shape((ns, 128), jnp.int32),
            shape((width, rows), BF16),
            shape((ns, width, BUCKET), BF16),
            shape((strip, 4 * width), F32),
            shape((1, 128), F32),
        ),
        in_specs=[VMEM, ANY, ANY, VMEM, ANY, ANY],
        out_specs=(VMEM,) * 5,
        scratch_shapes=[
            vmem((ns, 128), jnp.int32),
            vmem((ns, 128), jnp.int32),
            vmem((ns, 128), jnp.int32),
            vmem((ns, width, BUCKET), BF16),
            vmem((ns, width, BUCKET), BF16),
            vmem((ns * BUCKET, rows), BF16),
            vmem((channels, rows), BF16),
            vmem((channels, rows), BF16),
            vmem((1, rows), jnp.int32),
            vmem((channels, 128), F32),
            vmem((channels, rows), F32),
            vmem((channels, rows), BF16),
            vmem((width, rows), F32),
            vmem((width, rows), F32),
            vmem((width, rows), F32),
            vmem((width, rows), F32),
            vmem((width, rows), F32),
            vmem((3 * width, rows), BF16),
            vmem((width // HD, rows, rows), BF16),
            vmem((width // HD, 1, rows), F32),
            vmem((rows, 6 * HD), BF16),
            vmem((rows, 7 * HD), BF16),
            vmem((channels, rows), BF16),
            vmem((2, 2, width // 2, rows), F32),
            vmem((channels, rows), BF16),
            vmem((2, nx, width, rows), BF16),
            vmem((2, 2, width // 2, rows), BF16),
            vmem((2, 2, width // 2, rows), BF16),
            vmem((2, 2, width, rows), BF16),
            vmem((2, 2, width, rows), BF16),
            vmem((2, rows), F32),
            vmem((nh, 2, rows), F32),
            vmem((channels, 4 * width), BF16),
            vmem((ns, strip, 4 * width), BF16),
            vmem((1, 128), F32),
            vmem((ns, 1, 128), F32),
            vmem((ns, width, BUCKET), BF16),
            vmem((width, slot_count), BF16),
            vmem((3, width, channels), BF16),
            vmem((width, channels), BF16),
            dma((4,)),
            dma((5, ns)),
            dma((5, ns)),
            dma((8, nh)),
            dma((8, nh)),
        ],
        compiler_params=pltpu.CompilerParams(
            collective_id=1, has_side_effects=True, vmem_limit_bytes=LIMIT
        ),
        name="patch_block",
    )(owner_ids.reshape(1, rows), owned_points, cotangent, norm_gain.reshape(1, channels), qkv_weight, out_weight)
    mixed_rows, grad_owned, qkv_grad, out_grad, gain_grad = pl.pallas_call(
        functools.partial(slots_kernel, ns),
        out_shape=(
            shape((width, rows), BF16),
            shape((width, slot_count), BF16),
            shape((3, strip, width), F32),
            shape((strip, width), F32),
            shape((1, width), F32),
        ),
        in_specs=[SMEM] + [VMEM] * 4,
        out_specs=(VMEM,) * 5,
        scratch_shapes=[vmem((width, slot_count), F32)],
        compiler_params=pltpu.CompilerParams(vmem_limit_bytes=LIMIT),
        name="slots",
    )(sizes, back, mixed, wsum, gsum)
    return (
        mixed_rows,
        grad_owned,
        qkv_grad.transpose(0, 2, 1),
        out_grad.T,
        gain_grad.reshape(width),
    )


def solution(mesh):
    in_specs = (
        P("scan", None),
        P("head", "scan"),
        P(),
        P(None, "head", None),
        P("head", None),
        P("head", "scan"),
    )
    out_specs = (
        P("head", "scan"),
        P("head", "scan"),
        P(None, "head", "scan"),
        P("head", "scan"),
        P("head"),
    )
    return jax.shard_map(
        per_device, mesh=mesh, in_specs=in_specs, out_specs=out_specs, check_vma=False
    )
```

```python
import functools

import jax
import jax.numpy as jnp
from jax import lax
from jax.experimental import pallas as pl
from jax.experimental.pallas import tpu as pltpu
from jax.sharding import PartitionSpec as P

HD = 16
BUCKET = 128
EPS = 1e-05
SPAN = 1024
LOG2E = 1.4426950408889634
MESH = pl.DeviceIdType.MESH
F32 = jnp.float32
BF16 = jnp.bfloat16
VMEM = pl.BlockSpec(memory_space=pltpu.VMEM)
ANY = pl.BlockSpec(memory_space=pl.ANY)
SMEM = pl.BlockSpec(memory_space=pltpu.SMEM)
LIMIT = 56 * 1024 * 1024


def dot_nn(a, b):
    return lax.dot_general(a, b, (((1,), (0,)), ((), ())), preferred_element_type=F32)


def dot_nt(a, b):
    return lax.dot_general(a, b, (((1,), (1,)), ((), ())), preferred_element_type=F32)


def dot_tn(a, b):
    return lax.dot_general(a, b, (((0,), (0,)), ((), ())), preferred_element_type=F32)


def split2(x):
    high = x.astype(BF16)
    return high, (x - high.astype(F32)).astype(BF16)


def split3(x):
    high = x.astype(BF16)
    rest = x - high.astype(F32)
    middle = rest.astype(BF16)
    return high, middle, (rest - middle.astype(F32)).astype(BF16)


def left_stack(x):
    a, b, c = split3(x)
    return [a, b, a, b, c, a]


def right_stack(x):
    a, b, c = split3(x)
    return [a, a, b, b, a, c]


def hot_block(code, first, height):
    ids = lax.broadcasted_iota(jnp.int32, (height, code.shape[1]), 0) + first
    return jnp.where(ids == code, 1.0, 0.0).astype(BF16)


def aligned(first, size):
    return pl.ds(pl.multiple_of(first, size), size)


def each(first, last, act, unroll=True):
    def body(j, carry):
        act(j)
        return carry

    lax.fori_loop(first, last, body, 0, unroll=unroll)


TALLY, POINTS, WGRAD, BACK, GAIN = range(5)
COT, FULL, STATS, HALF, TWIN, _, SUM, _ = range(8)


def main_kernel(
    ns, nh, owner_ref, points_hbm, cot_hbm, gain_ref, weight_hbm, outw_hbm,
    sizes_ref, mixed_ref, back_ref, wsum_ref, gsum_ref,
    tall, tiles, offsets, windows, arrived, hots, full, cot, code_ref, gain_wide,
    normed, scaled, query, keys, value, gradc, context, grads, weights_all, shares,
    key_t, value_t, branch_out, near, part_out, twin_in, half_out, half_in, pair_out, pair_in, stats_out, stats_in,
    wgrad_out, wgrad_in, gain_out, gain_in, buckets, points_ref, weight_ref, outw_ref,
    local_sem, scan_send, scan_recv, head_send, head_recv,
):
    s, h = lax.axis_index("scan"), lax.axis_index("head")
    nx = nh // 2
    x, core = h // 2, lax.rem(h, 2)
    twin = x * 2 + 1 - core
    width, rows = cot_hbm.shape
    channels = width * nh
    strip = channels // ns
    mine = aligned(h * width, width)

    def remote(src, dst, send, recv, to):
        return pltpu.make_async_remote_copy(
            src_ref=src, dst_ref=dst, send_sem=send, recv_sem=recv, device_id=to, device_id_type=MESH
        )

    def scan_copy(which, j):
        peer = lax.rem(s + j, ns)
        if which == TALLY:
            src, dst = tall.at[pl.ds(peer, 1), :], sizes_ref.at[pl.ds(s, 1), :]
        elif which == POINTS:
            src, dst = windows.at[peer], arrived.at[s]
        elif which == WGRAD:
            src, dst = wgrad_out.at[aligned(peer * strip, strip), :], wgrad_in.at[s]
        elif which == BACK:
            src, dst = buckets.at[peer], back_ref.at[s]
        else:
            src, dst = gain_out, gain_in.at[s]
        return remote(src, dst, scan_send.at[which, j], scan_recv.at[which, j], (peer, h))

    def stats_copy(j):
        peer = lax.rem(h + j, nh)
        return remote(
            stats_out, stats_in.at[h], head_send.at[STATS, j], head_recv.at[STATS, j], (s, peer)
        )

    def push(which, ref, piece, slot, to):
        block = ref.at[aligned(piece * width, width), :]
        return remote(block, block, head_send.at[which, slot], head_recv.at[which, piece], (s, to))

    left, right, across = lax.rem(x + nx - 1, nx), lax.rem(x + 1, nx), lax.rem(x + 2, nx)
    mid = width // 2

    def half_piece(piece, half, slot, to):
        block = full.at[aligned(piece * width + half * mid, mid), :]
        return remote(block, block, head_send.at[HALF, slot], head_recv.at[HALF, slot], (s, to))

    def spread(which, ref):
        for j in (nx // 2, *[j for j in range(1, nx) if j != nx // 2]):
            push(which, ref, h, j, lax.rem(x + j, nx) * 2 + core).start()
        push(which, ref, h, 0, twin).start()

    def relay(which, ref):
        for j in range(1, nx):
            piece = lax.rem(x + nx - j, nx) * 2 + core
            push(which, ref, piece, nx + j, twin).wait_recv()
            push(which, ref, piece, nx + j, twin).start()

    def arrive(which, ref):
        for j in range(nx):
            piece = lax.rem(x + nx - j, nx) * 2 + 1 - core
            push(which, ref, piece, 0, twin).wait_recv()

    def sent(which, ref):
        for j in range(1, nx):
            push(which, ref, h, j, twin).wait_send()
            push(which, ref, h, nx + j, twin).wait_send()
        push(which, ref, h, 0, twin).wait_send()

    def twin_copy(k, j):
        to = lax.rem(x + j, nx)
        src = (part_out, branch_out)[k].at[aligned((to * 2 + 1 - core) * width, width), :]
        dst = twin_in.at[k, j]
        return remote(src, dst, head_send.at[TWIN + k, j], head_recv.at[TWIN + k, j], (s, twin))

    def sum_copy(k, slot):
        side, half = ((0, 0), (1, 1), (0, 1), (1, 0), (0, 0), (1, 1))[slot]
        if slot < 2:
            src, dst = half_out.at[k, side], half_in.at[k, side]
        else:
            rows_of = pl.ds(half * mid, mid)
            src, dst = pair_out.at[k, side, rows_of, :], pair_in.at[k, side, rows_of, :]
        to = (right, left)[side] * 2 + core
        return remote(src, dst, head_send.at[SUM + k, slot], head_recv.at[SUM + k, slot], (s, to))

    def pair_sum(k, j):
        twin_copy(k, j).wait_recv()
        ref = (part_out, branch_out)[k]
        own = ref[aligned((lax.rem(x + j, nx) * 2 + core) * width, width), :]
        return own.astype(F32) + twin_in[k, j].astype(F32)

    def sum_begin(k):
        for j in (2, 1, 3, 0):
            twin_copy(k, j).start()

    def sum_far(k):
        far_sum = pair_sum(k, 2).astype(BF16)
        half_out[k, 0] = far_sum[:mid]
        half_out[k, 1] = far_sum[mid:]
        sum_copy(k, 0).start()
        sum_copy(k, 1).start()
        to_right, to_left = pair_sum(k, 1), pair_sum(k, 3)
        pair_out[k, 0, mid:, :] = to_right[mid:].astype(BF16)
        sum_copy(k, 2).start()
        pair_out[k, 1, :mid, :] = to_left[:mid].astype(BF16)
        sum_copy(k, 3).start()
        near[k, 0] = to_right[:mid]
        near[k, 1] = to_left[mid:]

    def sum_near(k):
        sum_copy(k, 0).wait_recv()
        pair_out[k, 0, :mid, :] = (near[k, 0] + half_in[k, 0].astype(F32)).astype(BF16)
        sum_copy(k, 4).start()
        sum_copy(k, 1).wait_recv()
        pair_out[k, 1, mid:, :] = (near[k, 1] + half_in[k, 1].astype(F32)).astype(BF16)
        sum_copy(k, 5).start()

    def sum_end(k):
        own = pair_sum(k, 0)
        for slot in range(2, 6):
            sum_copy(k, slot).wait_recv()
        return own + pair_in[k, 0].astype(F32) + pair_in[k, 1].astype(F32)

    def sum_sent(k):
        for j in range(nx):
            twin_copy(k, j).wait_send()
        for slot in range(6):
            sum_copy(k, slot).wait_send()

    barrier = pltpu.get_barrier_semaphore()

    def greet_scan(j):
        pl.semaphore_signal(
            barrier, inc=1, device_id=(lax.rem(s + j, ns), h), device_id_type=MESH
        )

    def greet_head(j):
        pl.semaphore_signal(
            barrier, inc=1, device_id=(s, lax.rem(h + j, nh)), device_id_type=MESH
        )

    each(1, ns, greet_scan)
    each(1, nh, greet_head)
    fetches = [
        pltpu.make_async_copy(src, dst, local_sem.at[i])
        for i, (src, dst) in enumerate(
            [
                (cot_hbm, cot.at[mine, :]),
                (points_hbm, points_ref),
                (outw_hbm, outw_ref),
                (weight_hbm, weight_ref),
            ]
        )
    ]
    for fetch in fetches:
        fetch.start()
    owners = owner_ref[...]
    hot = lax.broadcasted_iota(jnp.int32, (ns, rows), 0) == owners
    ones = jnp.where(hot, 1.0, 0.0)
    total = jnp.sum(jnp.where(hot, 1, 0), axis=1, keepdims=True)
    tall[...] = jnp.broadcast_to(total, (ns, 128))
    pl.semaphore_wait(barrier, ns + nh - 2)

    each(1, ns, lambda j: scan_copy(TALLY, j).start())
    fetches[0].wait()
    spread(COT, cot)
    sizes_ref[pl.ds(s, 1), :] = tall[pl.ds(s, 1), :]
    before = jnp.where(
        lax.broadcasted_iota(jnp.int32, (128, 128), 0)
        < lax.broadcasted_iota(jnp.int32, (128, 128), 1),
        1.0,
        0.0,
    ).astype(BF16)
    carried = jnp.zeros((ns, 1), F32)
    for b in range(0, rows, 128):
        part = ones[:, b : b + 128]
        running = dot_nn(part.astype(BF16), before) + carried
        rank = jnp.sum(running * part, axis=0, keepdims=True)
        code_ref[:, b : b + 128] = owners[:, b : b + 128] * BUCKET + rank.astype(jnp.int32)
        carried = carried + jnp.sum(part, axis=1, keepdims=True)
    code = code_ref[...]

    def build(i):
        first = pl.multiple_of(i * 256, 256)
        hots[pl.ds(first, 256), :] = hot_block(code, first, 256)

    each(0, ns // 2, build, False)
    gain = jnp.transpose(jnp.broadcast_to(gain_ref[...], (8, channels)))[:, :1]
    gain_wide[...] = jnp.broadcast_to(gain, gain_wide.shape)
    each(1, ns, lambda j: scan_copy(TALLY, j).wait())

    earlier = jnp.where(
        lax.broadcasted_iota(jnp.int32, (ns, ns), 1) < lax.broadcasted_iota(jnp.int32, (ns, ns), 0),
        1.0,
        0.0,
    ).astype(BF16)
    begins = dot_nn(earlier, sizes_ref[...].astype(F32).astype(BF16)).astype(jnp.int32)
    tiles[...] = begins // 128
    offsets[...] = begins - begins // 128 * 128
    span = lax.broadcasted_iota(jnp.int32, (256, 128), 0) - lax.broadcasted_iota(
        jnp.int32, (256, 128), 1
    )
    groups = ns // 4

    def nth_group(i):
        half = (i + 1) // 2
        shift = groups // 2 + half * (lax.rem(i, 2) * 2 - 1)
        return lax.rem(s // 4 + shift + groups, groups)

    def send_group(which, group, last):
        for t in range(4):
            peer = group * 4 + t
            if last:

                @pl.when(peer != s)
                def _():
                    scan_copy(which, lax.rem(peer - s + ns, ns)).start()

            else:
                scan_copy(which, lax.rem(peer - s + ns, ns)).start()

    def cut_and_send(i, last):
        group = nth_group(i)
        places = [
            jnp.broadcast_to(tiles[pl.ds(group * 4 + t, 1), :], (16, 128)).astype(F32).astype(BF16)
            for t in range(4)
        ]
        zero = jnp.zeros((width // 16, 16, 128), BF16)

        held = [zero] * 8
        for n in range(ns + 1):
            tile = points_ref[:, 128 * n : 128 * (n + 1)].reshape(zero.shape)
            for t in range(4):
                if n < ns:
                    held[t] = jnp.where((places[t] == n)[None], tile, held[t])
                if n > 0:
                    held[4 + t] = jnp.where((places[t] == n - 1)[None], tile, held[4 + t])
        low, high = held[:4], held[4:]
        for t in range(4):
            peer = group * 4 + t
            window = jnp.concatenate(
                [low[t].reshape(width, 128), high[t].reshape(width, 128)], axis=1
            )
            pick = jnp.where(span == offsets[pl.ds(peer, 1), :], 1.0, 0.0).astype(BF16)
            windows[peer] = dot_nn(window, pick).astype(BF16)
        send_group(POINTS, group, last)

    for fetch in fetches[1:]:
        fetch.wait()
    each(0, groups - 1, lambda i: cut_and_send(i, False), False)
    cut_and_send(groups - 1, True)
    arrived[pl.ds(s, 1)] = windows[pl.ds(s, 1)]
    relay(COT, cot)

    gathered = jnp.zeros((width, rows), F32)
    for i in range(groups):
        group = nth_group(i)
        for t in range(4):
            source = group * 4 + t

            def landed(source=source):
                scan_copy(POINTS, lax.rem(s - source + ns, ns)).wait_recv()

            if i < groups - 1:
                landed()
            else:
                pl.when(source != s)(landed)
        pieces = jnp.concatenate([arrived[group * 4 + t] for t in range(4)], axis=1)
        gathered = gathered + dot_nn(pieces, hots[aligned(group * 512, 512), :])
    full[mine, :] = gathered.astype(BF16)
    push(FULL, full, h, 1, right * 2 + core).start()
    push(FULL, full, h, 3, left * 2 + core).start()
    push(FULL, full, h, 0, twin).start()
    arrive(COT, cot)
    gradc[...] = dot_nn(outw_ref[...], cot[...])
    for at, side, half, to in ((left, 1, 0, right), (right, 3, 1, left)):
        piece = at * 2 + core
        push(FULL, full, piece, nx + side, twin).wait_recv()
        half_piece(piece, half, half, to * 2 + core).start()
        push(FULL, full, piece, nx + side, twin).start()
    for half in range(2):
        half_piece(across * 2 + core, half, half, twin).wait_recv()
        half_piece(across * 2 + core, half, 2 + half, twin).start()
    for at in (x, left, right):
        push(FULL, full, at * 2 + 1 - core, 0, twin).wait_recv()
    for half in range(2):
        half_piece(across * 2 + 1 - core, half, 2 + half, twin).wait_recv()

    floats = full[...].astype(F32)
    mean = jnp.sum(floats, axis=0, keepdims=True) * (1.0 / channels)
    centered = floats - mean
    inv = lax.rsqrt(jnp.sum(centered * centered, axis=0, keepdims=True) * (1.0 / channels) + EPS)
    normed[...] = centered * inv
    scaled[...] = (normed[...] * gain_wide[:, :1]).astype(BF16)
    for i, ref in enumerate((query, keys, value)):
        ref[...] = dot_nn(weight_ref[i], scaled[...])

    def forward(head):
        at = aligned(head * HD, HD)
        q, k, v = query[at, :], keys[at, :], value[at, :]
        key_t[...] = jnp.transpose(jnp.concatenate(left_stack(k), axis=0))
        v_rows = jnp.concatenate(list(split2(v)) + [jnp.ones((HD, rows), BF16)], axis=0)
        for b in range(0, rows, SPAN):
            q_stack = jnp.concatenate(
                right_stack(q[:, b : b + SPAN] * (HD**-0.5 * LOG2E)), axis=0
            )
            scores = dot_nn(key_t[...], q_stack)
            peak = jnp.max(scores, axis=0, keepdims=True)
            weights = jnp.exp2(scores - peak).astype(BF16)
            weights_all[head, :, b : b + SPAN] = weights
            sums = dot_nn(v_rows, weights)
            share = 1.0 / sums[2 * HD : 2 * HD + 1]
            shares[head, :, b : b + SPAN] = share
            ctx = (sums[:HD] + sums[HD : 2 * HD]) * share
            context[at, b : b + SPAN] = ctx

    for head in range(width // HD):
        forward(head)
    context_b = context[...].astype(BF16)
    branch_out[...] = dot_tn(outw_ref[...], context_b).astype(BF16)
    sum_begin(1)

    def backward(head):
        at = aligned(head * HD, HD)
        q, k, v = query[at, :], keys[at, :], value[at, :]
        row = lax.broadcasted_iota(jnp.int32, (HD, rows), 0)
        ones = jnp.ones((HD, rows), BF16)
        value_t[...] = jnp.transpose(jnp.concatenate(left_stack(v) + [ones], axis=0))
        k_rows = jnp.concatenate(list(split2(k)), axis=0)
        gs = gradc[at, :] * shares[head]
        center = jnp.sum(gs * context[at, :], axis=0, keepdims=True) * (-(HD**-0.5))
        parts = [t.astype(F32) for t in split3(center)]
        tail = jnp.where(
            row == 0, parts[0], jnp.where(row == 1, parts[1], jnp.where(row == 2, parts[2], 0.0))
        ).astype(BF16)
        g_stack = jnp.concatenate(right_stack(gs * HD**-0.5) + [tail], axis=0)
        g_rows = jnp.concatenate(list(split2(gs)), axis=0)
        q_rows = jnp.concatenate(list(split2(q)), axis=0)
        key_grad = jnp.zeros((HD * 2, rows), F32)
        value_grad = jnp.zeros((HD * 2, rows), F32)
        for b in range(0, rows, SPAN):
            weights = weights_all[head, :, b : b + SPAN]
            delta = dot_nn(value_t[...], g_stack[:, b : b + SPAN])
            score_grad = (weights.astype(F32) * delta).astype(BF16)
            value_grad = value_grad + dot_nt(g_rows[:, b : b + SPAN], weights)
            dq = dot_nn(k_rows, score_grad)
            grads[at, b : b + SPAN] = (dq[:HD] + dq[HD:]).astype(BF16)
            key_grad = key_grad + dot_nt(q_rows[:, b : b + SPAN], score_grad)
        k_at = aligned(width + head * HD, HD)
        v_at = aligned(2 * width + head * HD, HD)
        grads[k_at, :] = (key_grad[:HD] + key_grad[HD:]).astype(BF16)
        grads[v_at, :] = (value_grad[:HD] + value_grad[HD:]).astype(BF16)

    for head in range(width // HD):
        backward(head)
        if head == 0:
            sum_far(1)
        elif head == 1:
            sum_near(1)

    whole = jnp.concatenate([weight_ref[i] for i in range(3)], axis=0)
    part_out[...] = dot_tn(whole, grads[...]).astype(BF16)

    sum_begin(0)
    wgrad_out[:, : 3 * width] = dot_nt(scaled[...], grads[...]).astype(BF16)
    wgrad_out[:, 3 * width :] = dot_nt(cot[...], context_b).astype(BF16)
    each(1, ns, lambda j: scan_copy(WGRAD, j).start())
    sum_far(0)
    weighted = part_out[...].astype(F32) * gain_wide[:, :1]
    stats_out[0:1, :] = jnp.sum(weighted, axis=0, keepdims=True)
    stats_out[1:2, :] = jnp.sum(weighted * normed[...], axis=0, keepdims=True)
    each(1, nh, lambda j: stats_copy(j).start())

    sum_near(0)
    wgrad_in[pl.ds(s, 1)] = wgrad_out[aligned(s * strip, strip), :][None]
    branch = sum_end(1)
    mixed_ref[...] = (full[mine, :].astype(F32) + branch).astype(BF16)
    each(1, nh, lambda j: stats_copy(j).wait())
    stats = stats_out[...]
    for i in range(1, nh):
        stats = stats + stats_in[lax.rem(h + i, nh)]
    normed_grad = sum_end(0)
    normed_own = normed[mine, :]
    first, second = stats[0:1] * (1.0 / channels), stats[1:2] * (1.0 / channels)
    grad = inv * (normed_grad * gain_wide[mine, :1] - first - normed_own * second)
    points_grad = (cot[mine, :].astype(F32) + grad).astype(BF16)

    for i in range(groups):
        group = nth_group(i)
        block = dot_nt(points_grad, hots[aligned(group * 512, 512), :]).astype(BF16)
        for t in range(4):
            buckets[group * 4 + t] = block[:, 128 * t : 128 * (t + 1)]
        send_group(BACK, group, i == groups - 1)

    back_ref[pl.ds(s, 1)] = buckets[pl.ds(s, 1)]
    product = normed_grad * normed_own
    folded = product[:, :128]
    for b in range(128, rows, 128):
        folded = folded + product[:, b : b + 128]
    gain_out[...] = jnp.zeros_like(gain_out)
    gain_out[:, :width] = jnp.sum(jnp.transpose(folded), axis=0, keepdims=True)
    each(1, ns, lambda j: scan_copy(GAIN, j).start())
    gain_in[pl.ds(s, 1)] = gain_out[...][None]
    each(1, ns, lambda j: scan_copy(WGRAD, j).wait())
    wsum_ref[...] = jnp.sum(wgrad_in[...].astype(F32), axis=0)
    each(1, ns, lambda j: scan_copy(GAIN, j).wait())
    gsum_ref[...] = jnp.sum(gain_in[...], axis=0)
    sent(COT, cot)
    for slot in (0, 1, 3, nx + 1, nx + 3):
        push(FULL, full, h, slot, twin).wait_send()
    for slot in range(4):
        half_piece(h, 0, slot, twin).wait_send()
    sum_sent(0)
    sum_sent(1)
    each(1, ns, lambda j: scan_copy(POINTS, j).wait_send())
    each(1, ns, lambda j: scan_copy(BACK, j).wait())


def slots_kernel(
    ns, sizes_ref, back_ref, mixed_in, wsum_ref, gsum_ref,
    mixed_ref, owned_ref, qkv_ref, out_ref, gain_ref, slots,
):
    width = back_ref.shape[1]
    slots[...] = jnp.zeros_like(slots)
    lane = lax.broadcasted_iota(jnp.int32, (width, 128), 1)

    def one(d, begin):
        size = sizes_ref[d, 0]
        tile = begin // 128
        off = begin - tile * 128
        block = jnp.where(lane < size, back_ref[d].astype(F32), 0.0)
        wide = jnp.concatenate([block, jnp.zeros_like(block)], axis=1)
        at = pl.ds(pl.multiple_of(tile * 128, 128), 256)
        slots[:, at] = slots[:, at] + pltpu.roll(wide, off, 1)
        return begin + size

    lax.fori_loop(0, ns, one, jnp.int32(0), unroll=8)
    owned_ref[...] = slots[...].astype(BF16)
    mixed_ref[...] = mixed_in[...]
    for i in range(3):
        qkv_ref[i] = wsum_ref[:, i * width : (i + 1) * width]
    out_ref[...] = wsum_ref[:, 3 * width :]
    gain_ref[...] = gsum_ref[:, :width]


def per_device(owner_ids, owned_points, norm_gain, qkv_weight, out_weight, cotangent):
    ns, nh = lax.axis_size("scan"), lax.axis_size("head")
    nx = nh // 2
    rows = owner_ids.shape[0]
    width, slot_count = owned_points.shape
    channels = width * nh
    strip = channels // ns
    shape = jax.ShapeDtypeStruct
    dma = pltpu.SemaphoreType.DMA
    vmem = pltpu.VMEM
    sizes, mixed, back, wsum, gsum = pl.pallas_call(
        functools.partial(main_kernel, ns, nh),
        out_shape=(
            shape((ns, 128), jnp.int32),
            shape((width, rows), BF16),
            shape((ns, width, BUCKET), BF16),
            shape((strip, 4 * width), F32),
            shape((1, 128), F32),
        ),
        in_specs=[VMEM, ANY, ANY, VMEM, ANY, ANY],
        out_specs=(VMEM,) * 5,
        scratch_shapes=[
            vmem((ns, 128), jnp.int32),
            vmem((ns, 128), jnp.int32),
            vmem((ns, 128), jnp.int32),
            vmem((ns, width, BUCKET), BF16),
            vmem((ns, width, BUCKET), BF16),
            vmem((ns * BUCKET, rows), BF16),
            vmem((channels, rows), BF16),
            vmem((channels, rows), BF16),
            vmem((1, rows), jnp.int32),
            vmem((channels, 128), F32),
            vmem((channels, rows), F32),
            vmem((channels, rows), BF16),
            vmem((width, rows), F32),
            vmem((width, rows), F32),
            vmem((width, rows), F32),
            vmem((width, rows), F32),
            vmem((width, rows), F32),
            vmem((3 * width, rows), BF16),
            vmem((width // HD, rows, rows), BF16),
            vmem((width // HD, 1, rows), F32),
            vmem((rows, 6 * HD), BF16),
            vmem((rows, 7 * HD), BF16),
            vmem((channels, rows), BF16),
            vmem((2, 2, width // 2, rows), F32),
            vmem((channels, rows), BF16),
            vmem((2, nx, width, rows), BF16),
            vmem((2, 2, width // 2, rows), BF16),
            vmem((2, 2, width // 2, rows), BF16),
            vmem((2, 2, width, rows), BF16),
            vmem((2, 2, width, rows), BF16),
            vmem((2, rows), F32),
            vmem((nh, 2, rows), F32),
            vmem((channels, 4 * width), BF16),
            vmem((ns, strip, 4 * width), BF16),
            vmem((1, 128), F32),
            vmem((ns, 1, 128), F32),
            vmem((ns, width, BUCKET), BF16),
            vmem((width, slot_count), BF16),
            vmem((3, width, channels), BF16),
            vmem((width, channels), BF16),
            dma((4,)),
            dma((5, ns)),
            dma((5, ns)),
            dma((8, nh)),
            dma((8, nh)),
        ],
        compiler_params=pltpu.CompilerParams(
            collective_id=1, has_side_effects=True, vmem_limit_bytes=LIMIT
        ),
        name="patch_block",
    )(owner_ids.reshape(1, rows), owned_points, cotangent, norm_gain.reshape(1, channels), qkv_weight, out_weight)
    mixed_rows, grad_owned, qkv_grad, out_grad, gain_grad = pl.pallas_call(
        functools.partial(slots_kernel, ns),
        out_shape=(
            shape((width, rows), BF16),
            shape((width, slot_count), BF16),
            shape((3, strip, width), F32),
            shape((strip, width), F32),
            shape((1, width), F32),
        ),
        in_specs=[SMEM] + [VMEM] * 4,
        out_specs=(VMEM,) * 5,
        scratch_shapes=[vmem((width, slot_count), F32)],
        compiler_params=pltpu.CompilerParams(vmem_limit_bytes=LIMIT),
        name="slots",
    )(sizes, back, mixed, wsum, gsum)
    return (
        mixed_rows,
        grad_owned,
        qkv_grad.transpose(0, 2, 1),
        out_grad.T,
        gain_grad.reshape(width),
    )


def solution(mesh):
    in_specs = (
        P("scan", None),
        P("head", "scan"),
        P(),
        P(None, "head", None),
        P("head", None),
        P("head", "scan"),
    )
    out_specs = (
        P("head", "scan"),
        P("head", "scan"),
        P(None, "head", "scan"),
        P("head", "scan"),
        P("head"),
    )
    return jax.shard_map(
        per_device, mesh=mesh, in_specs=in_specs, out_specs=out_specs, check_vma=False
    )
```

```python
import functools

import jax
import jax.numpy as jnp
from jax import lax
from jax.experimental import pallas as pl
from jax.experimental.pallas import tpu as pltpu
from jax.sharding import PartitionSpec as P

HD = 16
BUCKET = 128
EPS = 1e-05
SPAN = 1024
LOG2E = 1.4426950408889634
MESH = pl.DeviceIdType.MESH
F32 = jnp.float32
BF16 = jnp.bfloat16
VMEM = pl.BlockSpec(memory_space=pltpu.VMEM)
ANY = pl.BlockSpec(memory_space=pl.ANY)
SMEM = pl.BlockSpec(memory_space=pltpu.SMEM)
LIMIT = 56 * 1024 * 1024


def dot_nn(a, b):
    return lax.dot_general(a, b, (((1,), (0,)), ((), ())), preferred_element_type=F32)


def dot_nt(a, b):
    return lax.dot_general(a, b, (((1,), (1,)), ((), ())), preferred_element_type=F32)


def dot_tn(a, b):
    return lax.dot_general(a, b, (((0,), (0,)), ((), ())), preferred_element_type=F32)


def split2(x):
    high = x.astype(BF16)
    return high, (x - high.astype(F32)).astype(BF16)


def split3(x):
    high = x.astype(BF16)
    rest = x - high.astype(F32)
    middle = rest.astype(BF16)
    return high, middle, (rest - middle.astype(F32)).astype(BF16)


def left_stack(x):
    a, b, c = split3(x)
    return [a, b, a, b, c, a]


def right_stack(x):
    a, b, c = split3(x)
    return [a, a, b, b, a, c]


def hot_block(code, first, height):
    ids = lax.broadcasted_iota(jnp.int32, (height, code.shape[1]), 0) + first
    return jnp.where(ids == code, 1.0, 0.0).astype(BF16)


def aligned(first, size):
    return pl.ds(pl.multiple_of(first, size), size)


def each(first, last, act, unroll=True):
    def body(j, carry):
        act(j)
        return carry

    lax.fori_loop(first, last, body, 0, unroll=unroll)


TALLY, POINTS, WGRAD, BACK, GAIN = range(5)
COT, FULL, STATS, HALF, TWIN, _, SUM, _ = range(8)


def main_kernel(
    ns, nh, owner_ref, points_hbm, cot_hbm, gain_ref, weight_hbm, outw_hbm,
    sizes_ref, mixed_ref, back_ref, wsum_ref, gsum_ref,
    tall, tiles, offsets, windows, arrived, hots, full, cot, code_ref, gain_wide,
    normed, scaled, query, keys, value, gradc, context, grads, weights_all, shares,
    key_t, value_t, branch_out, near, part_out, twin_in, half_out, half_in, pair_out, pair_in, stats_out, stats_in,
    wgrad_out, wgrad_in, gain_out, gain_in, buckets, points_ref, weight_ref, outw_ref,
    local_sem, scan_send, scan_recv, head_send, head_recv,
):
    s, h = lax.axis_index("scan"), lax.axis_index("head")
    nx = nh // 2
    x, core = h // 2, lax.rem(h, 2)
    twin = x * 2 + 1 - core
    width, rows = cot_hbm.shape
    channels = width * nh
    strip = channels // ns
    mine = aligned(h * width, width)

    def remote(src, dst, send, recv, to):
        return pltpu.make_async_remote_copy(
            src_ref=src, dst_ref=dst, send_sem=send, recv_sem=recv, device_id=to, device_id_type=MESH
        )

    def scan_copy(which, j):
        peer = lax.rem(s + j, ns)
        if which == TALLY:
            src, dst = tall.at[pl.ds(peer, 1), :], sizes_ref.at[pl.ds(s, 1), :]
        elif which == POINTS:
            src, dst = windows.at[peer], arrived.at[s]
        elif which == WGRAD:
            src, dst = wgrad_out.at[aligned(peer * strip, strip), :], wgrad_in.at[s]
        elif which == BACK:
            src, dst = buckets.at[peer], back_ref.at[s]
        else:
            src, dst = gain_out, gain_in.at[s]
        return remote(src, dst, scan_send.at[which, j], scan_recv.at[which, j], (peer, h))

    def stats_copy(j):
        peer = lax.rem(h + j, nh)
        return remote(
            stats_out, stats_in.at[h], head_send.at[STATS, j], head_recv.at[STATS, j], (s, peer)
        )

    def push(which, ref, piece, slot, to):
        block = ref.at[aligned(piece * width, width), :]
        return remote(block, block, head_send.at[which, slot], head_recv.at[which, piece], (s, to))

    left, right, across = lax.rem(x + nx - 1, nx), lax.rem(x + 1, nx), lax.rem(x + 2, nx)
    mid = width // 2

    def half_piece(piece, half, slot, to):
        block = full.at[aligned(piece * width + half * mid, mid), :]
        return remote(block, block, head_send.at[HALF, slot], head_recv.at[HALF, slot], (s, to))

    def spread(which, ref):
        for j in (nx // 2, *[j for j in range(1, nx) if j != nx // 2]):
            push(which, ref, h, j, lax.rem(x + j, nx) * 2 + core).start()
        push(which, ref, h, 0, twin).start()

    def relay(which, ref):
        for j in range(1, nx):
            piece = lax.rem(x + nx - j, nx) * 2 + core
            push(which, ref, piece, nx + j, twin).wait_recv()
            push(which, ref, piece, nx + j, twin).start()

    def arrive(which, ref):
        for j in range(nx):
            piece = lax.rem(x + nx - j, nx) * 2 + 1 - core
            push(which, ref, piece, 0, twin).wait_recv()

    def sent(which, ref):
        for j in range(1, nx):
            push(which, ref, h, j, twin).wait_send()
            push(which, ref, h, nx + j, twin).wait_send()
        push(which, ref, h, 0, twin).wait_send()

    def twin_copy(k, j):
        to = lax.rem(x + j, nx)
        src = (part_out, branch_out)[k].at[aligned((to * 2 + 1 - core) * width, width), :]
        dst = twin_in.at[k, j]
        return remote(src, dst, head_send.at[TWIN + k, j], head_recv.at[TWIN + k, j], (s, twin))

    def sum_copy(k, slot):
        side, half = ((0, 0), (1, 1), (0, 1), (1, 0), (0, 0), (1, 1))[slot]
        if slot < 2:
            src, dst = half_out.at[k, side], half_in.at[k, side]
        else:
            rows_of = pl.ds(half * mid, mid)
            src, dst = pair_out.at[k, side, rows_of, :], pair_in.at[k, side, rows_of, :]
        to = (right, left)[side] * 2 + core
        return remote(src, dst, head_send.at[SUM + k, slot], head_recv.at[SUM + k, slot], (s, to))

    def pair_sum(k, j):
        twin_copy(k, j).wait_recv()
        ref = (part_out, branch_out)[k]
        own = ref[aligned((lax.rem(x + j, nx) * 2 + core) * width, width), :]
        return own.astype(F32) + twin_in[k, j].astype(F32)

    def sum_begin(k):
        for j in (2, 1, 3, 0):
            twin_copy(k, j).start()

    def sum_far(k):
        far_sum = pair_sum(k, 2).astype(BF16)
        half_out[k, 0] = far_sum[:mid]
        half_out[k, 1] = far_sum[mid:]
        sum_copy(k, 0).start()
        sum_copy(k, 1).start()
        to_right, to_left = pair_sum(k, 1), pair_sum(k, 3)
        pair_out[k, 0, mid:, :] = to_right[mid:].astype(BF16)
        sum_copy(k, 2).start()
        pair_out[k, 1, :mid, :] = to_left[:mid].astype(BF16)
        sum_copy(k, 3).start()
        near[k, 0] = to_right[:mid]
        near[k, 1] = to_left[mid:]

    def sum_near(k):
        sum_copy(k, 0).wait_recv()
        pair_out[k, 0, :mid, :] = (near[k, 0] + half_in[k, 0].astype(F32)).astype(BF16)
        sum_copy(k, 4).start()
        sum_copy(k, 1).wait_recv()
        pair_out[k, 1, mid:, :] = (near[k, 1] + half_in[k, 1].astype(F32)).astype(BF16)
        sum_copy(k, 5).start()

    def sum_end(k):
        own = pair_sum(k, 0)
        for slot in range(2, 6):
            sum_copy(k, slot).wait_recv()
        return own + pair_in[k, 0].astype(F32) + pair_in[k, 1].astype(F32)

    def sum_sent(k):
        for j in range(nx):
            twin_copy(k, j).wait_send()
        for slot in range(6):
            sum_copy(k, slot).wait_send()

    barrier = pltpu.get_barrier_semaphore()

    def greet_scan(j):
        pl.semaphore_signal(
            barrier, inc=1, device_id=(lax.rem(s + j, ns), h), device_id_type=MESH
        )

    def greet_head(j):
        pl.semaphore_signal(
            barrier, inc=1, device_id=(s, lax.rem(h + j, nh)), device_id_type=MESH
        )

    each(1, ns, greet_scan)
    each(1, nh, greet_head)
    fetches = [
        pltpu.make_async_copy(src, dst, local_sem.at[i])
        for i, (src, dst) in enumerate(
            [
                (cot_hbm, cot.at[mine, :]),
                (points_hbm, points_ref),
                (outw_hbm, outw_ref),
                (weight_hbm, weight_ref),
            ]
        )
    ]
    for fetch in fetches:
        fetch.start()
    owners = owner_ref[...]
    hot = lax.broadcasted_iota(jnp.int32, (ns, rows), 0) == owners
    ones = jnp.where(hot, 1.0, 0.0)
    total = jnp.sum(jnp.where(hot, 1, 0), axis=1, keepdims=True)
    tall[...] = jnp.broadcast_to(total, (ns, 128))
    pl.semaphore_wait(barrier, ns + nh - 2)

    each(1, ns, lambda j: scan_copy(TALLY, j).start())
    fetches[0].wait()
    spread(COT, cot)
    sizes_ref[pl.ds(s, 1), :] = tall[pl.ds(s, 1), :]
    before = jnp.where(
        lax.broadcasted_iota(jnp.int32, (128, 128), 0)
        < lax.broadcasted_iota(jnp.int32, (128, 128), 1),
        1.0,
        0.0,
    ).astype(BF16)
    carried = jnp.zeros((ns, 1), F32)
    for b in range(0, rows, 128):
        part = ones[:, b : b + 128]
        running = dot_nn(part.astype(BF16), before) + carried
        rank = jnp.sum(running * part, axis=0, keepdims=True)
        code_ref[:, b : b + 128] = owners[:, b : b + 128] * BUCKET + rank.astype(jnp.int32)
        carried = carried + jnp.sum(part, axis=1, keepdims=True)
    code = code_ref[...]

    def build(i):
        first = pl.multiple_of(i * 256, 256)
        hots[pl.ds(first, 256), :] = hot_block(code, first, 256)

    each(0, ns // 2, build, False)
    gain = jnp.transpose(jnp.broadcast_to(gain_ref[...], (8, channels)))[:, :1]
    gain_wide[...] = jnp.broadcast_to(gain, gain_wide.shape)
    each(1, ns, lambda j: scan_copy(TALLY, j).wait())

    earlier = jnp.where(
        lax.broadcasted_iota(jnp.int32, (ns, ns), 1) < lax.broadcasted_iota(jnp.int32, (ns, ns), 0),
        1.0,
        0.0,
    ).astype(BF16)
    begins = dot_nn(earlier, sizes_ref[...].astype(F32).astype(BF16)).astype(jnp.int32)
    tiles[...] = begins // 128
    offsets[...] = begins - begins // 128 * 128
    span = lax.broadcasted_iota(jnp.int32, (256, 128), 0) - lax.broadcasted_iota(
        jnp.int32, (256, 128), 1
    )
    groups = ns // 4

    def nth_group(i):
        half = (i + 1) // 2
        shift = groups // 2 + half * (lax.rem(i, 2) * 2 - 1)
        return lax.rem(s // 4 + shift + groups, groups)

    def send_group(which, group, last):
        for t in range(4):
            peer = group * 4 + t
            if last:

                @pl.when(peer != s)
                def _():
                    scan_copy(which, lax.rem(peer - s + ns, ns)).start()

            else:
                scan_copy(which, lax.rem(peer - s + ns, ns)).start()

    def cut(group):
        high_of = group * 4 + 4
        places = [
            jnp.broadcast_to(tiles[group * 4 + t : group * 4 + t + 1, :], (16, 128)).astype(F32).astype(BF16)
            for t in range(4)
        ]
        zero = jnp.zeros((width // 16, 16, 128), BF16)

        held = [zero] * 8
        for n in range(high_of + 1):
            tile = points_ref[:, 128 * n : 128 * (n + 1)].reshape(zero.shape)
            for t in range(4):
                if n < high_of:
                    held[t] = jnp.where((places[t] == n)[None], tile, held[t])
                if n > 0:
                    held[4 + t] = jnp.where((places[t] == n - 1)[None], tile, held[4 + t])
        low, high = held[:4], held[4:]
        for t in range(4):
            peer = group * 4 + t
            window = jnp.concatenate(
                [low[t].reshape(width, 128), high[t].reshape(width, 128)], axis=1
            )
            pick = jnp.where(span == offsets[peer : peer + 1, :], 1.0, 0.0).astype(BF16)
            windows[peer] = dot_nn(window, pick).astype(BF16)

    def cut_and_send(i, last):
        group = nth_group(i)
        lax.switch(group, [functools.partial(cut, n) for n in range(groups)])
        send_group(POINTS, group, last)

    for fetch in fetches[1:]:
        fetch.wait()
    each(0, groups - 1, lambda i: cut_and_send(i, False), False)
    cut_and_send(groups - 1, True)
    arrived[pl.ds(s, 1)] = windows[pl.ds(s, 1)]
    relay(COT, cot)

    gathered = jnp.zeros((width, rows), F32)
    for i in range(groups):
        group = nth_group(i)
        for t in range(4):
            source = group * 4 + t

            def landed(source=source):
                scan_copy(POINTS, lax.rem(s - source + ns, ns)).wait_recv()

            if i < groups - 1:
                landed()
            else:
                pl.when(source != s)(landed)
        pieces = jnp.concatenate([arrived[group * 4 + t] for t in range(4)], axis=1)
        gathered = gathered + dot_nn(pieces, hots[aligned(group * 512, 512), :])
    full[mine, :] = gathered.astype(BF16)
    push(FULL, full, h, 1, right * 2 + core).start()
    push(FULL, full, h, 3, left * 2 + core).start()
    push(FULL, full, h, 0, twin).start()
    arrive(COT, cot)
    gradc[...] = dot_nn(outw_ref[...], cot[...])
    for at, side, half, to in ((left, 1, 0, right), (right, 3, 1, left)):
        piece = at * 2 + core
        push(FULL, full, piece, nx + side, twin).wait_recv()
        half_piece(piece, half, half, to * 2 + core).start()
        push(FULL, full, piece, nx + side, twin).start()
    for half in range(2):
        half_piece(across * 2 + core, half, half, twin).wait_recv()
        half_piece(across * 2 + core, half, 2 + half, twin).start()
    for at in (x, left, right):
        push(FULL, full, at * 2 + 1 - core, 0, twin).wait_recv()
    for half in range(2):
        half_piece(across * 2 + 1 - core, half, 2 + half, twin).wait_recv()

    floats = full[...].astype(F32)
    mean = jnp.sum(floats, axis=0, keepdims=True) * (1.0 / channels)
    centered = floats - mean
    inv = lax.rsqrt(jnp.sum(centered * centered, axis=0, keepdims=True) * (1.0 / channels) + EPS)
    normed[...] = centered * inv
    scaled[...] = (normed[...] * gain_wide[:, :1]).astype(BF16)
    for i, ref in enumerate((query, keys, value)):
        ref[...] = dot_nn(weight_ref[i], scaled[...])

    def forward(head):
        at = aligned(head * HD, HD)
        q, k, v = query[at, :], keys[at, :], value[at, :]
        key_t[...] = jnp.transpose(jnp.concatenate(left_stack(k), axis=0))
        v_rows = jnp.concatenate(list(split2(v)) + [jnp.ones((HD, rows), BF16)], axis=0)
        for b in range(0, rows, SPAN):
            q_stack = jnp.concatenate(
                right_stack(q[:, b : b + SPAN] * (HD**-0.5 * LOG2E)), axis=0
            )
            scores = dot_nn(key_t[...], q_stack)
            peak = jnp.max(scores, axis=0, keepdims=True)
            weights = jnp.exp2(scores - peak).astype(BF16)
            weights_all[head, :, b : b + SPAN] = weights
            sums = dot_nn(v_rows, weights)
            share = 1.0 / sums[2 * HD : 2 * HD + 1]
            shares[head, :, b : b + SPAN] = share
            ctx = (sums[:HD] + sums[HD : 2 * HD]) * share
            context[at, b : b + SPAN] = ctx

    for head in range(width // HD):
        forward(head)
    context_b = context[...].astype(BF16)
    branch_out[...] = dot_tn(outw_ref[...], context_b).astype(BF16)
    sum_begin(1)

    def backward(head):
        at = aligned(head * HD, HD)
        q, k, v = query[at, :], keys[at, :], value[at, :]
        row = lax.broadcasted_iota(jnp.int32, (HD, rows), 0)
        ones = jnp.ones((HD, rows), BF16)
        value_t[...] = jnp.transpose(jnp.concatenate(left_stack(v) + [ones], axis=0))
        k_rows = jnp.concatenate(list(split2(k)), axis=0)
        gs = gradc[at, :] * shares[head]
        center = jnp.sum(gs * context[at, :], axis=0, keepdims=True) * (-(HD**-0.5))
        parts = [t.astype(F32) for t in split3(center)]
        tail = jnp.where(
            row == 0, parts[0], jnp.where(row == 1, parts[1], jnp.where(row == 2, parts[2], 0.0))
        ).astype(BF16)
        g_stack = jnp.concatenate(right_stack(gs * HD**-0.5) + [tail], axis=0)
        g_rows = jnp.concatenate(list(split2(gs)), axis=0)
        q_rows = jnp.concatenate(list(split2(q)), axis=0)
        key_grad = jnp.zeros((HD * 2, rows), F32)
        value_grad = jnp.zeros((HD * 2, rows), F32)
        for b in range(0, rows, SPAN):
            weights = weights_all[head, :, b : b + SPAN]
            delta = dot_nn(value_t[...], g_stack[:, b : b + SPAN])
            score_grad = (weights.astype(F32) * delta).astype(BF16)
            value_grad = value_grad + dot_nt(g_rows[:, b : b + SPAN], weights)
            dq = dot_nn(k_rows, score_grad)
            grads[at, b : b + SPAN] = (dq[:HD] + dq[HD:]).astype(BF16)
            key_grad = key_grad + dot_nt(q_rows[:, b : b + SPAN], score_grad)
        k_at = aligned(width + head * HD, HD)
        v_at = aligned(2 * width + head * HD, HD)
        grads[k_at, :] = (key_grad[:HD] + key_grad[HD:]).astype(BF16)
        grads[v_at, :] = (value_grad[:HD] + value_grad[HD:]).astype(BF16)

    for head in range(width // HD):
        backward(head)
        if head == 0:
            sum_far(1)
        elif head == 1:
            sum_near(1)

    whole = jnp.concatenate([weight_ref[i] for i in range(3)], axis=0)
    part_out[...] = dot_tn(whole, grads[...]).astype(BF16)

    sum_begin(0)
    wgrad_out[:, : 3 * width] = dot_nt(scaled[...], grads[...]).astype(BF16)
    wgrad_out[:, 3 * width :] = dot_nt(cot[...], context_b).astype(BF16)
    each(1, ns, lambda j: scan_copy(WGRAD, j).start())
    sum_far(0)
    weighted = part_out[...].astype(F32) * gain_wide[:, :1]
    stats_out[0:1, :] = jnp.sum(weighted, axis=0, keepdims=True)
    stats_out[1:2, :] = jnp.sum(weighted * normed[...], axis=0, keepdims=True)
    each(1, nh, lambda j: stats_copy(j).start())

    sum_near(0)
    wgrad_in[pl.ds(s, 1)] = wgrad_out[aligned(s * strip, strip), :][None]
    branch = sum_end(1)
    mixed_ref[...] = (full[mine, :].astype(F32) + branch).astype(BF16)
    each(1, nh, lambda j: stats_copy(j).wait())
    stats = stats_out[...]
    for i in range(1, nh):
        stats = stats + stats_in[lax.rem(h + i, nh)]
    normed_grad = sum_end(0)
    normed_own = normed[mine, :]
    first, second = stats[0:1] * (1.0 / channels), stats[1:2] * (1.0 / channels)
    grad = inv * (normed_grad * gain_wide[mine, :1] - first - normed_own * second)
    points_grad = (cot[mine, :].astype(F32) + grad).astype(BF16)

    for i in range(groups):
        group = nth_group(i)
        block = dot_nt(points_grad, hots[aligned(group * 512, 512), :]).astype(BF16)
        for t in range(4):
            buckets[group * 4 + t] = block[:, 128 * t : 128 * (t + 1)]
        send_group(BACK, group, i == groups - 1)

    back_ref[pl.ds(s, 1)] = buckets[pl.ds(s, 1)]
    product = normed_grad * normed_own
    folded = product[:, :128]
    for b in range(128, rows, 128):
        folded = folded + product[:, b : b + 128]
    gain_out[...] = jnp.zeros_like(gain_out)
    gain_out[:, :width] = jnp.sum(jnp.transpose(folded), axis=0, keepdims=True)
    each(1, ns, lambda j: scan_copy(GAIN, j).start())
    gain_in[pl.ds(s, 1)] = gain_out[...][None]
    each(1, ns, lambda j: scan_copy(WGRAD, j).wait())
    wsum_ref[...] = jnp.sum(wgrad_in[...].astype(F32), axis=0)
    each(1, ns, lambda j: scan_copy(GAIN, j).wait())
    gsum_ref[...] = jnp.sum(gain_in[...], axis=0)
    sent(COT, cot)
    for slot in (0, 1, 3, nx + 1, nx + 3):
        push(FULL, full, h, slot, twin).wait_send()
    for slot in range(4):
        half_piece(h, 0, slot, twin).wait_send()
    sum_sent(0)
    sum_sent(1)
    each(1, ns, lambda j: scan_copy(POINTS, j).wait_send())
    each(1, ns, lambda j: scan_copy(BACK, j).wait())


def slots_kernel(
    ns, sizes_ref, back_ref, mixed_in, wsum_ref, gsum_ref,
    mixed_ref, owned_ref, qkv_ref, out_ref, gain_ref, slots,
):
    width = back_ref.shape[1]
    slots[...] = jnp.zeros_like(slots)
    lane = lax.broadcasted_iota(jnp.int32, (width, 128), 1)

    def one(d, begin):
        size = sizes_ref[d, 0]
        tile = begin // 128
        off = begin - tile * 128
        block = jnp.where(lane < size, back_ref[d].astype(F32), 0.0)
        wide = jnp.concatenate([block, jnp.zeros_like(block)], axis=1)
        at = pl.ds(pl.multiple_of(tile * 128, 128), 256)
        slots[:, at] = slots[:, at] + pltpu.roll(wide, off, 1)
        return begin + size

    lax.fori_loop(0, ns, one, jnp.int32(0), unroll=8)
    owned_ref[...] = slots[...].astype(BF16)
    mixed_ref[...] = mixed_in[...]
    for i in range(3):
        qkv_ref[i] = wsum_ref[:, i * width : (i + 1) * width]
    out_ref[...] = wsum_ref[:, 3 * width :]
    gain_ref[...] = gsum_ref[:, :width]


def per_device(owner_ids, owned_points, norm_gain, qkv_weight, out_weight, cotangent):
    ns, nh = lax.axis_size("scan"), lax.axis_size("head")
    nx = nh // 2
    rows = owner_ids.shape[0]
    width, slot_count = owned_points.shape
    channels = width * nh
    strip = channels // ns
    shape = jax.ShapeDtypeStruct
    dma = pltpu.SemaphoreType.DMA
    vmem = pltpu.VMEM
    sizes, mixed, back, wsum, gsum = pl.pallas_call(
        functools.partial(main_kernel, ns, nh),
        out_shape=(
            shape((ns, 128), jnp.int32),
            shape((width, rows), BF16),
            shape((ns, width, BUCKET), BF16),
            shape((strip, 4 * width), F32),
            shape((1, 128), F32),
        ),
        in_specs=[VMEM, ANY, ANY, VMEM, ANY, ANY],
        out_specs=(VMEM,) * 5,
        scratch_shapes=[
            vmem((ns, 128), jnp.int32),
            vmem((ns, 128), jnp.int32),
            vmem((ns, 128), jnp.int32),
            vmem((ns, width, BUCKET), BF16),
            vmem((ns, width, BUCKET), BF16),
            vmem((ns * BUCKET, rows), BF16),
            vmem((channels, rows), BF16),
            vmem((channels, rows), BF16),
            vmem((1, rows), jnp.int32),
            vmem((channels, 128), F32),
            vmem((channels, rows), F32),
            vmem((channels, rows), BF16),
            vmem((width, rows), F32),
            vmem((width, rows), F32),
            vmem((width, rows), F32),
            vmem((width, rows), F32),
            vmem((width, rows), F32),
            vmem((3 * width, rows), BF16),
            vmem((width // HD, rows, rows), BF16),
            vmem((width // HD, 1, rows), F32),
            vmem((rows, 6 * HD), BF16),
            vmem((rows, 7 * HD), BF16),
            vmem((channels, rows), BF16),
            vmem((2, 2, width // 2, rows), F32),
            vmem((channels, rows), BF16),
            vmem((2, nx, width, rows), BF16),
            vmem((2, 2, width // 2, rows), BF16),
            vmem((2, 2, width // 2, rows), BF16),
            vmem((2, 2, width, rows), BF16),
            vmem((2, 2, width, rows), BF16),
            vmem((2, rows), F32),
            vmem((nh, 2, rows), F32),
            vmem((channels, 4 * width), BF16),
            vmem((ns, strip, 4 * width), BF16),
            vmem((1, 128), F32),
            vmem((ns, 1, 128), F32),
            vmem((ns, width, BUCKET), BF16),
            vmem((width, slot_count), BF16),
            vmem((3, width, channels), BF16),
            vmem((width, channels), BF16),
            dma((4,)),
            dma((5, ns)),
            dma((5, ns)),
            dma((8, nh)),
            dma((8, nh)),
        ],
        compiler_params=pltpu.CompilerParams(
            collective_id=1, has_side_effects=True, vmem_limit_bytes=LIMIT
        ),
        name="patch_block",
    )(owner_ids.reshape(1, rows), owned_points, cotangent, norm_gain.reshape(1, channels), qkv_weight, out_weight)
    mixed_rows, grad_owned, qkv_grad, out_grad, gain_grad = pl.pallas_call(
        functools.partial(slots_kernel, ns),
        out_shape=(
            shape((width, rows), BF16),
            shape((width, slot_count), BF16),
            shape((3, strip, width), F32),
            shape((strip, width), F32),
            shape((1, width), F32),
        ),
        in_specs=[SMEM] + [VMEM] * 4,
        out_specs=(VMEM,) * 5,
        scratch_shapes=[vmem((width, slot_count), F32)],
        compiler_params=pltpu.CompilerParams(vmem_limit_bytes=LIMIT),
        name="slots",
    )(sizes, back, mixed, wsum, gsum)
    return (
        mixed_rows,
        grad_owned,
        qkv_grad.transpose(0, 2, 1),
        out_grad.T,
        gain_grad.reshape(width),
    )


def solution(mesh):
    in_specs = (
        P("scan", None),
        P("head", "scan"),
        P(),
        P(None, "head", None),
        P("head", None),
        P("head", "scan"),
    )
    out_specs = (
        P("head", "scan"),
        P("head", "scan"),
        P(None, "head", "scan"),
        P("head", "scan"),
        P("head"),
    )
    return jax.shard_map(
        per_device, mesh=mesh, in_specs=in_specs, out_specs=out_specs, check_vma=False
    )
```

```python
import functools

import jax
import jax.numpy as jnp
from jax import lax
from jax.experimental import pallas as pl
from jax.experimental.pallas import tpu as pltpu
from jax.sharding import PartitionSpec as P

HD = 16
BUCKET = 128
EPS = 1e-05
SPAN = 1024
LOG2E = 1.4426950408889634
MESH = pl.DeviceIdType.MESH
F32 = jnp.float32
BF16 = jnp.bfloat16
VMEM = pl.BlockSpec(memory_space=pltpu.VMEM)
ANY = pl.BlockSpec(memory_space=pl.ANY)
SMEM = pl.BlockSpec(memory_space=pltpu.SMEM)
LIMIT = 56 * 1024 * 1024


def dot_nn(a, b):
    return lax.dot_general(a, b, (((1,), (0,)), ((), ())), preferred_element_type=F32)


def dot_nt(a, b):
    return lax.dot_general(a, b, (((1,), (1,)), ((), ())), preferred_element_type=F32)


def dot_tn(a, b):
    return lax.dot_general(a, b, (((0,), (0,)), ((), ())), preferred_element_type=F32)


def split2(x):
    high = x.astype(BF16)
    return high, (x - high.astype(F32)).astype(BF16)


def split3(x):
    high = x.astype(BF16)
    rest = x - high.astype(F32)
    middle = rest.astype(BF16)
    return high, middle, (rest - middle.astype(F32)).astype(BF16)


def left_stack(x):
    a, b, c = split3(x)
    return [a, b, a, b, c, a]


def right_stack(x):
    a, b, c = split3(x)
    return [a, a, b, b, a, c]


def hot_block(code, first, height):
    ids = lax.broadcasted_iota(jnp.int32, (height, code.shape[1]), 0) + first
    return jnp.where(ids == code, 1.0, 0.0).astype(BF16)


def aligned(first, size):
    return pl.ds(pl.multiple_of(first, size), size)


def each(first, last, act, unroll=True):
    def body(j, carry):
        act(j)
        return carry

    lax.fori_loop(first, last, body, 0, unroll=unroll)


TALLY, POINTS, WGRAD, BACK, GAIN = range(5)
COT, FULL, STATS, HALF, TWIN, _, SUM, _ = range(8)


def main_kernel(
    ns, nh, owner_ref, points_hbm, cot_hbm, gain_ref, weight_hbm, outw_hbm,
    sizes_ref, mixed_ref, back_ref, wsum_ref, gsum_ref,
    tall, tiles, offsets, windows, arrived, hots, full, cot, code_ref, gain_wide,
    normed, scaled, query, keys, value, gradc, context, grads, weights_all, shares,
    key_t, value_t, branch_out, near, part_out, twin_in, half_out, half_in, pair_out, pair_in, stats_out, stats_in,
    wgrad_out, wgrad_in, gain_out, gain_in, buckets, points_ref, weight_ref, outw_ref,
    local_sem, scan_send, scan_recv, head_send, head_recv,
):
    s, h = lax.axis_index("scan"), lax.axis_index("head")
    nx = nh // 2
    x, core = h // 2, lax.rem(h, 2)
    twin = x * 2 + 1 - core
    width, rows = cot_hbm.shape
    channels = width * nh
    strip = channels // ns
    mine = aligned(h * width, width)

    def remote(src, dst, send, recv, to):
        return pltpu.make_async_remote_copy(
            src_ref=src, dst_ref=dst, send_sem=send, recv_sem=recv, device_id=to, device_id_type=MESH
        )

    def scan_copy(which, j):
        peer = lax.rem(s + j, ns)
        if which == TALLY:
            src, dst = tall.at[pl.ds(peer, 1), :], sizes_ref.at[pl.ds(s, 1), :]
        elif which == POINTS:
            src, dst = windows.at[peer], arrived.at[s]
        elif which == WGRAD:
            src, dst = wgrad_out.at[aligned(peer * strip, strip), :], wgrad_in.at[s]
        elif which == BACK:
            src, dst = buckets.at[peer], back_ref.at[s]
        else:
            src, dst = gain_out, gain_in.at[s]
        return remote(src, dst, scan_send.at[which, j], scan_recv.at[which, j], (peer, h))

    def stats_copy(j):
        peer = lax.rem(h + j, nh)
        return remote(
            stats_out, stats_in.at[h], head_send.at[STATS, j], head_recv.at[STATS, j], (s, peer)
        )

    def push(which, ref, piece, slot, to):
        block = ref.at[aligned(piece * width, width), :]
        return remote(block, block, head_send.at[which, slot], head_recv.at[which, piece], (s, to))

    left, right, across = lax.rem(x + nx - 1, nx), lax.rem(x + 1, nx), lax.rem(x + 2, nx)
    mid = width // 2

    def half_piece(piece, half, slot, to):
        block = full.at[aligned(piece * width + half * mid, mid), :]
        return remote(block, block, head_send.at[HALF, slot], head_recv.at[HALF, slot], (s, to))

    def spread(which, ref):
        for j in (nx // 2, *[j for j in range(1, nx) if j != nx // 2]):
            push(which, ref, h, j, lax.rem(x + j, nx) * 2 + core).start()
        push(which, ref, h, 0, twin).start()

    def relay(which, ref):
        for j in range(1, nx):
            piece = lax.rem(x + nx - j, nx) * 2 + core
            push(which, ref, piece, nx + j, twin).wait_recv()
            push(which, ref, piece, nx + j, twin).start()

    def arrive(which, ref):
        for j in range(nx):
            piece = lax.rem(x + nx - j, nx) * 2 + 1 - core
            push(which, ref, piece, 0, twin).wait_recv()

    def sent(which, ref):
        for j in range(1, nx):
            push(which, ref, h, j, twin).wait_send()
            push(which, ref, h, nx + j, twin).wait_send()
        push(which, ref, h, 0, twin).wait_send()

    def twin_copy(k, j):
        to = lax.rem(x + j, nx)
        src = (part_out, branch_out)[k].at[aligned((to * 2 + 1 - core) * width, width), :]
        dst = twin_in.at[k, j]
        return remote(src, dst, head_send.at[TWIN + k, j], head_recv.at[TWIN + k, j], (s, twin))

    def sum_copy(k, slot):
        side, half = ((0, 0), (1, 1), (0, 1), (1, 0), (0, 0), (1, 1))[slot]
        if slot < 2:
            src, dst = half_out.at[k, side], half_in.at[k, side]
        else:
            rows_of = pl.ds(half * mid, mid)
            src, dst = pair_out.at[k, side, rows_of, :], pair_in.at[k, side, rows_of, :]
        to = (right, left)[side] * 2 + core
        return remote(src, dst, head_send.at[SUM + k, slot], head_recv.at[SUM + k, slot], (s, to))

    def pair_sum(k, j):
        twin_copy(k, j).wait_recv()
        ref = (part_out, branch_out)[k]
        own = ref[aligned((lax.rem(x + j, nx) * 2 + core) * width, width), :]
        return own.astype(F32) + twin_in[k, j].astype(F32)

    def sum_begin(k):
        for j in (2, 1, 3, 0):
            twin_copy(k, j).start()

    def sum_far(k):
        far_sum = pair_sum(k, 2).astype(BF16)
        half_out[k, 0] = far_sum[:mid]
        half_out[k, 1] = far_sum[mid:]
        sum_copy(k, 0).start()
        sum_copy(k, 1).start()
        to_right, to_left = pair_sum(k, 1), pair_sum(k, 3)
        pair_out[k, 0, mid:, :] = to_right[mid:].astype(BF16)
        sum_copy(k, 2).start()
        pair_out[k, 1, :mid, :] = to_left[:mid].astype(BF16)
        sum_copy(k, 3).start()
        near[k, 0] = to_right[:mid]
        near[k, 1] = to_left[mid:]

    def sum_near(k):
        sum_copy(k, 0).wait_recv()
        pair_out[k, 0, :mid, :] = (near[k, 0] + half_in[k, 0].astype(F32)).astype(BF16)
        sum_copy(k, 4).start()
        sum_copy(k, 1).wait_recv()
        pair_out[k, 1, mid:, :] = (near[k, 1] + half_in[k, 1].astype(F32)).astype(BF16)
        sum_copy(k, 5).start()

    def sum_end(k):
        own = pair_sum(k, 0)
        for slot in range(2, 6):
            sum_copy(k, slot).wait_recv()
        return own + pair_in[k, 0].astype(F32) + pair_in[k, 1].astype(F32)

    def sum_sent(k):
        for j in range(nx):
            twin_copy(k, j).wait_send()
        for slot in range(6):
            sum_copy(k, slot).wait_send()

    barrier = pltpu.get_barrier_semaphore()

    def greet_scan(j):
        pl.semaphore_signal(
            barrier, inc=1, device_id=(lax.rem(s + j, ns), h), device_id_type=MESH
        )

    def greet_head(j):
        pl.semaphore_signal(
            barrier, inc=1, device_id=(s, lax.rem(h + j, nh)), device_id_type=MESH
        )

    each(1, ns, greet_scan)
    each(1, nh, greet_head)
    fetches = [
        pltpu.make_async_copy(src, dst, local_sem.at[i])
        for i, (src, dst) in enumerate(
            [
                (cot_hbm, cot.at[mine, :]),
                (points_hbm, points_ref),
                (outw_hbm, outw_ref),
                (weight_hbm, weight_ref),
            ]
        )
    ]
    for fetch in fetches:
        fetch.start()
    owners = owner_ref[...]
    hot = lax.broadcasted_iota(jnp.int32, (ns, rows), 0) == owners
    ones = jnp.where(hot, 1.0, 0.0)
    total = jnp.sum(jnp.where(hot, 1, 0), axis=1, keepdims=True)
    tall[...] = jnp.broadcast_to(total, (ns, 128))
    pl.semaphore_wait(barrier, ns + nh - 2)

    each(1, ns, lambda j: scan_copy(TALLY, j).start())
    fetches[0].wait()
    spread(COT, cot)
    sizes_ref[pl.ds(s, 1), :] = tall[pl.ds(s, 1), :]
    before = jnp.where(
        lax.broadcasted_iota(jnp.int32, (128, 128), 0)
        < lax.broadcasted_iota(jnp.int32, (128, 128), 1),
        1.0,
        0.0,
    ).astype(BF16)
    carried = jnp.zeros((ns, 1), F32)
    for b in range(0, rows, 128):
        part = ones[:, b : b + 128]
        running = dot_nn(part.astype(BF16), before) + carried
        rank = jnp.sum(running * part, axis=0, keepdims=True)
        code_ref[:, b : b + 128] = owners[:, b : b + 128] * BUCKET + rank.astype(jnp.int32)
        carried = carried + jnp.sum(part, axis=1, keepdims=True)
    code = code_ref[...]

    def build(i):
        first = pl.multiple_of(i * 256, 256)
        hots[pl.ds(first, 256), :] = hot_block(code, first, 256)

    each(0, ns // 2, build, False)
    gain = jnp.transpose(jnp.broadcast_to(gain_ref[...], (8, channels)))[:, :1]
    gain_wide[...] = jnp.broadcast_to(gain, gain_wide.shape)
    each(1, ns, lambda j: scan_copy(TALLY, j).wait())

    earlier = jnp.where(
        lax.broadcasted_iota(jnp.int32, (ns, ns), 1) < lax.broadcasted_iota(jnp.int32, (ns, ns), 0),
        1.0,
        0.0,
    ).astype(BF16)
    begins = dot_nn(earlier, sizes_ref[...].astype(F32).astype(BF16)).astype(jnp.int32)
    tiles[...] = begins // 128
    offsets[...] = begins - begins // 128 * 128
    span = lax.broadcasted_iota(jnp.int32, (256, 128), 0) - lax.broadcasted_iota(
        jnp.int32, (256, 128), 1
    )
    groups = ns // 4

    def nth_group(i):
        half = (i + 1) // 2
        shift = groups // 2 + half * (lax.rem(i, 2) * 2 - 1)
        return lax.rem(s // 4 + shift + groups, groups)

    def send_group(which, group, last):
        for t in range(4):
            peer = group * 4 + t
            if last:

                @pl.when(peer != s)
                def _():
                    scan_copy(which, lax.rem(peer - s + ns, ns)).start()

            else:
                scan_copy(which, lax.rem(peer - s + ns, ns)).start()

    def cut_and_send(i, last):
        group = nth_group(i)
        places = [
            jnp.broadcast_to(tiles[pl.ds(group * 4 + t, 1), :], (16, 128)).astype(F32).astype(BF16)
            for t in range(4)
        ]
        zero = jnp.zeros((width // 16, 16, 128), BF16)

        held = [zero] * 8
        for n in range(ns + 1):
            tile = points_ref[:, 128 * n : 128 * (n + 1)].reshape(zero.shape)
            for t in range(4):
                if n < ns:
                    held[t] = jnp.where((places[t] == n)[None], tile, held[t])
                if n > 0:
                    held[4 + t] = jnp.where((places[t] == n - 1)[None], tile, held[4 + t])
        low, high = held[:4], held[4:]
        for t in range(4):
            peer = group * 4 + t
            window = jnp.concatenate(
                [low[t].reshape(width, 128), high[t].reshape(width, 128)], axis=1
            )
            pick = jnp.where(span == offsets[pl.ds(peer, 1), :], 1.0, 0.0).astype(BF16)
            windows[peer] = dot_nn(window, pick).astype(BF16)
        send_group(POINTS, group, last)

    for fetch in fetches[1:]:
        fetch.wait()
    each(0, groups - 1, lambda i: cut_and_send(i, False), False)
    cut_and_send(groups - 1, True)
    arrived[pl.ds(s, 1)] = windows[pl.ds(s, 1)]
    relay(COT, cot)

    gathered = jnp.zeros((width, rows), F32)
    for i in range(groups):
        group = nth_group(i)
        for t in range(4):
            source = group * 4 + t

            def landed(source=source):
                scan_copy(POINTS, lax.rem(s - source + ns, ns)).wait_recv()

            if i < groups - 1:
                landed()
            else:
                pl.when(source != s)(landed)
        pieces = jnp.concatenate([arrived[group * 4 + t] for t in range(4)], axis=1)
        gathered = gathered + dot_nn(pieces, hots[aligned(group * 512, 512), :])
    full[mine, :] = gathered.astype(BF16)
    half_piece(h, 0, 4, right * 2 + core).start()
    half_piece(h, 1, 6, left * 2 + core).start()
    half_piece(h, 1, 5, right * 2 + core).start()
    half_piece(h, 0, 7, left * 2 + core).start()
    push(FULL, full, h, 0, twin).start()
    from_left, from_right = left * 2 + core, right * 2 + core
    half_piece(from_left, 0, 4, twin).wait_recv()
    half_piece(from_left, 0, 0, right * 2 + core).start()
    half_piece(from_right, 1, 6, twin).wait_recv()
    half_piece(from_right, 1, 1, left * 2 + core).start()
    half_piece(from_left, 1, 5, twin).wait_recv()
    push(FULL, full, from_left, nx + 1, twin).start()
    half_piece(from_right, 0, 7, twin).wait_recv()
    push(FULL, full, from_right, nx + 3, twin).start()
    arrive(COT, cot)
    gradc[...] = dot_nn(outw_ref[...], cot[...])
    for half in range(2):
        half_piece(across * 2 + core, half, half, twin).wait_recv()
        half_piece(across * 2 + core, half, 2 + half, twin).start()
    for at in (x, left, right):
        push(FULL, full, at * 2 + 1 - core, 0, twin).wait_recv()
    for half in range(2):
        half_piece(across * 2 + 1 - core, half, 2 + half, twin).wait_recv()

    floats = full[...].astype(F32)
    mean = jnp.sum(floats, axis=0, keepdims=True) * (1.0 / channels)
    centered = floats - mean
    inv = lax.rsqrt(jnp.sum(centered * centered, axis=0, keepdims=True) * (1.0 / channels) + EPS)
    normed[...] = centered * inv
    scaled[...] = (normed[...] * gain_wide[:, :1]).astype(BF16)
    for i, ref in enumerate((query, keys, value)):
        ref[...] = dot_nn(weight_ref[i], scaled[...])

    def forward(head):
        at = aligned(head * HD, HD)
        q, k, v = query[at, :], keys[at, :], value[at, :]
        key_t[...] = jnp.transpose(jnp.concatenate(left_stack(k), axis=0))
        v_rows = jnp.concatenate(list(split2(v)) + [jnp.ones((HD, rows), BF16)], axis=0)
        for b in range(0, rows, SPAN):
            q_stack = jnp.concatenate(
                right_stack(q[:, b : b + SPAN] * (HD**-0.5 * LOG2E)), axis=0
            )
            scores = dot_nn(key_t[...], q_stack)
            peak = jnp.max(scores, axis=0, keepdims=True)
            weights = jnp.exp2(scores - peak).astype(BF16)
            weights_all[head, :, b : b + SPAN] = weights
            sums = dot_nn(v_rows, weights)
            share = 1.0 / sums[2 * HD : 2 * HD + 1]
            shares[head, :, b : b + SPAN] = share
            ctx = (sums[:HD] + sums[HD : 2 * HD]) * share
            context[at, b : b + SPAN] = ctx

    for head in range(width // HD):
        forward(head)
    context_b = context[...].astype(BF16)
    branch_out[...] = dot_tn(outw_ref[...], context_b).astype(BF16)
    sum_begin(1)

    def backward(head):
        at = aligned(head * HD, HD)
        q, k, v = query[at, :], keys[at, :], value[at, :]
        row = lax.broadcasted_iota(jnp.int32, (HD, rows), 0)
        ones = jnp.ones((HD, rows), BF16)
        value_t[...] = jnp.transpose(jnp.concatenate(left_stack(v) + [ones], axis=0))
        k_rows = jnp.concatenate(list(split2(k)), axis=0)
        gs = gradc[at, :] * shares[head]
        center = jnp.sum(gs * context[at, :], axis=0, keepdims=True) * (-(HD**-0.5))
        parts = [t.astype(F32) for t in split3(center)]
        tail = jnp.where(
            row == 0, parts[0], jnp.where(row == 1, parts[1], jnp.where(row == 2, parts[2], 0.0))
        ).astype(BF16)
        g_stack = jnp.concatenate(right_stack(gs * HD**-0.5) + [tail], axis=0)
        g_rows = jnp.concatenate(list(split2(gs)), axis=0)
        q_rows = jnp.concatenate(list(split2(q)), axis=0)
        key_grad = jnp.zeros((HD * 2, rows), F32)
        value_grad = jnp.zeros((HD * 2, rows), F32)
        for b in range(0, rows, SPAN):
            weights = weights_all[head, :, b : b + SPAN]
            delta = dot_nn(value_t[...], g_stack[:, b : b + SPAN])
            score_grad = (weights.astype(F32) * delta).astype(BF16)
            value_grad = value_grad + dot_nt(g_rows[:, b : b + SPAN], weights)
            dq = dot_nn(k_rows, score_grad)
            grads[at, b : b + SPAN] = (dq[:HD] + dq[HD:]).astype(BF16)
            key_grad = key_grad + dot_nt(q_rows[:, b : b + SPAN], score_grad)
        k_at = aligned(width + head * HD, HD)
        v_at = aligned(2 * width + head * HD, HD)
        grads[k_at, :] = (key_grad[:HD] + key_grad[HD:]).astype(BF16)
        grads[v_at, :] = (value_grad[:HD] + value_grad[HD:]).astype(BF16)

    for head in range(width // HD):
        backward(head)
        if head == 0:
            sum_far(1)
        elif head == 1:
            sum_near(1)

    whole = jnp.concatenate([weight_ref[i] for i in range(3)], axis=0)
    part_out[...] = dot_tn(whole, grads[...]).astype(BF16)

    sum_begin(0)
    wgrad_out[:, : 3 * width] = dot_nt(scaled[...], grads[...]).astype(BF16)
    wgrad_out[:, 3 * width :] = dot_nt(cot[...], context_b).astype(BF16)
    each(1, ns, lambda j: scan_copy(WGRAD, j).start())
    sum_far(0)
    weighted = part_out[...].astype(F32) * gain_wide[:, :1]
    stats_out[0:1, :] = jnp.sum(weighted, axis=0, keepdims=True)
    stats_out[1:2, :] = jnp.sum(weighted * normed[...], axis=0, keepdims=True)
    each(1, nh, lambda j: stats_copy(j).start())

    sum_near(0)
    wgrad_in[pl.ds(s, 1)] = wgrad_out[aligned(s * strip, strip), :][None]
    branch = sum_end(1)
    mixed_ref[...] = (full[mine, :].astype(F32) + branch).astype(BF16)
    each(1, nh, lambda j: stats_copy(j).wait())
    stats = stats_out[...]
    for i in range(1, nh):
        stats = stats + stats_in[lax.rem(h + i, nh)]
    normed_grad = sum_end(0)
    normed_own = normed[mine, :]
    first, second = stats[0:1] * (1.0 / channels), stats[1:2] * (1.0 / channels)
    grad = inv * (normed_grad * gain_wide[mine, :1] - first - normed_own * second)
    points_grad = (cot[mine, :].astype(F32) + grad).astype(BF16)

    for i in range(groups):
        group = nth_group(i)
        block = dot_nt(points_grad, hots[aligned(group * 512, 512), :]).astype(BF16)
        for t in range(4):
            buckets[group * 4 + t] = block[:, 128 * t : 128 * (t + 1)]
        send_group(BACK, group, i == groups - 1)

    back_ref[pl.ds(s, 1)] = buckets[pl.ds(s, 1)]
    product = normed_grad * normed_own
    folded = product[:, :128]
    for b in range(128, rows, 128):
        folded = folded + product[:, b : b + 128]
    gain_out[...] = jnp.zeros_like(gain_out)
    gain_out[:, :width] = jnp.sum(jnp.transpose(folded), axis=0, keepdims=True)
    each(1, ns, lambda j: scan_copy(GAIN, j).start())
    gain_in[pl.ds(s, 1)] = gain_out[...][None]
    each(1, ns, lambda j: scan_copy(WGRAD, j).wait())
    wsum_ref[...] = jnp.sum(wgrad_in[...].astype(F32), axis=0)
    each(1, ns, lambda j: scan_copy(GAIN, j).wait())
    gsum_ref[...] = jnp.sum(gain_in[...], axis=0)
    sent(COT, cot)
    for slot in (0, nx + 1, nx + 3):
        push(FULL, full, h, slot, twin).wait_send()
    for slot in range(8):
        half_piece(h, 0, slot, twin).wait_send()
    sum_sent(0)
    sum_sent(1)
    each(1, ns, lambda j: scan_copy(POINTS, j).wait_send())
    each(1, ns, lambda j: scan_copy(BACK, j).wait())


def slots_kernel(
    ns, sizes_ref, back_ref, mixed_in, wsum_ref, gsum_ref,
    mixed_ref, owned_ref, qkv_ref, out_ref, gain_ref, slots,
):
    width = back_ref.shape[1]
    slots[...] = jnp.zeros_like(slots)
    lane = lax.broadcasted_iota(jnp.int32, (width, 128), 1)

    def one(d, begin):
        size = sizes_ref[d, 0]
        tile = begin // 128
        off = begin - tile * 128
        block = jnp.where(lane < size, back_ref[d].astype(F32), 0.0)
        wide = jnp.concatenate([block, jnp.zeros_like(block)], axis=1)
        at = pl.ds(pl.multiple_of(tile * 128, 128), 256)
        slots[:, at] = slots[:, at] + pltpu.roll(wide, off, 1)
        return begin + size

    lax.fori_loop(0, ns, one, jnp.int32(0), unroll=8)
    owned_ref[...] = slots[...].astype(BF16)
    mixed_ref[...] = mixed_in[...]
    for i in range(3):
        qkv_ref[i] = wsum_ref[:, i * width : (i + 1) * width]
    out_ref[...] = wsum_ref[:, 3 * width :]
    gain_ref[...] = gsum_ref[:, :width]


def per_device(owner_ids, owned_points, norm_gain, qkv_weight, out_weight, cotangent):
    ns, nh = lax.axis_size("scan"), lax.axis_size("head")
    nx = nh // 2
    rows = owner_ids.shape[0]
    width, slot_count = owned_points.shape
    channels = width * nh
    strip = channels // ns
    shape = jax.ShapeDtypeStruct
    dma = pltpu.SemaphoreType.DMA
    vmem = pltpu.VMEM
    sizes, mixed, back, wsum, gsum = pl.pallas_call(
        functools.partial(main_kernel, ns, nh),
        out_shape=(
            shape((ns, 128), jnp.int32),
            shape((width, rows), BF16),
            shape((ns, width, BUCKET), BF16),
            shape((strip, 4 * width), F32),
            shape((1, 128), F32),
        ),
        in_specs=[VMEM, ANY, ANY, VMEM, ANY, ANY],
        out_specs=(VMEM,) * 5,
        scratch_shapes=[
            vmem((ns, 128), jnp.int32),
            vmem((ns, 128), jnp.int32),
            vmem((ns, 128), jnp.int32),
            vmem((ns, width, BUCKET), BF16),
            vmem((ns, width, BUCKET), BF16),
            vmem((ns * BUCKET, rows), BF16),
            vmem((channels, rows), BF16),
            vmem((channels, rows), BF16),
            vmem((1, rows), jnp.int32),
            vmem((channels, 128), F32),
            vmem((channels, rows), F32),
            vmem((channels, rows), BF16),
            vmem((width, rows), F32),
            vmem((width, rows), F32),
            vmem((width, rows), F32),
            vmem((width, rows), F32),
            vmem((width, rows), F32),
            vmem((3 * width, rows), BF16),
            vmem((width // HD, rows, rows), BF16),
            vmem((width // HD, 1, rows), F32),
            vmem((rows, 6 * HD), BF16),
            vmem((rows, 7 * HD), BF16),
            vmem((channels, rows), BF16),
            vmem((2, 2, width // 2, rows), F32),
            vmem((channels, rows), BF16),
            vmem((2, nx, width, rows), BF16),
            vmem((2, 2, width // 2, rows), BF16),
            vmem((2, 2, width // 2, rows), BF16),
            vmem((2, 2, width, rows), BF16),
            vmem((2, 2, width, rows), BF16),
            vmem((2, rows), F32),
            vmem((nh, 2, rows), F32),
            vmem((channels, 4 * width), BF16),
            vmem((ns, strip, 4 * width), BF16),
            vmem((1, 128), F32),
            vmem((ns, 1, 128), F32),
            vmem((ns, width, BUCKET), BF16),
            vmem((width, slot_count), BF16),
            vmem((3, width, channels), BF16),
            vmem((width, channels), BF16),
            dma((4,)),
            dma((5, ns)),
            dma((5, ns)),
            dma((8, nh)),
            dma((8, nh)),
        ],
        compiler_params=pltpu.CompilerParams(
            collective_id=1, has_side_effects=True, vmem_limit_bytes=LIMIT
        ),
        name="patch_block",
    )(owner_ids.reshape(1, rows), owned_points, cotangent, norm_gain.reshape(1, channels), qkv_weight, out_weight)
    mixed_rows, grad_owned, qkv_grad, out_grad, gain_grad = pl.pallas_call(
        functools.partial(slots_kernel, ns),
        out_shape=(
            shape((width, rows), BF16),
            shape((width, slot_count), BF16),
            shape((3, strip, width), F32),
            shape((strip, width), F32),
            shape((1, width), F32),
        ),
        in_specs=[SMEM] + [VMEM] * 4,
        out_specs=(VMEM,) * 5,
        scratch_shapes=[vmem((width, slot_count), F32)],
        compiler_params=pltpu.CompilerParams(vmem_limit_bytes=LIMIT),
        name="slots",
    )(sizes, back, mixed, wsum, gsum)
    return (
        mixed_rows,
        grad_owned,
        qkv_grad.transpose(0, 2, 1),
        out_grad.T,
        gain_grad.reshape(width),
    )


def solution(mesh):
    in_specs = (
        P("scan", None),
        P("head", "scan"),
        P(),
        P(None, "head", None),
        P("head", None),
        P("head", "scan"),
    )
    out_specs = (
        P("head", "scan"),
        P("head", "scan"),
        P(None, "head", "scan"),
        P("head", "scan"),
        P("head"),
    )
    return jax.shard_map(
        per_device, mesh=mesh, in_specs=in_specs, out_specs=out_specs, check_vma=False
    )
```

```python
import functools

import jax
import jax.numpy as jnp
from jax import lax
from jax.experimental import pallas as pl
from jax.experimental.pallas import tpu as pltpu
from jax.sharding import PartitionSpec as P

HD = 16
BUCKET = 128
EPS = 1e-05
SPAN = 1024
LOG2E = 1.4426950408889634
MESH = pl.DeviceIdType.MESH
F32 = jnp.float32
BF16 = jnp.bfloat16
VMEM = pl.BlockSpec(memory_space=pltpu.VMEM)
ANY = pl.BlockSpec(memory_space=pl.ANY)
SMEM = pl.BlockSpec(memory_space=pltpu.SMEM)
LIMIT = 56 * 1024 * 1024


def dot_nn(a, b):
    return lax.dot_general(a, b, (((1,), (0,)), ((), ())), preferred_element_type=F32)


def dot_nt(a, b):
    return lax.dot_general(a, b, (((1,), (1,)), ((), ())), preferred_element_type=F32)


def dot_tn(a, b):
    return lax.dot_general(a, b, (((0,), (0,)), ((), ())), preferred_element_type=F32)


def split2(x):
    high = x.astype(BF16)
    return high, (x - high.astype(F32)).astype(BF16)


def split3(x):
    high = x.astype(BF16)
    rest = x - high.astype(F32)
    middle = rest.astype(BF16)
    return high, middle, (rest - middle.astype(F32)).astype(BF16)


def left_stack(x):
    a, b, c = split3(x)
    return [a, b, a, b, c, a]


def right_stack(x):
    a, b, c = split3(x)
    return [a, a, b, b, a, c]


def hot_block(code, first, height):
    ids = lax.broadcasted_iota(jnp.int32, (height, code.shape[1]), 0) + first
    return jnp.where(ids == code, 1.0, 0.0).astype(BF16)


def aligned(first, size):
    return pl.ds(pl.multiple_of(first, size), size)


def each(first, last, act, unroll=True):
    def body(j, carry):
        act(j)
        return carry

    lax.fori_loop(first, last, body, 0, unroll=unroll)


TALLY, POINTS, WGRAD, BACK, GAIN = range(5)
COT, FULL, STATS, HALF, TWIN, _, SUM, _ = range(8)


def main_kernel(
    ns, nh, owner_ref, points_hbm, cot_hbm, gain_ref, weight_hbm, outw_hbm,
    sizes_ref, mixed_ref, back_ref, wsum_ref, gsum_ref,
    tall, tiles, offsets, windows, arrived, hots, full, cot, code_ref, gain_wide,
    normed, scaled, query, keys, value, gradc, context, grads, weights_all, shares,
    key_t, value_t, branch_out, near, part_out, twin_in, half_out, half_in, pair_out, pair_in, stats_out, stats_in,
    wgrad_out, wgrad_in, gain_out, gain_in, buckets, points_ref, weight_ref, outw_ref,
    local_sem, scan_send, scan_recv, head_send, head_recv,
):
    s, h = lax.axis_index("scan"), lax.axis_index("head")
    nx = nh // 2
    x, core = h // 2, lax.rem(h, 2)
    twin = x * 2 + 1 - core
    width, rows = cot_hbm.shape
    channels = width * nh
    strip = channels // ns
    mine = aligned(h * width, width)

    def remote(src, dst, send, recv, to):
        return pltpu.make_async_remote_copy(
            src_ref=src, dst_ref=dst, send_sem=send, recv_sem=recv, device_id=to, device_id_type=MESH
        )

    def scan_copy(which, j):
        peer = lax.rem(s + j, ns)
        if which == TALLY:
            src, dst = tall.at[pl.ds(peer, 1), :], sizes_ref.at[pl.ds(s, 1), :]
        elif which == POINTS:
            src, dst = windows.at[peer], arrived.at[s]
        elif which == WGRAD:
            src, dst = wgrad_out.at[aligned(peer * strip, strip), :], wgrad_in.at[s]
        elif which == BACK:
            src, dst = buckets.at[peer], back_ref.at[s]
        else:
            src, dst = gain_out, gain_in.at[s]
        return remote(src, dst, scan_send.at[which, j], scan_recv.at[which, j], (peer, h))

    def stats_copy(j):
        peer = lax.rem(h + j, nh)
        return remote(
            stats_out, stats_in.at[h], head_send.at[STATS, j], head_recv.at[STATS, j], (s, peer)
        )

    def push(which, ref, piece, slot, to):
        block = ref.at[aligned(piece * width, width), :]
        return remote(block, block, head_send.at[which, slot], head_recv.at[which, piece], (s, to))

    left, right, across = lax.rem(x + nx - 1, nx), lax.rem(x + 1, nx), lax.rem(x + 2, nx)
    mid = width // 2

    def half_piece(piece, half, slot, to):
        block = full.at[aligned(piece * width + half * mid, mid), :]
        return remote(block, block, head_send.at[HALF, slot], head_recv.at[HALF, slot], (s, to))

    def spread(which, ref):
        for j in (nx // 2, *[j for j in range(1, nx) if j != nx // 2]):
            push(which, ref, h, j, lax.rem(x + j, nx) * 2 + core).start()
        push(which, ref, h, 0, twin).start()

    def relay(which, ref):
        for j in range(1, nx):
            piece = lax.rem(x + nx - j, nx) * 2 + core
            push(which, ref, piece, nx + j, twin).wait_recv()
            push(which, ref, piece, nx + j, twin).start()

    def arrive(which, ref):
        for j in range(nx):
            piece = lax.rem(x + nx - j, nx) * 2 + 1 - core
            push(which, ref, piece, 0, twin).wait_recv()

    def sent(which, ref):
        for j in range(1, nx):
            push(which, ref, h, j, twin).wait_send()
            push(which, ref, h, nx + j, twin).wait_send()
        push(which, ref, h, 0, twin).wait_send()

    def twin_copy(k, j):
        to = lax.rem(x + j, nx)
        src = (part_out, branch_out)[k].at[aligned((to * 2 + 1 - core) * width, width), :]
        dst = twin_in.at[k, j]
        return remote(src, dst, head_send.at[TWIN + k, j], head_recv.at[TWIN + k, j], (s, twin))

    def sum_copy(k, slot):
        side, half = ((0, 0), (1, 1), (0, 1), (1, 0), (0, 0), (1, 1))[slot]
        if slot < 2:
            src, dst = half_out.at[k, side], half_in.at[k, side]
        else:
            rows_of = pl.ds(half * mid, mid)
            src, dst = pair_out.at[k, side, rows_of, :], pair_in.at[k, side, rows_of, :]
        to = (right, left)[side] * 2 + core
        return remote(src, dst, head_send.at[SUM + k, slot], head_recv.at[SUM + k, slot], (s, to))

    def pair_sum(k, j):
        twin_copy(k, j).wait_recv()
        ref = (part_out, branch_out)[k]
        own = ref[aligned((lax.rem(x + j, nx) * 2 + core) * width, width), :]
        return own.astype(F32) + twin_in[k, j].astype(F32)

    def sum_begin(k):
        for j in (2, 1, 3, 0):
            twin_copy(k, j).start()

    def sum_far(k):
        far_sum = pair_sum(k, 2).astype(BF16)
        half_out[k, 0] = far_sum[:mid]
        half_out[k, 1] = far_sum[mid:]
        sum_copy(k, 0).start()
        sum_copy(k, 1).start()
        to_right, to_left = pair_sum(k, 1), pair_sum(k, 3)
        pair_out[k, 0, mid:, :] = to_right[mid:].astype(BF16)
        sum_copy(k, 2).start()
        pair_out[k, 1, :mid, :] = to_left[:mid].astype(BF16)
        sum_copy(k, 3).start()
        near[k, 0] = to_right[:mid]
        near[k, 1] = to_left[mid:]

    def sum_near(k):
        sum_copy(k, 0).wait_recv()
        pair_out[k, 0, :mid, :] = (near[k, 0] + half_in[k, 0].astype(F32)).astype(BF16)
        sum_copy(k, 4).start()
        sum_copy(k, 1).wait_recv()
        pair_out[k, 1, mid:, :] = (near[k, 1] + half_in[k, 1].astype(F32)).astype(BF16)
        sum_copy(k, 5).start()

    def sum_end(k):
        own = pair_sum(k, 0)
        for slot in range(2, 6):
            sum_copy(k, slot).wait_recv()
        return own + pair_in[k, 0].astype(F32) + pair_in[k, 1].astype(F32)

    def sum_sent(k):
        for j in range(nx):
            twin_copy(k, j).wait_send()
        for slot in range(6):
            sum_copy(k, slot).wait_send()

    barrier = pltpu.get_barrier_semaphore()

    def greet_scan(j):
        pl.semaphore_signal(
            barrier, inc=1, device_id=(lax.rem(s + j, ns), h), device_id_type=MESH
        )

    def greet_head(j):
        pl.semaphore_signal(
            barrier, inc=1, device_id=(s, lax.rem(h + j, nh)), device_id_type=MESH
        )

    each(1, ns, greet_scan)
    each(1, nh, greet_head)
    fetches = [
        pltpu.make_async_copy(src, dst, local_sem.at[i])
        for i, (src, dst) in enumerate(
            [
                (cot_hbm, cot.at[mine, :]),
                (points_hbm, points_ref),
                (outw_hbm, outw_ref),
                (weight_hbm, weight_ref),
            ]
        )
    ]
    for fetch in fetches:
        fetch.start()
    owners = owner_ref[...]
    hot = lax.broadcasted_iota(jnp.int32, (ns, rows), 0) == owners
    ones = jnp.where(hot, 1.0, 0.0)
    total = jnp.sum(jnp.where(hot, 1, 0), axis=1, keepdims=True)
    tall[...] = jnp.broadcast_to(total, (ns, 128))
    pl.semaphore_wait(barrier, ns + nh - 2)

    each(1, ns, lambda j: scan_copy(TALLY, j).start())
    fetches[0].wait()
    spread(COT, cot)
    sizes_ref[pl.ds(s, 1), :] = tall[pl.ds(s, 1), :]
    before = jnp.where(
        lax.broadcasted_iota(jnp.int32, (128, 128), 0)
        < lax.broadcasted_iota(jnp.int32, (128, 128), 1),
        1.0,
        0.0,
    ).astype(BF16)
    carried = jnp.zeros((ns, 1), F32)
    for b in range(0, rows, 128):
        part = ones[:, b : b + 128]
        running = dot_nn(part.astype(BF16), before) + carried
        rank = jnp.sum(running * part, axis=0, keepdims=True)
        code_ref[:, b : b + 128] = owners[:, b : b + 128] * BUCKET + rank.astype(jnp.int32)
        carried = carried + jnp.sum(part, axis=1, keepdims=True)
    code = code_ref[...]

    def build(i):
        first = pl.multiple_of(i * 256, 256)
        hots[pl.ds(first, 256), :] = hot_block(code, first, 256)

    each(0, ns // 2, build, False)
    gain = jnp.transpose(jnp.broadcast_to(gain_ref[...], (8, channels)))[:, :1]
    gain_wide[...] = jnp.broadcast_to(gain, gain_wide.shape)
    each(1, ns, lambda j: scan_copy(TALLY, j).wait())

    earlier = jnp.where(
        lax.broadcasted_iota(jnp.int32, (ns, ns), 1) < lax.broadcasted_iota(jnp.int32, (ns, ns), 0),
        1.0,
        0.0,
    ).astype(BF16)
    begins = dot_nn(earlier, sizes_ref[...].astype(F32).astype(BF16)).astype(jnp.int32)
    tiles[...] = begins // 128
    offsets[...] = begins - begins // 128 * 128
    span = lax.broadcasted_iota(jnp.int32, (256, 128), 0) - lax.broadcasted_iota(
        jnp.int32, (256, 128), 1
    )
    groups = ns // 4

    def nth_group(i):
        half = (i + 1) // 2
        shift = groups // 2 + half * (lax.rem(i, 2) * 2 - 1)
        return lax.rem(s // 4 + shift + groups, groups)

    def send_group(which, group, last):
        for t in range(4):
            peer = group * 4 + t
            if last:

                @pl.when(peer != s)
                def _():
                    scan_copy(which, lax.rem(peer - s + ns, ns)).start()

            else:
                scan_copy(which, lax.rem(peer - s + ns, ns)).start()

    def cut_and_send(i, last):
        group = nth_group(i)
        places = [
            jnp.broadcast_to(tiles[pl.ds(group * 4 + t, 1), :], (16, 128)).astype(F32).astype(BF16)
            for t in range(4)
        ]
        zero = jnp.zeros((width // 16, 16, 128), BF16)

        held = [zero] * 8
        for n in range(ns + 1):
            tile = points_ref[:, 128 * n : 128 * (n + 1)].reshape(zero.shape)
            for t in range(4):
                if n < ns:
                    held[t] = jnp.where((places[t] == n)[None], tile, held[t])
                if n > 0:
                    held[4 + t] = jnp.where((places[t] == n - 1)[None], tile, held[4 + t])
        low, high = held[:4], held[4:]
        for t in range(4):
            peer = group * 4 + t
            window = jnp.concatenate(
                [low[t].reshape(width, 128), high[t].reshape(width, 128)], axis=1
            )
            pick = jnp.where(span == offsets[pl.ds(peer, 1), :], 1.0, 0.0).astype(BF16)
            windows[peer] = dot_nn(window, pick).astype(BF16)
        send_group(POINTS, group, last)

    for fetch in fetches[1:]:
        fetch.wait()
    each(0, groups - 1, lambda i: cut_and_send(i, False), False)
    cut_and_send(groups - 1, True)
    arrived[pl.ds(s, 1)] = windows[pl.ds(s, 1)]
    relay(COT, cot)

    gathered = jnp.zeros((width, rows), F32)
    for i in range(groups):
        group = nth_group(i)
        for t in range(4):
            source = group * 4 + t

            def landed(source=source):
                scan_copy(POINTS, lax.rem(s - source + ns, ns)).wait_recv()

            if i < groups - 1:
                landed()
            else:
                pl.when(source != s)(landed)
        pieces = jnp.concatenate([arrived[group * 4 + t] for t in range(4)], axis=1)
        gathered = gathered + dot_nn(pieces, hots[aligned(group * 512, 512), :])
    full[mine, :] = gathered.astype(BF16)
    half_piece(h, 0, 4, right * 2 + core).start()
    half_piece(h, 1, 6, left * 2 + core).start()
    half_piece(h, 1, 5, right * 2 + core).start()
    half_piece(h, 0, 7, left * 2 + core).start()
    push(FULL, full, h, 0, twin).start()
    from_left, from_right = left * 2 + core, right * 2 + core
    half_piece(from_left, 0, 4, twin).wait_recv()
    half_piece(from_left, 0, 0, right * 2 + core).start()
    half_piece(from_right, 1, 6, twin).wait_recv()
    half_piece(from_right, 1, 1, left * 2 + core).start()
    half_piece(from_left, 1, 5, twin).wait_recv()
    push(FULL, full, from_left, nx + 1, twin).start()
    half_piece(from_right, 0, 7, twin).wait_recv()
    push(FULL, full, from_right, nx + 3, twin).start()
    arrive(COT, cot)
    gradc[...] = dot_nn(outw_ref[...], cot[...])
    for half in range(2):
        half_piece(across * 2 + core, half, half, twin).wait_recv()
        half_piece(across * 2 + core, half, 2 + half, twin).start()
    for at in (x, left, right):
        push(FULL, full, at * 2 + 1 - core, 0, twin).wait_recv()
    for half in range(2):
        half_piece(across * 2 + 1 - core, half, 2 + half, twin).wait_recv()

    floats = full[...].astype(F32)
    mean = jnp.sum(floats, axis=0, keepdims=True) * (1.0 / channels)
    centered = floats - mean
    inv = lax.rsqrt(jnp.sum(centered * centered, axis=0, keepdims=True) * (1.0 / channels) + EPS)
    normed[...] = centered * inv
    scaled[...] = (normed[...] * gain_wide[:, :1]).astype(BF16)
    for i, ref in enumerate((query, keys, value)):
        ref[...] = dot_nn(weight_ref[i], scaled[...])

    def forward(head):
        at = aligned(head * HD, HD)
        q, k, v = query[at, :], keys[at, :], value[at, :]
        key_t[...] = jnp.transpose(jnp.concatenate(left_stack(k), axis=0))
        v_rows = jnp.concatenate(list(split2(v)) + [jnp.ones((HD, rows), BF16)], axis=0)
        for b in range(0, rows, SPAN):
            q_stack = jnp.concatenate(
                right_stack(q[:, b : b + SPAN] * (HD**-0.5 * LOG2E)), axis=0
            )
            scores = dot_nn(key_t[...], q_stack)
            peak = jnp.max(scores, axis=0, keepdims=True)
            weights = jnp.exp2(scores - peak).astype(BF16)
            weights_all[head, :, b : b + SPAN] = weights
            sums = dot_nn(v_rows, weights)
            share = 1.0 / sums[2 * HD : 2 * HD + 1]
            shares[head, :, b : b + SPAN] = share
            ctx = (sums[:HD] + sums[HD : 2 * HD]) * share
            context[at, b : b + SPAN] = ctx

    for head in range(width // HD):
        forward(head)
    context_b = context[...].astype(BF16)
    branch_out[...] = dot_tn(outw_ref[...], context_b).astype(BF16)
    sum_begin(1)

    def backward(head):
        at = aligned(head * HD, HD)
        q, k, v = query[at, :], keys[at, :], value[at, :]
        row = lax.broadcasted_iota(jnp.int32, (HD, rows), 0)
        ones = jnp.ones((HD, rows), BF16)
        value_t[...] = jnp.transpose(jnp.concatenate(left_stack(v) + [ones], axis=0))
        k_rows = jnp.concatenate(list(split2(k)), axis=0)
        gs = gradc[at, :] * shares[head]
        center = jnp.sum(gs * context[at, :], axis=0, keepdims=True) * (-(HD**-0.5))
        parts = [t.astype(F32) for t in split3(center)]
        tail = jnp.where(
            row == 0, parts[0], jnp.where(row == 1, parts[1], jnp.where(row == 2, parts[2], 0.0))
        ).astype(BF16)
        g_stack = jnp.concatenate(right_stack(gs * HD**-0.5) + [tail], axis=0)
        g_rows = jnp.concatenate(list(split2(gs)), axis=0)
        q_rows = jnp.concatenate(list(split2(q)), axis=0)
        key_grad = jnp.zeros((HD * 2, rows), F32)
        value_grad = jnp.zeros((HD * 2, rows), F32)
        for b in range(0, rows, SPAN):
            weights = weights_all[head, :, b : b + SPAN]
            delta = dot_nn(value_t[...], g_stack[:, b : b + SPAN])
            score_grad = (weights.astype(F32) * delta).astype(BF16)
            value_grad = value_grad + dot_nt(g_rows[:, b : b + SPAN], weights)
            dq = dot_nn(k_rows, score_grad)
            grads[at, b : b + SPAN] = (dq[:HD] + dq[HD:]).astype(BF16)
            key_grad = key_grad + dot_nt(q_rows[:, b : b + SPAN], score_grad)
        k_at = aligned(width + head * HD, HD)
        v_at = aligned(2 * width + head * HD, HD)
        grads[k_at, :] = (key_grad[:HD] + key_grad[HD:]).astype(BF16)
        grads[v_at, :] = (value_grad[:HD] + value_grad[HD:]).astype(BF16)

    for head in range(width // HD):
        backward(head)
        if head == 0:
            sum_far(1)
        elif head == 1:
            sum_near(1)

    whole = jnp.concatenate([weight_ref[i] for i in range(3)], axis=0)
    part_out[...] = dot_tn(whole, grads[...]).astype(BF16)

    sum_begin(0)
    wgrad_out[:, : 3 * width] = dot_nt(scaled[...], grads[...]).astype(BF16)
    wgrad_out[:, 3 * width :] = dot_nt(cot[...], context_b).astype(BF16)
    sum_far(0)
    each(1, ns, lambda j: scan_copy(WGRAD, j).start())
    weighted = part_out[...].astype(F32) * gain_wide[:, :1]
    stats_out[0:1, :] = jnp.sum(weighted, axis=0, keepdims=True)
    stats_out[1:2, :] = jnp.sum(weighted * normed[...], axis=0, keepdims=True)
    each(1, nh, lambda j: stats_copy(j).start())

    sum_near(0)
    wgrad_in[pl.ds(s, 1)] = wgrad_out[aligned(s * strip, strip), :][None]
    branch = sum_end(1)
    mixed_ref[...] = (full[mine, :].astype(F32) + branch).astype(BF16)
    each(1, nh, lambda j: stats_copy(j).wait())
    stats = stats_out[...]
    for i in range(1, nh):
        stats = stats + stats_in[lax.rem(h + i, nh)]
    normed_grad = sum_end(0)
    normed_own = normed[mine, :]
    first, second = stats[0:1] * (1.0 / channels), stats[1:2] * (1.0 / channels)
    grad = inv * (normed_grad * gain_wide[mine, :1] - first - normed_own * second)
    points_grad = (cot[mine, :].astype(F32) + grad).astype(BF16)

    for i in range(groups):
        group = nth_group(i)
        block = dot_nt(points_grad, hots[aligned(group * 512, 512), :]).astype(BF16)
        for t in range(4):
            buckets[group * 4 + t] = block[:, 128 * t : 128 * (t + 1)]
        send_group(BACK, group, i == groups - 1)

    back_ref[pl.ds(s, 1)] = buckets[pl.ds(s, 1)]
    product = normed_grad * normed_own
    folded = product[:, :128]
    for b in range(128, rows, 128):
        folded = folded + product[:, b : b + 128]
    gain_out[...] = jnp.zeros_like(gain_out)
    gain_out[:, :width] = jnp.sum(jnp.transpose(folded), axis=0, keepdims=True)
    each(1, ns, lambda j: scan_copy(GAIN, j).start())
    gain_in[pl.ds(s, 1)] = gain_out[...][None]
    each(1, ns, lambda j: scan_copy(WGRAD, j).wait())
    wsum_ref[...] = jnp.sum(wgrad_in[...].astype(F32), axis=0)
    each(1, ns, lambda j: scan_copy(GAIN, j).wait())
    gsum_ref[...] = jnp.sum(gain_in[...], axis=0)
    sent(COT, cot)
    for slot in (0, nx + 1, nx + 3):
        push(FULL, full, h, slot, twin).wait_send()
    for slot in range(8):
        half_piece(h, 0, slot, twin).wait_send()
    sum_sent(0)
    sum_sent(1)
    each(1, ns, lambda j: scan_copy(POINTS, j).wait_send())
    each(1, ns, lambda j: scan_copy(BACK, j).wait())


def slots_kernel(
    ns, sizes_ref, back_ref, mixed_in, wsum_ref, gsum_ref,
    mixed_ref, owned_ref, qkv_ref, out_ref, gain_ref, slots,
):
    width = back_ref.shape[1]
    slots[...] = jnp.zeros_like(slots)
    lane = lax.broadcasted_iota(jnp.int32, (width, 128), 1)

    def one(d, begin):
        size = sizes_ref[d, 0]
        tile = begin // 128
        off = begin - tile * 128
        block = jnp.where(lane < size, back_ref[d].astype(F32), 0.0)
        wide = jnp.concatenate([block, jnp.zeros_like(block)], axis=1)
        at = pl.ds(pl.multiple_of(tile * 128, 128), 256)
        slots[:, at] = slots[:, at] + pltpu.roll(wide, off, 1)
        return begin + size

    lax.fori_loop(0, ns, one, jnp.int32(0), unroll=8)
    owned_ref[...] = slots[...].astype(BF16)
    mixed_ref[...] = mixed_in[...]
    for i in range(3):
        qkv_ref[i] = wsum_ref[:, i * width : (i + 1) * width]
    out_ref[...] = wsum_ref[:, 3 * width :]
    gain_ref[...] = gsum_ref[:, :width]


def per_device(owner_ids, owned_points, norm_gain, qkv_weight, out_weight, cotangent):
    ns, nh = lax.axis_size("scan"), lax.axis_size("head")
    nx = nh // 2
    rows = owner_ids.shape[0]
    width, slot_count = owned_points.shape
    channels = width * nh
    strip = channels // ns
    shape = jax.ShapeDtypeStruct
    dma = pltpu.SemaphoreType.DMA
    vmem = pltpu.VMEM
    sizes, mixed, back, wsum, gsum = pl.pallas_call(
        functools.partial(main_kernel, ns, nh),
        out_shape=(
            shape((ns, 128), jnp.int32),
            shape((width, rows), BF16),
            shape((ns, width, BUCKET), BF16),
            shape((strip, 4 * width), F32),
            shape((1, 128), F32),
        ),
        in_specs=[VMEM, ANY, ANY, VMEM, ANY, ANY],
        out_specs=(VMEM,) * 5,
        scratch_shapes=[
            vmem((ns, 128), jnp.int32),
            vmem((ns, 128), jnp.int32),
            vmem((ns, 128), jnp.int32),
            vmem((ns, width, BUCKET), BF16),
            vmem((ns, width, BUCKET), BF16),
            vmem((ns * BUCKET, rows), BF16),
            vmem((channels, rows), BF16),
            vmem((channels, rows), BF16),
            vmem((1, rows), jnp.int32),
            vmem((channels, 128), F32),
            vmem((channels, rows), F32),
            vmem((channels, rows), BF16),
            vmem((width, rows), F32),
            vmem((width, rows), F32),
            vmem((width, rows), F32),
            vmem((width, rows), F32),
            vmem((width, rows), F32),
            vmem((3 * width, rows), BF16),
            vmem((width // HD, rows, rows), BF16),
            vmem((width // HD, 1, rows), F32),
            vmem((rows, 6 * HD), BF16),
            vmem((rows, 7 * HD), BF16),
            vmem((channels, rows), BF16),
            vmem((2, 2, width // 2, rows), F32),
            vmem((channels, rows), BF16),
            vmem((2, nx, width, rows), BF16),
            vmem((2, 2, width // 2, rows), BF16),
            vmem((2, 2, width // 2, rows), BF16),
            vmem((2, 2, width, rows), BF16),
            vmem((2, 2, width, rows), BF16),
            vmem((2, rows), F32),
            vmem((nh, 2, rows), F32),
            vmem((channels, 4 * width), BF16),
            vmem((ns, strip, 4 * width), BF16),
            vmem((1, 128), F32),
            vmem((ns, 1, 128), F32),
            vmem((ns, width, BUCKET), BF16),
            vmem((width, slot_count), BF16),
            vmem((3, width, channels), BF16),
            vmem((width, channels), BF16),
            dma((4,)),
            dma((5, ns)),
            dma((5, ns)),
            dma((8, nh)),
            dma((8, nh)),
        ],
        compiler_params=pltpu.CompilerParams(
            collective_id=1, has_side_effects=True, vmem_limit_bytes=LIMIT
        ),
        name="patch_block",
    )(owner_ids.reshape(1, rows), owned_points, cotangent, norm_gain.reshape(1, channels), qkv_weight, out_weight)
    mixed_rows, grad_owned, qkv_grad, out_grad, gain_grad = pl.pallas_call(
        functools.partial(slots_kernel, ns),
        out_shape=(
            shape((width, rows), BF16),
            shape((width, slot_count), BF16),
            shape((3, strip, width), F32),
            shape((strip, width), F32),
            shape((1, width), F32),
        ),
        in_specs=[SMEM] + [VMEM] * 4,
        out_specs=(VMEM,) * 5,
        scratch_shapes=[vmem((width, slot_count), F32)],
        compiler_params=pltpu.CompilerParams(vmem_limit_bytes=LIMIT),
        name="slots",
    )(sizes, back, mixed, wsum, gsum)
    return (
        mixed_rows,
        grad_owned,
        qkv_grad.transpose(0, 2, 1),
        out_grad.T,
        gain_grad.reshape(width),
    )


def solution(mesh):
    in_specs = (
        P("scan", None),
        P("head", "scan"),
        P(),
        P(None, "head", None),
        P("head", None),
        P("head", "scan"),
    )
    out_specs = (
        P("head", "scan"),
        P("head", "scan"),
        P(None, "head", "scan"),
        P("head", "scan"),
        P("head"),
    )
    return jax.shard_map(
        per_device, mesh=mesh, in_specs=in_specs, out_specs=out_specs, check_vma=False
    )
```
